256 devices in a mesh: user: 64 (over z, y, x_hi), feat: 4 (over x_lo, core).
Axes of the slice: x: 4 (x_hi: 2, x_lo: 2; x = x_hi * 2 + x_lo), y: 4, z: 8, core: 2. Of those that a mesh axis runs over, the one named last changes fastest.
Arguments:
- view_one: bfloat16 [8192, 2048], P('user', 'feat'), may hold values from -8 to 8
- view_two: bfloat16 [8192, 2048], P('user', 'feat'), may hold values from -8 to 8
- partner: int32 [8192], P('user'), may hold values from 0 to 8191, each once
Outputs:
- grad_one: float32 [8192, 2048], P('user', 'feat')
- grad_two: float32 [8192, 2048], P('user', 'feat')
The draws below stay inside these ranges and needn't reach their ends.
Inputs may be any that keep to these rules, and one draw needn't show every extreme that they name: `partner`: each index of view_two appears exactly once.
All inputs are finite; a program needn't handle non-finite values.
Results may differ from the reference program's by a relative error of at most 0.0028.
Values may be sent and summed in bfloat16 or wider, within the bound.
No kernel may reach another device: no remote copies, remote signals or barrier semaphores. Data moves between devices by JAX's collectives and lax.ppermute only.
A program may use at most 128 MiB of HBM per device.

```python
import math
import jax
import jax.numpy as jnp
from jax import lax

D = 2048
USERS = 8192


def aligned_bases(key):
    signs = jax.random.bernoulli(key, 0.5, (8, D))
    return jnp.where(signs, 1.0, -1.0).astype(jnp.float32)


def drawn_rows(offset):
    stride_rows = USERS // 8
    row_index = jnp.arange(USERS)
    chosen = row_index % stride_rows == offset
    which = jnp.minimum(row_index // stride_rows, 7)
    return (chosen, which)


def drawn_strength(which):
    target = 120.0 + 40.0 * which.astype(jnp.float32)
    return jnp.sqrt(target / (2.0 * math.sqrt(D)))


def draw_view_one(key, part):
    bases = aligned_bases(key)
    key = jax.random.fold_in(key, 3)
    values = jnp.clip(jax.random.normal(key, (USERS, D), jnp.float32), -6.0, 6.0)
    chosen, which = drawn_rows(0)
    strength = drawn_strength(which)
    values = jnp.where(chosen[:, None], strength[:, None] * bases[which], values)
    return values.astype(jnp.bfloat16)


def draw_view_two(key, part):
    bases = aligned_bases(key)
    key = jax.random.fold_in(key, 7)
    values = jnp.clip(jax.random.normal(key, (USERS, D), jnp.float32), -6.0, 6.0)
    noise = jnp.clip(jax.random.normal(jax.random.fold_in(key, 13), (USERS, D), jnp.float32), -3.0, 3.0)
    half_stride = USERS // 16
    chosen, which = drawn_rows(half_stride)
    twin, twin_which = drawn_rows(half_stride + 1)
    strength = drawn_strength(which)
    twin_strength = drawn_strength(twin_which)
    values = jnp.where(chosen[:, None], strength[:, None] * bases[which], values)
    twin_values = 0.995 * twin_strength[:, None] * bases[twin_which] + 0.3 * noise
    values = jnp.where(twin[:, None], twin_values, values)
    return values.astype(jnp.bfloat16)


def setup_inputs(seed: int = 0) -> dict:
    streams_of = jax.random.split(jax.random.key(seed), 4)
    view_one = draw_view_one(jax.random.fold_in(streams_of[3], 71), 0)
    view_two = draw_view_two(jax.random.fold_in(streams_of[3], 71), 0)
    partner = jax.random.permutation(streams_of[2], USERS).astype(jnp.int32)
    return {"view_one": view_one, "view_two": view_two, "partner": partner}


def reference(view_one, view_two, partner):
    logit_scale = 2.0 / math.sqrt(D)
    block_size = math.gcd(USERS, 512)
    blocks_count = USERS // block_size
    view_blocks = view_one.reshape(blocks_count, block_size, D)
    partner_blocks = partner.reshape(blocks_count, block_size)

    def block_scores(block_rows):
        return logit_scale * jnp.dot(block_rows, view_two.T, preferred_element_type=jnp.float32)

    def stats_step(running, block_rows):
        col_highest, col_total = running
        scores = block_scores(block_rows)
        row_highest = lax.optimization_barrier(jnp.max(scores, axis=1))
        row_lse = row_highest + jnp.log(lax.optimization_barrier(jnp.sum(jnp.exp(scores - row_highest[:, None]), axis=1)))
        new_highest = jnp.maximum(col_highest, lax.optimization_barrier(jnp.max(scores, axis=0)))
        col_total = col_total * jnp.exp(col_highest - new_highest) + lax.optimization_barrier(jnp.sum(jnp.exp(scores - new_highest[None, :]), axis=0))
        return ((new_highest, col_total), row_lse)
    initial = (jnp.full((USERS,), -jnp.inf, jnp.float32), jnp.zeros((USERS,), jnp.float32))
    (col_highest, col_total), row_lses = lax.scan(stats_step, initial, view_blocks)
    col_lse = col_highest + jnp.log(col_total)

    def grad_step(accumulated, inputs):
        block_rows, row_lse, block_partner = inputs
        scores = block_scores(block_rows)
        column_index = lax.broadcasted_iota(jnp.int32, scores.shape, 1)
        positive_mask = (column_index == block_partner[:, None]).astype(jnp.float32)
        coupling = (0.5 * (jnp.exp(scores - row_lse[:, None]) + jnp.exp(scores - col_lse[None, :])) - positive_mask).astype(jnp.bfloat16)
        first_grad = jnp.dot(coupling, view_two, preferred_element_type=jnp.float32)
        accumulated = accumulated + jnp.dot(coupling.T, block_rows, preferred_element_type=jnp.float32)
        return (accumulated, first_grad)
    grad_two, first_blocks = lax.scan(grad_step, jnp.zeros((USERS, D), jnp.float32), (view_blocks, row_lses, partner_blocks))
    grad_one = first_blocks.reshape(USERS, D)
    return (grad_one, grad_two)
```

```python
import math

import jax
import jax.numpy as jnp
from jax import lax
from jax.experimental import pallas as pl
from jax.experimental.pallas import tpu as pltpu
from jax.sharding import Mesh
from jax.sharding import PartitionSpec as P

D = 2048
NZ, NY, NXH, NXL, NC = 8, 4, 2, 2, 2
PLANE = ("y", "xh", "xl")
EVERY = ("z", "y", "xh", "xl", "core")
ROWS = 128
HALF = 64
WIDTH = 512
NI = NY * NXH * ROWS
NJ = NZ * HALF


def score_kernel(v1_ref, *refs):
    v2_refs, s_ref, cat_ref = refs[:NZ], refs[NZ], refs[NZ + 1]
    for k in range(NZ):
        cat_ref[:, k * HALF : (k + 1) * HALF, :] = v2_refs[k][...]
    contract = (((1,), (1,)), ((), ()))
    for u in range(NI // ROWS):
        s_ref[u * ROWS : (u + 1) * ROWS, :] = lax.dot_general(
            v1_ref[u, 0], cat_ref[0], contract, preferred_element_type=jnp.float32
        ) + lax.dot_general(
            v1_ref[u, 1], cat_ref[1], contract, preferred_element_type=jnp.float32
        )
    most_two = jnp.max(jnp.abs(cat_ref[...]).astype(jnp.float32))
    most_one = jnp.max(jnp.abs(v1_ref[...]).astype(jnp.float32))
    row = lax.broadcasted_iota(jnp.int32, (8, NJ), 0)
    s_ref[NI : NI + 8, :] = jnp.where(row < 4, most_two, most_one)


def partial_scores(v1_all, v2_parts):
    vmem = pl.BlockSpec(memory_space=pltpu.VMEM)
    return pl.pallas_call(
        score_kernel,
        out_shape=(
            jax.ShapeDtypeStruct((NI + 8, NJ), jnp.float32),
            jax.ShapeDtypeStruct((NXL, NJ, WIDTH), jnp.bfloat16),
        ),
        in_specs=[vmem] * (1 + NZ),
        out_specs=(vmem, vmem),
        compiler_params=pltpu.CompilerParams(vmem_limit_bytes=48 * 1024 * 1024),
        cost_estimate=pl.CostEstimate(
            flops=2 * NI * NJ * NXL * WIDTH, bytes_accessed=6 * 2**20, transcendentals=0
        ),
    )(v1_all, *v2_parts)


def swap(x, axis):
    return lax.ppermute(x, axis, [(0, 1), (1, 0)])


def merged_lse(highest, total):
    top = jnp.max(highest, axis=0)
    return top + jnp.log(jnp.sum(total * jnp.exp(highest - top[None]), axis=0))


def stat_groups():
    def number(z, y, xh, xl, c):
        return (((z * NY + y) * NXH + xh) * NXL + xl) * NC + c

    planes = [
        [number(z, y, xh, xl, 0) for y in range(NY) for xh in range(NXH) for xl in range(NXL)]
        for z in range(NZ)
    ]
    columns = [
        [number(z, y, xh, xl, 1) for z in range(NZ) for xl in range(NXL)]
        for y in range(NY)
        for xh in range(NXH)
    ]
    return planes + columns


def on_device(view_one, view_two, partner):
    logit_scale = 2.0 / math.sqrt(D)
    z = lax.axis_index("z")
    uhigh = lax.axis_index("y") * NXH + lax.axis_index("xh")
    xl = lax.axis_index("xl")
    core = lax.axis_index("core")

    keep = lax.dynamic_slice(view_two, (xl * HALF, 0), (HALF, WIDTH))
    give = lax.dynamic_slice(view_two, ((1 - xl) * HALF, 0), (HALF, WIDTH))
    got = swap(give, "xl")
    mine = jnp.where(xl == 0, jnp.stack([keep, got]), jnp.stack([got, keep]))
    v2_parts = [mine] + [
        lax.ppermute(mine, "z", [(i, (i + k) % NZ) for i in range(NZ)]) for k in range(1, NZ)
    ]
    v1_all = lax.all_to_all(
        jnp.broadcast_to(view_one[None], (16, ROWS, WIDTH)), PLANE, 0, 0, tiled=True
    ).reshape(NY * NXH, NXL, ROWS, WIDTH)

    part, v2_all = partial_scores(v1_all, v2_parts)
    other = swap(part, "core")
    scores = logit_scale * (part[:NI] + other[:NI])
    most = jnp.maximum(part[NI:, 0], other[NI:, 0])
    most_two = jnp.maximum(most[0], 1e-30)
    most_one = jnp.maximum(most[4], 1e-30)

    row_highest = jnp.max(scores, axis=1)
    row_total = jnp.sum(jnp.exp(scores - row_highest[:, None]), axis=1)
    col_highest = jnp.max(scores, axis=0)
    col_total = jnp.sum(jnp.exp(scores - col_highest[None, :]), axis=0)

    turn = (z - jnp.arange(NZ)) % NZ
    pick = turn[:, None] == jnp.arange(NZ)[None, :]

    def reorder(x):
        return jnp.sum(jnp.where(pick[:, :, None], x.reshape(1, NZ, HALF), 0.0), axis=1).reshape(-1)

    row_tail = jnp.concatenate(
        [partner.astype(jnp.float32), jnp.full((128,), most_two), jnp.zeros((256,), jnp.float32)]
    )
    row_pack = jnp.concatenate(
        [row_highest, row_total, row_tail, jnp.zeros((3 * 512,), jnp.float32)]
    )
    col_pack = jnp.concatenate(
        [
            reorder(col_highest),
            reorder(col_total),
            jnp.zeros((2 * 512,), jnp.float32),
            jnp.full((512,), most_one),
            jnp.zeros((3 * 512,), jnp.float32),
        ]
    )
    pack = jnp.where(core == 0, row_pack, col_pack).reshape(8, 512)
    seen = lax.all_to_all(
        jnp.broadcast_to(pack[None], (16, 8, 512)),
        EVERY,
        0,
        0,
        axis_index_groups=stat_groups(),
        tiled=True,
    )
    row_lse = merged_lse(seen[:, 0:2].reshape(16, NI), seen[:, 2:4].reshape(16, NI))
    row_partner = seen.reshape(8, 2, 8, 512)[:, 0, 4, :ROWS].reshape(NI)
    two_most = seen[:, 4, 128]
    by_z = seen.reshape(NZ, NXL, 8, 512)
    by_z = jnp.where(xl == 0, by_z[:, 0], by_z[:, 1])
    col_lse = reorder(merged_lse(by_z[:, 0], by_z[:, 1]))
    one_most = by_z[:, 4, 128]
    tail0 = jnp.concatenate([two_most, jnp.zeros((512 - 16,), jnp.float32)])
    tail1 = jnp.concatenate([one_most, jnp.zeros((512 - 8,), jnp.float32)])
    zeros = jnp.zeros((512,), jnp.float32)
    known0 = jnp.concatenate([row_lse, row_partner, tail0, zeros, zeros, zeros])
    known1 = jnp.concatenate([col_lse, zeros, zeros, zeros, tail1, zeros, zeros, zeros])
    known = jnp.where(core == 0, known0, known1).reshape(8, 512)
    told = swap(known, "core")
    rows = jnp.where(core == 0, known, told)
    cols = jnp.where(core == 0, told, known)
    row_lse = rows[0:2].reshape(NI)
    row_partner = rows[2:4].reshape(NI).astype(jnp.int32)
    two_most = rows[4, :16]
    col_lse = cols[0]
    one_most = cols[4, :NZ]

    block = (z - jnp.arange(NZ)) % NZ
    index = ((block * (NY * NXH) + uhigh) * ROWS + xl * HALF)[:, None] + jnp.arange(HALF)[None, :]
    positive = (index.reshape(1, NJ) == row_partner[:, None]).astype(jnp.float32)
    both = jnp.exp(scores - row_lse[:, None]) + jnp.exp(scores - col_lse[None, :])
    coupling = (0.5 * both - positive).astype(jnp.bfloat16)

    part_two = jnp.einsum(
        "uij,uxik->jxk",
        coupling.reshape(8, ROWS, NJ),
        v1_all,
        preferred_element_type=jnp.float32,
    )
    part_two = (part_two * (64.0 / most_one)).astype(jnp.float16).reshape(NZ, HALF, NXL, WIDTH)
    two_parts = [part_two[0]] + [
        lax.ppermute(part_two[k], "z", [(i, (i - k) % NZ) for i in range(NZ)])
        for k in range(1, NZ)
    ]
    part_one = jnp.einsum(
        "uij,xjk->uxik",
        coupling.reshape(8, ROWS, NJ),
        v2_all,
        preferred_element_type=jnp.float32,
    )
    part_one = (part_one * (128.0 / most_two)).astype(jnp.float16)
    one_parts = lax.all_to_all(
        part_one.reshape(16, ROWS, WIDTH), PLANE, 0, 0, tiled=True
    )
    grad_one = jnp.sum(one_parts.astype(jnp.float32) * (two_most / 128.0)[:, None, None], axis=0)

    grad_half = jnp.zeros((HALF, NXL, WIDTH), jnp.float32)
    for k in range(NZ):
        source = jnp.sum(jnp.where(jnp.arange(NZ) == (z + k) % NZ, one_most, 0.0))
        grad_half = grad_half + two_parts[k].astype(jnp.float32) * (source / 64.0)
    stay = jnp.where(xl == 0, grad_half[:, 0], grad_half[:, 1])
    leave = jnp.where(xl == 0, grad_half[:, 1], grad_half[:, 0])
    come = swap(leave, "xl")
    grad_two = jnp.where(
        xl == 0, jnp.concatenate([stay, come]), jnp.concatenate([come, stay])
    )
    return (grad_one, grad_two)


def solution(mesh):
    fine = Mesh(mesh.devices.reshape(NZ, NY, NXH, NXL, NC), EVERY)
    users = P(("z", "y", "xh"))
    both = P(("z", "y", "xh"), ("xl", "core"))
    return jax.shard_map(
        on_device,
        mesh=fine,
        in_specs=(both, both, users),
        out_specs=(both, both),
        check_vma=False,
    )
```

```python
import math

import jax
import jax.numpy as jnp
from jax import lax
from jax.experimental import pallas as pl
from jax.experimental.pallas import tpu as pltpu
from jax.sharding import Mesh
from jax.sharding import PartitionSpec as P

D = 2048
NZ, NY, NXH, NXL, NC = 8, 4, 2, 2, 2
PLANE = ("xl", "y", "xh")
COLUMN = ("xl", "z")
EVERY = ("z", "y", "xh", "xl", "core")
ROWS = 128
HALF = 64
WIDTH = 512
NI = NY * NXH * ROWS
NJ = NZ * HALF
LANES = 128
SCALE = 2.0 / math.sqrt(D)
VMEM = pl.BlockSpec(memory_space=pltpu.VMEM)
SMEM = pl.BlockSpec(memory_space=pltpu.SMEM)
LIMIT = pltpu.CompilerParams(vmem_limit_bytes=48 * 1024 * 1024)


def score_kernel(v1_ref, v2_ref, s_ref):
    contract = (((1,), (1,)), ((), ()))
    for u in range(NI // 256):
        rows = slice(u * 256, (u + 1) * 256)
        s_ref[rows, :] = lax.dot_general(
            v1_ref[0, rows, :], v2_ref[0], contract, preferred_element_type=jnp.float32
        ) + lax.dot_general(
            v1_ref[1, rows, :], v2_ref[1], contract, preferred_element_type=jnp.float32
        )


def partial_scores(v1_all, v2_all):
    return pl.pallas_call(
        score_kernel,
        out_shape=jax.ShapeDtypeStruct((NI, NJ), jnp.float32),
        in_specs=[VMEM, VMEM],
        out_specs=VMEM,
        compiler_params=LIMIT,
        cost_estimate=pl.CostEstimate(
            flops=2 * NI * NJ * NXL * WIDTH, bytes_accessed=5 * 2**20, transcendentals=0
        ),
    )(v1_all, v2_all)


def diagonal():
    shape = (LANES, LANES)
    return lax.broadcasted_iota(jnp.int32, shape, 0) == lax.broadcasted_iota(jnp.int32, shape, 1)


def stats_kernel(own_ref, other_ref, partner_ref, most_ref, s_ref, pack_ref):
    eye = diagonal()
    pack_ref[...] = jnp.zeros_like(pack_ref)
    col_highest = jnp.full((1, NJ), -jnp.inf, jnp.float32)
    col_total = jnp.zeros((1, NJ), jnp.float32)
    for u in range(NI // LANES):
        rows = slice(u * LANES, (u + 1) * LANES)
        s = SCALE * (own_ref[rows, :] + other_ref[rows, :])
        s_ref[rows, :] = s
        highest = jnp.max(s, axis=1, keepdims=True)
        lse = highest + jnp.log(jnp.sum(jnp.exp(s - highest), axis=1, keepdims=True))
        pack_ref[0, u : u + 1, :] = jnp.sum(jnp.where(eye, lse, 0.0), axis=0, keepdims=True)
        higher = jnp.maximum(col_highest, jnp.max(s, axis=0, keepdims=True))
        col_total = col_total * jnp.exp(col_highest - higher) + jnp.sum(
            jnp.exp(s - higher), axis=0, keepdims=True
        )
        col_highest = higher
    col_lse = col_highest + jnp.log(col_total)
    for t in range(NJ // LANES):
        pack_ref[1, t : t + 1, :] = col_lse[:, t * LANES : (t + 1) * LANES]
    pack_ref[0, 8:9, :] = partner_ref[...].astype(jnp.float32)
    pack_ref[0, 9:10, :] = most_ref[0:1, :]
    pack_ref[1, 9:10, :] = most_ref[1:2, :]


def local_stats(own, other, partner, most):
    return pl.pallas_call(
        stats_kernel,
        out_shape=(
            jax.ShapeDtypeStruct((NI, NJ), jnp.float32),
            jax.ShapeDtypeStruct((2, 16, LANES), jnp.float32),
        ),
        in_specs=[VMEM] * 4,
        out_specs=(VMEM, VMEM),
        compiler_params=LIMIT,
        cost_estimate=pl.CostEstimate(
            flops=10 * NI * NJ, bytes_accessed=6 * 2**20, transcendentals=2 * NI * NJ
        ),
    )(own, other, partner.reshape(1, ROWS), most)


def merged(lses):
    top = jnp.max(lses, axis=0)
    return top + jnp.log(jnp.sum(jnp.exp(lses - top[None]), axis=0))


def merge_kernel(place_ref, seen_ref, known_ref):
    core, xl = place_ref[0], place_ref[1]

    @pl.when(core == 0)
    def _():
        known_ref[0:8, :] = merged(seen_ref[:, 0:8, :])
        for u in range(8):
            known_ref[8 + u : 9 + u, :] = seen_ref[u, 8:9, :]
        for p in range(16):
            known_ref[16 + p : 17 + p, :] = seen_ref[p, 9:10, :]

    @pl.when(core != 0)
    def _():
        known_ref[...] = jnp.zeros_like(known_ref)
        known_ref[0:8, :] = merged(seen_ref[pl.ds(xl * NZ, NZ), 0:8, :])
        for p in range(16):
            known_ref[16 + p : 17 + p, :] = seen_ref[p, 9:10, :]


def merge_stats(place, seen):
    return pl.pallas_call(
        merge_kernel,
        out_shape=jax.ShapeDtypeStruct((32, LANES), jnp.float32),
        in_specs=[SMEM, VMEM],
        out_specs=VMEM,
        cost_estimate=pl.CostEstimate(flops=10**5, bytes_accessed=2**17, transcendentals=2**14),
    )(place, seen)


def swap(x, axis):
    return lax.ppermute(x, axis, [(0, 1), (1, 0)])


def stat_groups():
    def number(z, y, xh, xl, c):
        return (((z * NY + y) * NXH + xh) * NXL + xl) * NC + c

    planes = [
        [number(z, y, xh, xl, 0) for xl in range(NXL) for y in range(NY) for xh in range(NXH)]
        for z in range(NZ)
    ]
    columns = [
        [number(z, y, xh, xl, 1) for xl in range(NXL) for z in range(NZ)]
        for y in range(NY)
        for xh in range(NXH)
    ]
    return planes + columns


def on_device(view_one, view_two, partner):
    uhigh = lax.axis_index("y") * NXH + lax.axis_index("xh")
    xl = lax.axis_index("xl")
    core = lax.axis_index("core")

    v2_all = lax.all_to_all(
        jnp.broadcast_to(view_two.reshape(NXL, 1, HALF, WIDTH), (NXL, NZ, HALF, WIDTH)).reshape(
            NXL * NZ, HALF, WIDTH
        ),
        COLUMN,
        0,
        0,
        tiled=True,
    ).reshape(NXL, NJ, WIDTH)
    v1_all = lax.all_to_all(
        jnp.broadcast_to(view_one[None], (16, ROWS, WIDTH)), PLANE, 0, 0, tiled=True
    ).reshape(NXL, NI, WIDTH)

    own = partial_scores(v1_all, v2_all)
    other = swap(own, "core")
    most = jnp.stack([jnp.max(jnp.abs(v2_all)), jnp.max(jnp.abs(v1_all))]).astype(jnp.float32)
    most = jnp.broadcast_to(jnp.maximum(most, 1e-30)[:, None], (2, LANES))
    most = jnp.maximum(most, swap(most, "core"))

    scores, pack = local_stats(own, other, partner, most)
    pack = jnp.where(core == 0, pack[0], pack[1])
    seen = lax.all_to_all(
        jnp.broadcast_to(pack[None], (16, 16, LANES)),
        EVERY,
        0,
        0,
        axis_index_groups=stat_groups(),
        tiled=True,
    )
    known = merge_stats(jnp.stack([core, xl]).astype(jnp.int32), seen)
    told = swap(known, "core")
    rows = jnp.where(core == 0, known, told)
    cols = jnp.where(core == 0, told, known)
    row_lse = rows[0:8].reshape(NI)
    row_partner = rows[8:16].reshape(NI).astype(jnp.int32)
    two_most = rows[16:32, 0]
    col_lse = cols[0:4].reshape(NJ)
    one_most = cols[16:32, 0]

    block = jnp.arange(NZ)
    index = ((block * (NY * NXH) + uhigh) * ROWS + xl * HALF)[:, None] + jnp.arange(HALF)[None, :]
    positive = (index.reshape(1, NJ) == row_partner[:, None]).astype(jnp.float32)
    both = jnp.exp(scores - row_lse[:, None]) + jnp.exp(scores - col_lse[None, :])
    coupling = (0.5 * both - positive).astype(jnp.bfloat16)

    part_two = jnp.stack(
        [
            (
                lax.dot_general(
                    coupling, v1_all[x], (((0,), (0,)), ((), ())), preferred_element_type=jnp.float32
                )
                * (64.0 / most[1, 0])
            ).astype(jnp.float16)
            for x in range(NXL)
        ]
    )
    two_parts = lax.all_to_all(
        part_two.reshape(NXL * NZ, HALF, WIDTH), COLUMN, 0, 0, tiled=True
    )
    part_one = jnp.stack(
        [
            (
                jnp.dot(coupling, v2_all[x], preferred_element_type=jnp.float32)
                * (128.0 / most[0, 0])
            ).astype(jnp.float16)
            for x in range(NXL)
        ]
    )
    one_parts = lax.all_to_all(part_one.reshape(16, ROWS, WIDTH), PLANE, 0, 0, tiled=True)
    grad_two = jnp.sum(
        two_parts.reshape(NXL, NZ, HALF, WIDTH).astype(jnp.float32)
        * (one_most / 64.0).reshape(NXL, NZ, 1, 1),
        axis=1,
    ).reshape(ROWS, WIDTH)
    grad_one = jnp.sum(one_parts.astype(jnp.float32) * (two_most / 128.0)[:, None, None], axis=0)
    return (grad_one, grad_two)


def solution(mesh):
    fine = Mesh(mesh.devices.reshape(NZ, NY, NXH, NXL, NC), EVERY)
    users = P(("z", "y", "xh"))
    both = P(("z", "y", "xh"), ("xl", "core"))
    return jax.shard_map(
        on_device,
        mesh=fine,
        in_specs=(both, both, users),
        out_specs=(both, both),
        check_vma=False,
    )
```

```python
import math

import jax
import jax.numpy as jnp
from jax import lax
from jax.experimental import pallas as pl
from jax.experimental.pallas import tpu as pltpu
from jax.sharding import Mesh
from jax.sharding import PartitionSpec as P

D = 2048
NZ, NY, NXH, NXL, NC = 8, 4, 2, 2, 2
PLANE = ("xl", "y", "xh")
PAIR = ("z", "xl")
OFFSETS = (0, -1, 1, -2)
GROUP = 128
EVERY = ("z", "y", "xh", "xl", "core")
ROWS = 128
HALF = 64
WIDTH = 512
NI = NY * NXH * ROWS
NJ = NZ * HALF
LANES = 128
SCALE = 2.0 / math.sqrt(D)
VMEM = pl.BlockSpec(memory_space=pltpu.VMEM)
SMEM = pl.BlockSpec(memory_space=pltpu.SMEM)
LIMIT = pltpu.CompilerParams(vmem_limit_bytes=16 * 1024 * 1024)


def score_kernel(v1_ref, *refs):
    group_refs, s_ref, v2_ref = refs[:4], refs[4], refs[5]
    for g in range(4):
        v2_ref[:, g * GROUP : (g + 1) * GROUP, :] = group_refs[g][...]
    contract = (((1,), (1,)), ((), ()))
    for u in range(NI // 256):
        rows = slice(u * 256, (u + 1) * 256)
        s_ref[rows, :] = lax.dot_general(
            v1_ref[0, rows, :], v2_ref[0], contract, preferred_element_type=jnp.float32
        ) + lax.dot_general(
            v1_ref[1, rows, :], v2_ref[1], contract, preferred_element_type=jnp.float32
        )


def partial_scores(v1_all, groups):
    return pl.pallas_call(
        score_kernel,
        out_shape=(
            jax.ShapeDtypeStruct((NI, NJ), jnp.float32),
            jax.ShapeDtypeStruct((NXL, NJ, WIDTH), jnp.bfloat16),
        ),
        in_specs=[VMEM] * 5,
        out_specs=(VMEM, VMEM),
        compiler_params=LIMIT,
        cost_estimate=pl.CostEstimate(
            flops=2 * NI * NJ * NXL * WIDTH, bytes_accessed=6 * 2**20, transcendentals=0
        ),
    )(v1_all, *groups)


def diagonal():
    shape = (LANES, LANES)
    return lax.broadcasted_iota(jnp.int32, shape, 0) == lax.broadcasted_iota(jnp.int32, shape, 1)


def placed(z, g):
    first = lax.rem(z + OFFSETS[g] + NZ, NZ)
    return lax.rem(first, 4), first >= 4


def turned(row, trade):
    return jnp.where(trade, pltpu.roll(row, HALF, 1), row)


def stats_kernel(place_ref, own_ref, other_ref, partner_ref, most_ref, s_ref, pack_ref):
    eye = diagonal()
    pack_ref[...] = jnp.zeros_like(pack_ref)
    col_highest = jnp.full((1, NJ), -jnp.inf, jnp.float32)
    col_total = jnp.zeros((1, NJ), jnp.float32)
    for u in range(NI // LANES):
        rows = slice(u * LANES, (u + 1) * LANES)
        s = SCALE * (own_ref[rows, :] + other_ref[rows, :])
        s_ref[rows, :] = s
        highest = jnp.max(s, axis=1, keepdims=True)
        lse = highest + jnp.log(jnp.sum(jnp.exp(s - highest), axis=1, keepdims=True))
        pack_ref[0, u : u + 1, :] = jnp.sum(jnp.where(eye, lse, 0.0), axis=0, keepdims=True)
        higher = jnp.maximum(col_highest, jnp.max(s, axis=0, keepdims=True))
        col_total = col_total * jnp.exp(col_highest - higher) + jnp.sum(
            jnp.exp(s - higher), axis=0, keepdims=True
        )
        col_highest = higher
    col_lse = col_highest + jnp.log(col_total)
    for g in range(4):
        row, trade = placed(place_ref[2], g)
        pack_ref[1, pl.ds(row, 1), :] = turned(col_lse[:, g * LANES : (g + 1) * LANES], trade)
    pack_ref[0, 8:9, :] = partner_ref[...].astype(jnp.float32)
    pack_ref[0, 9:10, :] = most_ref[0:1, :]
    pack_ref[1, 9:10, :] = most_ref[1:2, :]


def local_stats(place, own, other, partner, most):
    return pl.pallas_call(
        stats_kernel,
        out_shape=(
            jax.ShapeDtypeStruct((NI, NJ), jnp.float32),
            jax.ShapeDtypeStruct((2, 16, LANES), jnp.float32),
        ),
        in_specs=[SMEM] + [VMEM] * 4,
        out_specs=(VMEM, VMEM),
        compiler_params=LIMIT,
        cost_estimate=pl.CostEstimate(
            flops=10 * NI * NJ, bytes_accessed=6 * 2**20, transcendentals=2 * NI * NJ
        ),
    )(place, own, other, partner.reshape(1, ROWS), most)


def merged(lses):
    top = jnp.max(lses, axis=0)
    return top + jnp.log(jnp.sum(jnp.exp(lses - top[None]), axis=0))


def merge_kernel(place_ref, seen_ref, known_ref, cols_ref):
    core, xl = place_ref[0], place_ref[1]

    @pl.when(core == 0)
    def _():
        known_ref[0:8, :] = merged(seen_ref[:, 0:8, :])
        for u in range(8):
            known_ref[8 + u : 9 + u, :] = seen_ref[u, 8:9, :]
        known_ref[16:24, :] = jnp.broadcast_to(jnp.max(seen_ref[:, 9:10, :], axis=0), (8, LANES))

    @pl.when(core != 0)
    def _():
        known_ref[...] = jnp.zeros_like(known_ref)
        cols_ref[...] = merged(seen_ref[pl.ds(xl * NZ, NZ), 0:8, :])
        for g in range(4):
            row, trade = placed(place_ref[2], g)
            known_ref[g : g + 1, :] = turned(cols_ref[pl.ds(row, 1), :], trade)
        known_ref[16:24, :] = jnp.broadcast_to(jnp.max(seen_ref[:, 9:10, :], axis=0), (8, LANES))


def merge_stats(place, seen):
    return pl.pallas_call(
        merge_kernel,
        out_shape=jax.ShapeDtypeStruct((24, LANES), jnp.float32),
        in_specs=[SMEM, VMEM],
        out_specs=VMEM,
        scratch_shapes=[pltpu.VMEM((8, LANES), jnp.float32)],
        cost_estimate=pl.CostEstimate(flops=10**5, bytes_accessed=2**17, transcendentals=2**14),
    )(place, seen)


def swap(x, axis):
    return lax.ppermute(x, axis, [(0, 1), (1, 0)])


def stat_groups():
    def number(z, y, xh, xl, c):
        return (((z * NY + y) * NXH + xh) * NXL + xl) * NC + c

    planes = [
        [number(z, y, xh, xl, 0) for xl in range(NXL) for y in range(NY) for xh in range(NXH)]
        for z in range(NZ)
    ]
    columns = [
        [number(z, y, xh, xl, 1) for xl in range(NXL) for z in range(NZ)]
        for y in range(NY)
        for xh in range(NXH)
    ]
    return planes + columns


def to_pair(x, dz, dxl):
    steps = [(z * NXL + l, (z + dz) % NZ * NXL + (l + dxl) % NXL) for z in range(NZ) for l in range(NXL)]
    return lax.ppermute(x, PAIR, steps)


def to_plane(x, dz):
    return lax.ppermute(x, "z", [(z, (z + dz) % NZ) for z in range(NZ)])


def on_device(view_one, view_two, partner):
    z = lax.axis_index("z")
    uhigh = lax.axis_index("y") * NXH + lax.axis_index("xh")
    xl = lax.axis_index("xl")
    core = lax.axis_index("core")
    place = jnp.stack([core, xl, z]).astype(jnp.int32)

    keep = jnp.where(xl == 0, view_two[:HALF], view_two[HALF:])
    give = jnp.where(xl == 0, view_two[HALF:], view_two[:HALF])
    side, far, far_side = to_pair(give, 0, 1), to_pair(keep, 4, 0), to_pair(give, 4, 1)
    view_one, side, far, far_side = lax.optimization_barrier((view_one, side, far, far_side))
    here = jnp.concatenate([keep, far])
    there = jnp.concatenate([side, far_side])
    pair = jnp.where(xl == 0, jnp.stack([here, there]), jnp.stack([there, here]))
    groups = [pair] + [to_plane(pair, -dz) for dz in OFFSETS[1:]]
    v1_all = lax.all_to_all(
        jnp.broadcast_to(view_one[None], (16, ROWS, WIDTH)), PLANE, 0, 0, tiled=True
    ).reshape(NXL, NI, WIDTH)

    own, v2_all = partial_scores(v1_all, groups)
    other = swap(own, "core")
    most = jnp.stack([jnp.max(jnp.abs(v2_all)), jnp.max(jnp.abs(v1_all))]).astype(jnp.float32)
    most = jnp.broadcast_to(jnp.maximum(most, 1e-30)[:, None], (2, LANES))
    most = jnp.maximum(most, swap(most, "core"))

    scores, pack = local_stats(place, own, other, partner, most)
    pack = jnp.where(core == 0, pack[0], pack[1])
    seen = lax.all_to_all(
        jnp.broadcast_to(pack[None], (16, 16, LANES)),
        EVERY,
        0,
        0,
        axis_index_groups=stat_groups(),
        tiled=True,
    )
    known = merge_stats(place, seen)
    told = swap(known, "core")
    rows = jnp.where(core == 0, known, told)
    cols = jnp.where(core == 0, told, known)
    row_lse = rows[0:8].reshape(NI)
    row_partner = rows[8:16].reshape(NI).astype(jnp.int32)
    most_two = rows[16, 0]
    col_lse = cols[0:4].reshape(NJ)
    most_one = cols[16, 0]

    block = (z + jnp.array(OFFSETS)[:, None] + 4 * jnp.arange(2)[None, :] + NZ) % NZ
    index = ((block * (NY * NXH) + uhigh) * ROWS + xl * HALF)[:, :, None] + jnp.arange(HALF)
    positive = (index.reshape(1, NJ) == row_partner[:, None]).astype(jnp.float32)
    both = jnp.exp(scores - row_lse[:, None]) + jnp.exp(scores - col_lse[None, :])
    coupling = (0.5 * both - positive).astype(jnp.bfloat16)

    part_two = [
        (
            lax.dot_general(
                coupling, v1_all[x], (((0,), (0,)), ((), ())), preferred_element_type=jnp.float32
            )
            * (64.0 / most_one)
        ).astype(jnp.float16)
        for x in range(NXL)
    ]
    parts = [
        jnp.stack([part_two[x][g * GROUP : (g + 1) * GROUP] for x in range(NXL)])
        for g in range(4)
    ]
    parts = [parts[0]] + [to_plane(parts[g], OFFSETS[g]) for g in range(1, 4)]
    part_one = jnp.stack(
        [
            (
                jnp.dot(coupling, v2_all[x], preferred_element_type=jnp.float32)
                * (128.0 / most_two)
            ).astype(jnp.float16)
            for x in range(NXL)
        ]
    )
    one_parts = lax.all_to_all(part_one.reshape(16, ROWS, WIDTH), PLANE, 0, 0, tiled=True)

    joined = sum(part.astype(jnp.float32) for part in parts)
    here = jnp.where(xl == 0, joined[0], joined[1])
    there = (jnp.where(xl == 0, joined[1], joined[0]) * 0.25).astype(jnp.float16)
    here_far = (here[HALF:] * 0.25).astype(jnp.float16)
    side, far, far_side = (
        to_pair(there[:HALF], 0, 1),
        to_pair(here_far, 4, 0),
        to_pair(there[HALF:], 4, 1),
    )
    mine = (here[:HALF] + 4.0 * far.astype(jnp.float32)) * (most_one / 64.0)
    rest = (side.astype(jnp.float32) + far_side.astype(jnp.float32)) * (most_one / 16.0)
    grad_two = jnp.where(
        xl == 0, jnp.concatenate([mine, rest]), jnp.concatenate([rest, mine])
    )
    grad_one = jnp.sum(one_parts.astype(jnp.float32), axis=0) * (most_two / 128.0)
    return (grad_one, grad_two)


def solution(mesh):
    fine = Mesh(mesh.devices.reshape(NZ, NY, NXH, NXL, NC), EVERY)
    users = P(("z", "y", "xh"))
    both = P(("z", "y", "xh"), ("xl", "core"))
    return jax.shard_map(
        on_device,
        mesh=fine,
        in_specs=(both, both, users),
        out_specs=(both, both),
        check_vma=False,
    )
```

```python
import math

import jax
import jax.numpy as jnp
from jax import lax
from jax.experimental import pallas as pl
from jax.experimental.pallas import tpu as pltpu
from jax.sharding import Mesh
from jax.sharding import PartitionSpec as P

D = 2048
NZ, NY, NXH, NXL, NC = 8, 4, 2, 2, 2
PLANE = ("xl", "y", "xh")
OFFSETS = (0, -1, 1, -2)
GROUP = 128
EVERY = ("z", "y", "xh", "xl", "core")
ROWS = 128
HALF = 64
WIDTH = 512
NI = NY * NXH * ROWS
NJ = NZ * HALF
LANES = 128
SCALE = 2.0 / math.sqrt(D)
VMEM = pl.BlockSpec(memory_space=pltpu.VMEM)
SMEM = pl.BlockSpec(memory_space=pltpu.SMEM)


def limit(mib):
    return pltpu.CompilerParams(vmem_limit_bytes=mib * 1024 * 1024)


def score_kernel(v1_ref, *refs):
    group_refs, s_ref, v2_ref = refs[:4], refs[4], refs[5]
    for g in range(4):
        v2_ref[:, g * GROUP : (g + 1) * GROUP, :] = group_refs[g][...]
    contract = (((1,), (1,)), ((), ()))
    for u in range(NI // 256):
        rows = slice(u * 256, (u + 1) * 256)
        s_ref[rows, :] = lax.dot_general(
            v1_ref[0, rows, :], v2_ref[0], contract, preferred_element_type=jnp.float32
        ) + lax.dot_general(
            v1_ref[1, rows, :], v2_ref[1], contract, preferred_element_type=jnp.float32
        )


def partial_scores(v1_all, groups):
    return pl.pallas_call(
        score_kernel,
        out_shape=(
            jax.ShapeDtypeStruct((NI, NJ), jnp.float32),
            jax.ShapeDtypeStruct((NXL, NJ, WIDTH), jnp.bfloat16),
        ),
        in_specs=[VMEM] * 5,
        out_specs=(VMEM, VMEM),
        compiler_params=limit(8),
        cost_estimate=pl.CostEstimate(
            flops=2 * NI * NJ * NXL * WIDTH, bytes_accessed=6 * 2**20, transcendentals=0
        ),
    )(v1_all, *groups)


def diagonal():
    shape = (LANES, LANES)
    return lax.broadcasted_iota(jnp.int32, shape, 0) == lax.broadcasted_iota(jnp.int32, shape, 1)


def placed(z, g):
    first = lax.rem(z + OFFSETS[g] + NZ, NZ)
    return lax.rem(first, 4), first >= 4


def turned(row, trade):
    return jnp.where(trade, pltpu.roll(row, HALF, 1), row)


def stats_kernel(
    place_ref, own_ref, other_ref, partner_ref, most_ref, most_other_ref, s_ref, out_ref, pack_ref
):
    eye = diagonal()
    core = place_ref[0]
    pack_ref[...] = jnp.zeros_like(pack_ref)
    col_highest = jnp.full((1, NJ), -jnp.inf, jnp.float32)
    col_total = jnp.zeros((1, NJ), jnp.float32)
    for u in range(NI // LANES):
        rows = slice(u * LANES, (u + 1) * LANES)
        s = SCALE * (own_ref[rows, :] + other_ref[rows, :])
        s_ref[rows, :] = s
        highest = jnp.max(s, axis=1, keepdims=True)
        lse = highest + jnp.log(jnp.sum(jnp.exp(s - highest), axis=1, keepdims=True))
        pack_ref[0, u : u + 1, :] = jnp.sum(jnp.where(eye, lse, 0.0), axis=0, keepdims=True)
        higher = jnp.maximum(col_highest, jnp.max(s, axis=0, keepdims=True))
        col_total = col_total * jnp.exp(col_highest - higher) + jnp.sum(
            jnp.exp(s - higher), axis=0, keepdims=True
        )
        col_highest = higher
    col_lse = col_highest + jnp.log(col_total)
    for g in range(4):
        row, trade = placed(place_ref[2], g)
        pack_ref[1, pl.ds(row, 1), :] = turned(col_lse[:, g * LANES : (g + 1) * LANES], trade)
    most = jnp.max(jnp.maximum(most_ref[...], most_other_ref[...]), axis=1, keepdims=True)
    most = jnp.broadcast_to(jnp.maximum(most, 1e-30), (2, LANES))
    pack_ref[0, 8:9, :] = partner_ref[...].astype(jnp.float32)
    pack_ref[0, 9:10, :] = most[0:1, :]
    pack_ref[1, 9:10, :] = most[1:2, :]
    chosen = jnp.where(core == 0, pack_ref[0], pack_ref[1])
    for p in range(16):
        out_ref[p] = chosen


def local_stats(place, own, other, partner, most, most_other):
    return pl.pallas_call(
        stats_kernel,
        out_shape=(
            jax.ShapeDtypeStruct((NI, NJ), jnp.float32),
            jax.ShapeDtypeStruct((16, 16, LANES), jnp.float32),
        ),
        in_specs=[SMEM] + [VMEM] * 5,
        out_specs=(VMEM, VMEM),
        scratch_shapes=[pltpu.VMEM((2, 16, LANES), jnp.float32)],
        compiler_params=limit(8),
        cost_estimate=pl.CostEstimate(
            flops=10 * NI * NJ, bytes_accessed=6 * 2**20, transcendentals=2 * NI * NJ
        ),
    )(place, own, other, partner.reshape(1, ROWS), most, most_other)


def merged(lses):
    top = jnp.max(lses, axis=0)
    return top + jnp.log(jnp.sum(jnp.exp(lses - top[None]), axis=0))


def merge_kernel(place_ref, seen_ref, known_ref, cols_ref):
    core, xl = place_ref[0], place_ref[1]

    @pl.when(core == 0)
    def _():
        known_ref[0:8, :] = merged(seen_ref[:, 0:8, :])
        for u in range(8):
            known_ref[8 + u : 9 + u, :] = seen_ref[u, 8:9, :]

    @pl.when(core != 0)
    def _():
        known_ref[...] = jnp.zeros_like(known_ref)
        cols_ref[...] = merged(seen_ref[pl.ds(xl * NZ, NZ), 0:8, :])
        for g in range(4):
            row, trade = placed(place_ref[2], g)
            known_ref[g : g + 1, :] = turned(cols_ref[pl.ds(row, 1), :], trade)

    known_ref[16:24, :] = jnp.broadcast_to(jnp.max(seen_ref[:, 9:10, :], axis=0), (8, LANES))


def merge_stats(place, seen):
    return pl.pallas_call(
        merge_kernel,
        out_shape=jax.ShapeDtypeStruct((24, LANES), jnp.float32),
        in_specs=[SMEM, VMEM],
        out_specs=VMEM,
        scratch_shapes=[pltpu.VMEM((8, LANES), jnp.float32)],
        compiler_params=limit(2),
        cost_estimate=pl.CostEstimate(flops=10**5, bytes_accessed=2**17, transcendentals=2**14),
    )(place, seen)


def couple_kernel(place_ref, s_ref, known_ref, told_ref, c_ref, size_ref):
    core, xl, z, uhigh = place_ref[0], place_ref[1], place_ref[2], place_ref[3]
    rows = jnp.where(core == 0, known_ref[...], told_ref[...])
    cols = jnp.where(core == 0, told_ref[...], known_ref[...])
    eye = diagonal()
    lane = lax.broadcasted_iota(jnp.int32, (1, LANES), 1)
    index, col_lse = [], []
    for g in range(4):
        first = lax.rem(z + OFFSETS[g] + NZ, NZ)
        second = lax.rem(first + 4, NZ)
        user = jnp.where(lane < HALF, first, second) * (NY * NXH) + uhigh
        inside = jnp.where(lane < HALF, lane, lane - HALF)
        index.append((user * ROWS + xl * HALF + inside).astype(jnp.float32))
        col_lse.append(cols[g : g + 1, :])
    index = jnp.concatenate(index, axis=1)
    col_lse = jnp.concatenate(col_lse, axis=1)
    for u in range(NI // LANES):
        here = slice(u * LANES, (u + 1) * LANES)
        s = s_ref[here, :]
        row_lse = jnp.sum(jnp.where(eye, rows[u : u + 1, :], 0.0), axis=1, keepdims=True)
        partner = jnp.sum(jnp.where(eye, rows[8 + u : 9 + u, :], 0.0), axis=1, keepdims=True)
        both = jnp.exp(s - row_lse) + jnp.exp(s - col_lse)
        positive = (partner == index).astype(jnp.float32)
        c_ref[here, :] = (0.5 * both - positive).astype(jnp.bfloat16)
    size_ref[0:1, :] = rows[16:17, :]
    size_ref[1:2, :] = cols[16:17, :]


def coupling_of(place, scores, known, told):
    return pl.pallas_call(
        couple_kernel,
        out_shape=(
            jax.ShapeDtypeStruct((NI, NJ), jnp.bfloat16),
            jax.ShapeDtypeStruct((2, LANES), jnp.float32),
        ),
        in_specs=[SMEM] + [VMEM] * 3,
        out_specs=(VMEM, VMEM),
        compiler_params=limit(5),
        cost_estimate=pl.CostEstimate(
            flops=8 * NI * NJ, bytes_accessed=3 * 2**20, transcendentals=2 * NI * NJ
        ),
    )(place, scores, known, told)


def swap(x, axis):
    return lax.ppermute(x, axis, [(0, 1), (1, 0)])


def stat_groups():
    def number(z, y, xh, xl, c):
        return (((z * NY + y) * NXH + xh) * NXL + xl) * NC + c

    planes = [
        [number(z, y, xh, xl, 0) for xl in range(NXL) for y in range(NY) for xh in range(NXH)]
        for z in range(NZ)
    ]
    columns = [
        [number(z, y, xh, xl, 1) for xl in range(NXL) for z in range(NZ)]
        for y in range(NY)
        for xh in range(NXH)
    ]
    return planes + columns


def to_plane(x, dz):
    return lax.ppermute(x, "z", [(z, (z + dz) % NZ) for z in range(NZ)])


def largest(x):
    return jnp.max(jnp.abs(x), axis=(0, 1)).astype(jnp.float32)


def on_device(view_one, view_two, partner):
    z = lax.axis_index("z")
    uhigh = lax.axis_index("y") * NXH + lax.axis_index("xh")
    xl = lax.axis_index("xl")
    core = lax.axis_index("core")
    place = jnp.stack([core, xl, z, uhigh]).astype(jnp.int32)

    keep = jnp.where(xl == 0, view_two[:HALF], view_two[HALF:])
    give = jnp.where(xl == 0, view_two[HALF:], view_two[:HALF])
    side = swap(give, "xl")
    copies = jnp.broadcast_to(view_one[None], (16, ROWS, WIDTH))
    copies, side = lax.optimization_barrier((copies, side))
    here = jnp.where(xl == 0, jnp.stack([keep, side]), jnp.stack([side, keep]))
    pair = jnp.concatenate([here, to_plane(here, 4)], axis=1)
    groups = [pair] + [to_plane(pair, -dz) for dz in OFFSETS[1:]]
    v1_all = lax.all_to_all(copies, PLANE, 0, 0, tiled=True).reshape(NXL, NI, WIDTH)

    own, v2_all = partial_scores(v1_all, groups)
    other = swap(own, "core")
    most = jnp.stack([largest(v2_all), largest(v1_all)])
    most_other = swap(most, "core")

    scores, pack = local_stats(place, own, other, partner, most, most_other)
    seen = lax.all_to_all(
        pack, EVERY, 0, 0, axis_index_groups=stat_groups(), tiled=True
    )
    known = merge_stats(place, seen)
    coupling, sizes = coupling_of(place, scores, known, swap(known, "core"))
    most_two, most_one = sizes[0, 0], sizes[1, 0]

    part_one = (
        lax.dot_general(
            jnp.broadcast_to(coupling[None], (NXL, NI, NJ)),
            v2_all,
            (((2,), (1,)), ((0,), (0,))),
            preferred_element_type=jnp.float32,
        )
        * (128.0 / most_two)
    ).astype(jnp.float16)
    coupling, part_one = lax.optimization_barrier((coupling, part_one))
    one_parts = lax.all_to_all(part_one.reshape(16, ROWS, WIDTH), PLANE, 0, 0, tiled=True)
    part_two = (
        lax.dot_general(
            jnp.broadcast_to(coupling[None], (NXL, NI, NJ)),
            v1_all,
            (((1,), (1,)), ((0,), (0,))),
            preferred_element_type=jnp.float32,
        )
        * (64.0 / most_one)
    ).astype(jnp.float16)
    parts = [part_two[:, :GROUP]] + [
        to_plane(part_two[:, g * GROUP : (g + 1) * GROUP], OFFSETS[g]) for g in range(1, 4)
    ]
    joined = sum(part.astype(jnp.float32) for part in parts)
    far = to_plane((joined[:, HALF:] * 0.25).astype(jnp.float16), 4)
    total = (joined[:, :HALF] + 4.0 * far.astype(jnp.float32)) * (most_one / 64.0)
    stay = jnp.where(xl == 0, total[0], total[1])
    come = swap(jnp.where(xl == 0, total[1], total[0]), "xl")
    grad_two = jnp.where(
        xl == 0, jnp.concatenate([stay, come]), jnp.concatenate([come, stay])
    )
    grad_one = jnp.sum(one_parts.astype(jnp.float32), axis=0) * (most_two / 128.0)
    return (grad_one, grad_two)


def solution(mesh):
    fine = Mesh(mesh.devices.reshape(NZ, NY, NXH, NXL, NC), EVERY)
    users = P(("z", "y", "xh"))
    both = P(("z", "y", "xh"), ("xl", "core"))
    return jax.shard_map(
        on_device,
        mesh=fine,
        in_specs=(both, both, users),
        out_specs=(both, both),
        check_vma=False,
    )
```

```python
import math

import jax
import jax.numpy as jnp
from jax import lax
from jax.experimental import pallas as pl
from jax.experimental.pallas import tpu as pltpu
from jax.sharding import Mesh
from jax.sharding import PartitionSpec as P

D = 2048
NZ, NY, NXH, NXL, NC = 8, 4, 2, 2, 2
PLANE = ("xl", "y", "xh")
OFFSETS = (0, -1, 1, -2)
GROUP = 128
EVERY = ("z", "y", "xh", "xl", "core")
ROWS = 128
HALF = 64
WIDTH = 512
NI = NY * NXH * ROWS
NJ = NZ * HALF
LANES = 128
SCALE = 2.0 / math.sqrt(D)
VMEM = pl.BlockSpec(memory_space=pltpu.VMEM)
SMEM = pl.BlockSpec(memory_space=pltpu.SMEM)


def limit(mib):
    return pltpu.CompilerParams(vmem_limit_bytes=mib * 1024 * 1024)


def copies_kernel(x_ref, o_ref, sems):
    copies = [pltpu.make_async_copy(x_ref, o_ref.at[p], sems.at[p]) for p in range(16)]
    for copy in copies:
        copy.start()
    for copy in copies:
        copy.wait()


def sixteen_copies(x):
    return pl.pallas_call(
        copies_kernel,
        out_shape=jax.ShapeDtypeStruct((16, ROWS, WIDTH), x.dtype),
        in_specs=[VMEM],
        out_specs=pl.BlockSpec(memory_space=pl.ANY),
        scratch_shapes=[pltpu.SemaphoreType.DMA((16,))],
        compiler_params=limit(1),
        cost_estimate=pl.CostEstimate(flops=0, bytes_accessed=3 * 2**20, transcendentals=0),
    )(x)


def join_kernel(own_ref, next_ref, last_ref, two0_ref, two1_ref, v2_ref, most_ref):
    v2_ref[:, :GROUP, :] = own_ref[...]
    v2_ref[:, GROUP : 2 * GROUP, :] = next_ref[...]
    v2_ref[:, 2 * GROUP : 3 * GROUP, :] = last_ref[...]
    v2_ref[0, 3 * GROUP : 3 * GROUP + HALF, :] = two0_ref[HALF:, :]
    v2_ref[0, 3 * GROUP + HALF :, :] = two0_ref[:HALF, :]
    v2_ref[1, 3 * GROUP :, :] = two1_ref[...]
    size = jnp.abs(jnp.maximum(jnp.abs(v2_ref[0]), jnp.abs(v2_ref[1])).astype(jnp.float32))
    most_ref[...] = jnp.max(size, axis=0, keepdims=True)


def join(parts):
    return pl.pallas_call(
        join_kernel,
        out_shape=(
            jax.ShapeDtypeStruct((NXL, NJ, WIDTH), jnp.bfloat16),
            jax.ShapeDtypeStruct((1, WIDTH), jnp.float32),
        ),
        in_specs=[VMEM] * 5,
        out_specs=(VMEM, VMEM),
        compiler_params=limit(4),
        cost_estimate=pl.CostEstimate(flops=2**20, bytes_accessed=2**21, transcendentals=0),
    )(*parts)


def score_kernel(v1_ref, v2_hbm, s_ref, v2_ref, sems):
    copies = [pltpu.make_async_copy(v2_hbm.at[x], v2_ref.at[x], sems.at[x]) for x in range(NXL)]
    for copy in copies:
        copy.start()
    for copy in copies:
        copy.wait()
    contract = (((1,), (1,)), ((), ()))
    for u in range(NI // 256):
        rows = slice(u * 256, (u + 1) * 256)
        s_ref[rows, :] = lax.dot_general(
            v1_ref[0, rows, :], v2_ref[0], contract, preferred_element_type=jnp.float32
        ) + lax.dot_general(
            v1_ref[1, rows, :], v2_ref[1], contract, preferred_element_type=jnp.float32
        )


def partial_scores(v1_all, v2_all):
    return pl.pallas_call(
        score_kernel,
        out_shape=jax.ShapeDtypeStruct((NI, NJ), jnp.float32),
        in_specs=[VMEM, pl.BlockSpec(memory_space=pl.ANY)],
        out_specs=VMEM,
        scratch_shapes=[
            pltpu.VMEM((NXL, NJ, WIDTH), jnp.bfloat16),
            pltpu.SemaphoreType.DMA((NXL,)),
        ],
        compiler_params=limit(8),
        cost_estimate=pl.CostEstimate(
            flops=2 * NI * NJ * NXL * WIDTH, bytes_accessed=6 * 2**20, transcendentals=0
        ),
    )(v1_all, v2_all)


def diagonal():
    shape = (LANES, LANES)
    return lax.broadcasted_iota(jnp.int32, shape, 0) == lax.broadcasted_iota(jnp.int32, shape, 1)


def placed(z, g):
    first = lax.rem(z + OFFSETS[g] + NZ, NZ)
    return lax.rem(first, 4), first >= 4


def turned(row, trade):
    return jnp.where(trade, pltpu.roll(row, HALF, 1), row)


def stats_kernel(
    place_ref, own_ref, other_ref, partner_ref, most_ref, most_other_ref, s_ref, out_ref, pack_ref
):
    eye = diagonal()
    core = place_ref[0]
    pack_ref[...] = jnp.zeros_like(pack_ref)
    col_highest = jnp.full((1, NJ), -jnp.inf, jnp.float32)
    col_total = jnp.zeros((1, NJ), jnp.float32)
    for u in range(NI // LANES):
        rows = slice(u * LANES, (u + 1) * LANES)
        s = SCALE * (own_ref[rows, :] + other_ref[rows, :])
        s_ref[rows, :] = s
        highest = jnp.max(s, axis=1, keepdims=True)
        lse = highest + jnp.log(jnp.sum(jnp.exp(s - highest), axis=1, keepdims=True))
        pack_ref[0, u : u + 1, :] = jnp.sum(jnp.where(eye, lse, 0.0), axis=0, keepdims=True)
        higher = jnp.maximum(col_highest, jnp.max(s, axis=0, keepdims=True))
        col_total = col_total * jnp.exp(col_highest - higher) + jnp.sum(
            jnp.exp(s - higher), axis=0, keepdims=True
        )
        col_highest = higher
    col_lse = col_highest + jnp.log(col_total)
    for g in range(4):
        row, trade = placed(place_ref[2], g)
        pack_ref[1, pl.ds(row, 1), :] = turned(col_lse[:, g * LANES : (g + 1) * LANES], trade)
    most = jnp.max(jnp.maximum(most_ref[...], most_other_ref[...]), axis=1, keepdims=True)
    most = jnp.broadcast_to(jnp.maximum(most, 1e-30), (2, LANES))
    pack_ref[0, 8:9, :] = partner_ref[...].astype(jnp.float32)
    pack_ref[0, 9:10, :] = most[0:1, :]
    pack_ref[1, 9:10, :] = most[1:2, :]
    chosen = jnp.where(core == 0, pack_ref[0], pack_ref[1])
    for p in range(16):
        out_ref[p] = chosen


def local_stats(place, own, other, partner, most, most_other):
    return pl.pallas_call(
        stats_kernel,
        out_shape=(
            jax.ShapeDtypeStruct((NI, NJ), jnp.float32),
            jax.ShapeDtypeStruct((16, 16, LANES), jnp.float32),
        ),
        in_specs=[SMEM] + [VMEM] * 5,
        out_specs=(VMEM, VMEM),
        scratch_shapes=[pltpu.VMEM((2, 16, LANES), jnp.float32)],
        compiler_params=limit(8),
        cost_estimate=pl.CostEstimate(
            flops=10 * NI * NJ, bytes_accessed=6 * 2**20, transcendentals=2 * NI * NJ
        ),
    )(place, own, other, partner.reshape(1, ROWS), most, most_other)


def merged(lses):
    top = jnp.max(lses, axis=0)
    return top + jnp.log(jnp.sum(jnp.exp(lses - top[None]), axis=0))


def merge_kernel(place_ref, seen_ref, known_ref, cols_ref):
    core, xl = place_ref[0], place_ref[1]

    @pl.when(core == 0)
    def _():
        known_ref[0:8, :] = merged(seen_ref[:, 0:8, :])
        for u in range(8):
            known_ref[8 + u : 9 + u, :] = seen_ref[u, 8:9, :]

    @pl.when(core != 0)
    def _():
        known_ref[...] = jnp.zeros_like(known_ref)
        cols_ref[...] = merged(seen_ref[pl.ds(xl * NZ, NZ), 0:8, :])
        for g in range(4):
            row, trade = placed(place_ref[2], g)
            known_ref[g : g + 1, :] = turned(cols_ref[pl.ds(row, 1), :], trade)

    known_ref[16:24, :] = jnp.broadcast_to(jnp.max(seen_ref[:, 9:10, :], axis=0), (8, LANES))


def merge_stats(place, seen):
    return pl.pallas_call(
        merge_kernel,
        out_shape=jax.ShapeDtypeStruct((24, LANES), jnp.float32),
        in_specs=[SMEM, VMEM],
        out_specs=VMEM,
        scratch_shapes=[pltpu.VMEM((8, LANES), jnp.float32)],
        compiler_params=limit(2),
        cost_estimate=pl.CostEstimate(flops=10**5, bytes_accessed=2**17, transcendentals=2**14),
    )(place, seen)


def couple_kernel(place_ref, s_ref, known_ref, told_ref, c_ref, size_ref):
    core, xl, z, uhigh = place_ref[0], place_ref[1], place_ref[2], place_ref[3]
    rows = jnp.where(core == 0, known_ref[...], told_ref[...])
    cols = jnp.where(core == 0, told_ref[...], known_ref[...])
    eye = diagonal()
    lane = lax.broadcasted_iota(jnp.int32, (1, LANES), 1)
    index, col_lse = [], []
    for g in range(4):
        first = lax.rem(z + OFFSETS[g] + NZ, NZ)
        second = lax.rem(first + 4, NZ)
        user = jnp.where(lane < HALF, first, second) * (NY * NXH) + uhigh
        inside = jnp.where(lane < HALF, lane, lane - HALF)
        index.append((user * ROWS + xl * HALF + inside).astype(jnp.float32))
        col_lse.append(cols[g : g + 1, :])
    index = jnp.concatenate(index, axis=1)
    col_lse = jnp.concatenate(col_lse, axis=1)
    for u in range(NI // LANES):
        here = slice(u * LANES, (u + 1) * LANES)
        s = s_ref[here, :]
        row_lse = jnp.sum(jnp.where(eye, rows[u : u + 1, :], 0.0), axis=1, keepdims=True)
        partner = jnp.sum(jnp.where(eye, rows[8 + u : 9 + u, :], 0.0), axis=1, keepdims=True)
        both = jnp.exp(s - row_lse) + jnp.exp(s - col_lse)
        positive = (partner == index).astype(jnp.float32)
        c_ref[here, :] = (0.5 * both - positive).astype(jnp.bfloat16)
    size_ref[0:1, :] = rows[16:17, :]
    size_ref[1:2, :] = cols[16:17, :]


def coupling_of(place, scores, known, told):
    return pl.pallas_call(
        couple_kernel,
        out_shape=(
            jax.ShapeDtypeStruct((NI, NJ), jnp.bfloat16),
            jax.ShapeDtypeStruct((2, LANES), jnp.float32),
        ),
        in_specs=[SMEM] + [VMEM] * 3,
        out_specs=(VMEM, VMEM),
        compiler_params=limit(5),
        cost_estimate=pl.CostEstimate(
            flops=8 * NI * NJ, bytes_accessed=3 * 2**20, transcendentals=2 * NI * NJ
        ),
    )(place, scores, known, told)


def swap(x, axis):
    return lax.ppermute(x, axis, [(0, 1), (1, 0)])


def stat_groups():
    def number(z, y, xh, xl, c):
        return (((z * NY + y) * NXH + xh) * NXL + xl) * NC + c

    planes = [
        [number(z, y, xh, xl, 0) for xl in range(NXL) for y in range(NY) for xh in range(NXH)]
        for z in range(NZ)
    ]
    columns = [
        [number(z, y, xh, xl, 1) for xl in range(NXL) for z in range(NZ)]
        for y in range(NY)
        for xh in range(NXH)
    ]
    return planes + columns


def to_plane(x, dz):
    return lax.ppermute(x, "z", [(z, (z + dz) % NZ) for z in range(NZ)])


def largest(x):
    return jnp.max(jnp.abs(x), axis=(0, 1)).astype(jnp.float32)


def on_device(view_one, view_two, partner):
    z = lax.axis_index("z")
    uhigh = lax.axis_index("y") * NXH + lax.axis_index("xh")
    xl = lax.axis_index("xl")
    core = lax.axis_index("core")
    place = jnp.stack([core, xl, z, uhigh]).astype(jnp.int32)

    keep = jnp.where(xl == 0, view_two[:HALF], view_two[HALF:])
    give = jnp.where(xl == 0, view_two[HALF:], view_two[:HALF])
    side = swap(give, "xl")
    copies = sixteen_copies(view_one)
    copies, side = lax.optimization_barrier((copies, side))
    here = jnp.where(xl == 0, jnp.stack([keep, side]), jnp.stack([side, keep]))
    pair = jnp.concatenate([here, to_plane(here, 4)], axis=1)
    v2_all, most_v2 = join(
        [
            pair,
            to_plane(pair, 1),
            to_plane(pair, -1),
            to_plane(pair[0], -2),
            to_plane(pair[1], 2),
        ]
    )
    v1_all = lax.all_to_all(copies, PLANE, 0, 0, tiled=True).reshape(NXL, NI, WIDTH)

    own = partial_scores(v1_all, v2_all)
    other = swap(own, "core")
    most = jnp.concatenate([most_v2, largest(v1_all)[None]])
    most_other = swap(most, "core")

    scores, pack = local_stats(place, own, other, partner, most, most_other)
    seen = lax.all_to_all(
        pack, EVERY, 0, 0, axis_index_groups=stat_groups(), tiled=True
    )
    known = merge_stats(place, seen)
    coupling, sizes = coupling_of(place, scores, known, swap(known, "core"))
    most_two, most_one = sizes[0, 0], sizes[1, 0]

    part_two = [
        (
            lax.dot_general(
                coupling, v1_all[x], (((0,), (0,)), ((), ())), preferred_element_type=jnp.float32
            )
            * (64.0 / most_one)
        ).astype(jnp.float16)
        for x in range(NXL)
    ]
    coupling, part_two = lax.optimization_barrier((coupling, part_two))

    def group(g):
        return jnp.stack([part[g * GROUP : (g + 1) * GROUP] for part in part_two])

    before, after = to_plane(group(1), -1), to_plane(group(2), 1)
    two0 = to_plane(part_two[0][3 * GROUP :], 2)
    two1 = to_plane(part_two[1][3 * GROUP :], -2)
    part_one = (
        lax.dot_general(
            jnp.broadcast_to(coupling[None], (NXL, NI, NJ)),
            v2_all,
            (((2,), (1,)), ((0,), (0,))),
            preferred_element_type=jnp.float32,
        )
        * (128.0 / most_two)
    ).astype(jnp.float16)
    one_parts = lax.all_to_all(part_one.reshape(16, ROWS, WIDTH), PLANE, 0, 0, tiled=True)
    two = jnp.stack([jnp.concatenate([two0[HALF:], two0[:HALF]]), two1])
    joined = sum(part.astype(jnp.float32) for part in (group(0), before, after, two))
    far = to_plane((joined[:, HALF:] * 0.25).astype(jnp.float16), 4)
    total = (joined[:, :HALF] + 4.0 * far.astype(jnp.float32)) * (most_one / 64.0)
    stay = jnp.where(xl == 0, total[0], total[1])
    come = swap(jnp.where(xl == 0, total[1], total[0]), "xl")
    grad_two = jnp.where(
        xl == 0, jnp.concatenate([stay, come]), jnp.concatenate([come, stay])
    )
    grad_one = jnp.sum(one_parts.astype(jnp.float32) * (most_two / 128.0), axis=0)
    return (grad_one, grad_two)


def solution(mesh):
    fine = Mesh(mesh.devices.reshape(NZ, NY, NXH, NXL, NC), EVERY)
    users = P(("z", "y", "xh"))
    both = P(("z", "y", "xh"), ("xl", "core"))
    return jax.shard_map(
        on_device,
        mesh=fine,
        in_specs=(both, both, users),
        out_specs=(both, both),
        check_vma=False,
    )
```

```python
import functools
import math

import jax
import jax.numpy as jnp
from jax import lax
from jax.experimental import pallas as pl
from jax.experimental.pallas import tpu as pltpu
from jax.sharding import Mesh
from jax.sharding import PartitionSpec as P

D = 2048
NZ, NY, NXH, NXL, NC = 8, 4, 2, 2, 2
PLANE = ("xl", "y", "xh")
OFFSETS = (0, -1, 1, -2)
GROUP = 128
EVERY = ("z", "y", "xh", "xl", "core")
ROWS = 128
HALF = 64
WIDTH = 512
NI = NY * NXH * ROWS
NJ = NZ * HALF
NP = NI // 2
LANES = 128
SCALE = 2.0 / math.sqrt(D)
VMEM = pl.BlockSpec(memory_space=pltpu.VMEM)
SMEM = pl.BlockSpec(memory_space=pltpu.SMEM)


def limit(mib):
    return pltpu.CompilerParams(vmem_limit_bytes=mib * 1024 * 1024)


def copies_kernel(x_ref, o_ref, sems):
    copies = [pltpu.make_async_copy(x_ref, o_ref.at[p], sems.at[p]) for p in range(16)]
    for copy in copies:
        copy.start()
    for copy in copies:
        copy.wait()


def sixteen_copies(x):
    return pl.pallas_call(
        copies_kernel,
        out_shape=jax.ShapeDtypeStruct((16, ROWS, WIDTH), x.dtype),
        in_specs=[pl.BlockSpec(memory_space=pltpu.HBM)],
        out_specs=pl.BlockSpec(memory_space=pltpu.HBM),
        scratch_shapes=[pltpu.SemaphoreType.DMA((16,))],
        compiler_params=limit(1),
        cost_estimate=pl.CostEstimate(flops=0, bytes_accessed=3 * 2**20, transcendentals=0),
    )(x)


def join_kernel(own_ref, next_ref, last_ref, two0_ref, two1_ref, v2_ref, most_ref):
    v2_ref[:, :GROUP, :] = own_ref[...]
    v2_ref[:, GROUP : 2 * GROUP, :] = next_ref[...]
    v2_ref[:, 2 * GROUP : 3 * GROUP, :] = last_ref[...]
    v2_ref[0, 3 * GROUP : 3 * GROUP + HALF, :] = two0_ref[HALF:, :]
    v2_ref[0, 3 * GROUP + HALF :, :] = two0_ref[:HALF, :]
    v2_ref[1, 3 * GROUP :, :] = two1_ref[...]
    size = jnp.abs(jnp.maximum(jnp.abs(v2_ref[0]), jnp.abs(v2_ref[1])).astype(jnp.float32))
    most_ref[...] = jnp.max(size, axis=0, keepdims=True)


def join(parts):
    return pl.pallas_call(
        join_kernel,
        out_shape=(
            jax.ShapeDtypeStruct((NXL, NJ, WIDTH), jnp.bfloat16),
            jax.ShapeDtypeStruct((1, WIDTH), jnp.float32),
        ),
        in_specs=[VMEM] * 5,
        out_specs=(VMEM, VMEM),
        compiler_params=limit(4),
        cost_estimate=pl.CostEstimate(flops=2**20, bytes_accessed=2**21, transcendentals=0),
    )(*parts)


def score_kernel(part, v1_ref, v2_hbm, s_ref, v2_ref, sems):
    copies = [pltpu.make_async_copy(v2_hbm.at[x], v2_ref.at[x], sems.at[x]) for x in range(NXL)]
    for copy in copies:
        copy.start()
    for copy in copies:
        copy.wait()
    contract = (((1,), (1,)), ((), ()))
    for u in range(NP // 256):
        rows = slice(u * 256, (u + 1) * 256)
        users = slice(part * NP + u * 256, part * NP + (u + 1) * 256)
        s_ref[rows, :] = lax.dot_general(
            v1_ref[0, users, :], v2_ref[0], contract, preferred_element_type=jnp.float32
        ) + lax.dot_general(
            v1_ref[1, users, :], v2_ref[1], contract, preferred_element_type=jnp.float32
        )


def partial_scores(part, v1_all, v2_all):
    return pl.pallas_call(
        functools.partial(score_kernel, part),
        out_shape=jax.ShapeDtypeStruct((NP, NJ), jnp.float32),
        in_specs=[VMEM, pl.BlockSpec(memory_space=pl.ANY)],
        out_specs=VMEM,
        scratch_shapes=[
            pltpu.VMEM((NXL, NJ, WIDTH), jnp.bfloat16),
            pltpu.SemaphoreType.DMA((NXL,)),
        ],
        compiler_params=limit(6),
        cost_estimate=pl.CostEstimate(
            flops=2 * NP * NJ * NXL * WIDTH, bytes_accessed=3 * 2**20, transcendentals=0
        ),
    )(v1_all, v2_all)


def diagonal():
    shape = (LANES, LANES)
    return lax.broadcasted_iota(jnp.int32, shape, 0) == lax.broadcasted_iota(jnp.int32, shape, 1)


def placed(z, g):
    first = lax.rem(z + OFFSETS[g] + NZ, NZ)
    return lax.rem(first, 4), first >= 4


def turned(row, trade):
    return jnp.where(trade, pltpu.roll(row, HALF, 1), row)


def block_stats(own_ref, other_ref, s_ref, row_ref, col_highest, col_total):
    eye = diagonal()
    for u in range(NP // LANES):
        rows = slice(u * LANES, (u + 1) * LANES)
        s = SCALE * (own_ref[rows, :] + other_ref[rows, :])
        s_ref[rows, :] = s
        highest = jnp.max(s, axis=1, keepdims=True)
        lse = highest + jnp.log(jnp.sum(jnp.exp(s - highest), axis=1, keepdims=True))
        row_ref[u : u + 1, :] = jnp.sum(jnp.where(eye, lse, 0.0), axis=0, keepdims=True)
        higher = jnp.maximum(col_highest, jnp.max(s, axis=0, keepdims=True))
        col_total = col_total * jnp.exp(col_highest - higher) + jnp.sum(
            jnp.exp(s - higher), axis=0, keepdims=True
        )
        col_highest = higher
    return col_highest, col_total


def first_kernel(own_ref, other_ref, s_ref, row_ref, col_ref):
    highest, total = block_stats(
        own_ref,
        other_ref,
        s_ref,
        row_ref,
        jnp.full((1, NJ), -jnp.inf, jnp.float32),
        jnp.zeros((1, NJ), jnp.float32),
    )
    col_ref[0:1, :] = highest
    col_ref[1:2, :] = total


def first_stats(own, other):
    return pl.pallas_call(
        first_kernel,
        out_shape=(
            jax.ShapeDtypeStruct((NP, NJ), jnp.float32),
            jax.ShapeDtypeStruct((NP // LANES, LANES), jnp.float32),
            jax.ShapeDtypeStruct((2, NJ), jnp.float32),
        ),
        in_specs=[VMEM] * 2,
        out_specs=(VMEM,) * 3,
        compiler_params=limit(4),
        cost_estimate=pl.CostEstimate(
            flops=10 * NP * NJ, bytes_accessed=3 * 2**20, transcendentals=2 * NP * NJ
        ),
    )(own, other)


def second_kernel(
    place_ref,
    own_ref,
    other_ref,
    first_ref,
    col_ref,
    partner_ref,
    most_ref,
    most_other_ref,
    s_ref,
    out_ref,
    pack_ref,
):
    half = NP // LANES
    pack_ref[...] = jnp.zeros_like(pack_ref)
    pack_ref[0, 0:half, :] = first_ref[...]
    col_highest, col_total = block_stats(
        own_ref,
        other_ref,
        s_ref,
        pack_ref.at[0, half : 2 * half, :],
        col_ref[0:1, :],
        col_ref[1:2, :],
    )
    col_lse = col_highest + jnp.log(col_total)
    for g in range(4):
        row, trade = placed(place_ref[2], g)
        pack_ref[1, pl.ds(row, 1), :] = turned(col_lse[:, g * LANES : (g + 1) * LANES], trade)
    most = jnp.max(jnp.maximum(most_ref[...], most_other_ref[...]), axis=1, keepdims=True)
    most = jnp.broadcast_to(jnp.maximum(most, 1e-30), (2, LANES))
    pack_ref[0, 8:9, :] = partner_ref[...].astype(jnp.float32)
    pack_ref[0, 9:10, :] = most[0:1, :]
    pack_ref[1, 9:10, :] = most[1:2, :]
    chosen = jnp.where(place_ref[0] == 0, pack_ref[0], pack_ref[1])
    for p in range(16):
        out_ref[p] = chosen


def second_stats(place, own, other, first, cols, partner, most, most_other):
    return pl.pallas_call(
        second_kernel,
        out_shape=(
            jax.ShapeDtypeStruct((NP, NJ), jnp.float32),
            jax.ShapeDtypeStruct((16, 16, LANES), jnp.float32),
        ),
        in_specs=[SMEM] + [VMEM] * 7,
        out_specs=(VMEM, VMEM),
        scratch_shapes=[pltpu.VMEM((2, 16, LANES), jnp.float32)],
        compiler_params=limit(4),
        cost_estimate=pl.CostEstimate(
            flops=10 * NP * NJ, bytes_accessed=3 * 2**20, transcendentals=2 * NP * NJ
        ),
    )(place, own, other, first, cols, partner.reshape(1, ROWS), most, most_other)


def merged(lses):
    top = jnp.max(lses, axis=0)
    return top + jnp.log(jnp.sum(jnp.exp(lses - top[None]), axis=0))


def merge_kernel(place_ref, seen_ref, known_ref, cols_ref):
    core, xl = place_ref[0], place_ref[1]

    @pl.when(core == 0)
    def _():
        known_ref[0:8, :] = merged(seen_ref[:, 0:8, :])
        for u in range(8):
            known_ref[8 + u : 9 + u, :] = seen_ref[u, 8:9, :]

    @pl.when(core != 0)
    def _():
        known_ref[...] = jnp.zeros_like(known_ref)
        cols_ref[...] = merged(seen_ref[pl.ds(xl * NZ, NZ), 0:8, :])
        for g in range(4):
            row, trade = placed(place_ref[2], g)
            known_ref[g : g + 1, :] = turned(cols_ref[pl.ds(row, 1), :], trade)

    known_ref[16:24, :] = jnp.broadcast_to(jnp.max(seen_ref[:, 9:10, :], axis=0), (8, LANES))


def merge_stats(place, seen):
    return pl.pallas_call(
        merge_kernel,
        out_shape=jax.ShapeDtypeStruct((24, LANES), jnp.float32),
        in_specs=[SMEM, VMEM],
        out_specs=VMEM,
        scratch_shapes=[pltpu.VMEM((8, LANES), jnp.float32)],
        compiler_params=limit(2),
        cost_estimate=pl.CostEstimate(flops=10**5, bytes_accessed=2**17, transcendentals=2**14),
    )(place, seen)


def couple_kernel(
    place_ref,
    s0_ref,
    s1_ref,
    known_ref,
    told_ref,
    c_ref,
    give_one_ref,
    give_two_ref,
    take_one_ref,
    take_two_ref,
):
    core, xl, z, uhigh = place_ref[0], place_ref[1], place_ref[2], place_ref[3]
    rows = jnp.where(core == 0, known_ref[...], told_ref[...])
    cols = jnp.where(core == 0, told_ref[...], known_ref[...])
    eye = diagonal()
    lane = lax.broadcasted_iota(jnp.int32, (1, LANES), 1)
    index, col_lse = [], []
    for g in range(4):
        first = lax.rem(z + OFFSETS[g] + NZ, NZ)
        second = lax.rem(first + 4, NZ)
        user = jnp.where(lane < HALF, first, second) * (NY * NXH) + uhigh
        inside = jnp.where(lane < HALF, lane, lane - HALF)
        index.append((user * ROWS + xl * HALF + inside).astype(jnp.float32))
        col_lse.append(cols[g : g + 1, :])
    index = jnp.concatenate(index, axis=1)
    col_lse = jnp.concatenate(col_lse, axis=1)
    for u in range(NI // LANES):
        here = slice(u * LANES, (u + 1) * LANES)
        half_ref = s0_ref if u < NP // LANES else s1_ref
        start = u * LANES % NP
        s = half_ref[start : start + LANES, :]
        row_lse = jnp.sum(jnp.where(eye, rows[u : u + 1, :], 0.0), axis=1, keepdims=True)
        partner = jnp.sum(jnp.where(eye, rows[8 + u : 9 + u, :], 0.0), axis=1, keepdims=True)
        both = jnp.exp(s - row_lse) + jnp.exp(s - col_lse)
        positive = (partner == index).astype(jnp.float32)
        c_ref[here, :] = (0.5 * both - positive).astype(jnp.bfloat16)
    most_two = jnp.concatenate([rows[16:17, :]] * 4, axis=1)
    most_one = jnp.concatenate([cols[16:17, :]] * 4, axis=1)
    give_one_ref[...] = 128.0 / most_two
    take_one_ref[...] = most_two / 128.0
    give_two_ref[...] = 64.0 / most_one
    take_two_ref[...] = most_one / 64.0


def coupling_of(place, scores0, scores1, known, told):
    return pl.pallas_call(
        couple_kernel,
        out_shape=(
            jax.ShapeDtypeStruct((NI, NJ), jnp.bfloat16),
        )
        + (jax.ShapeDtypeStruct((1, WIDTH), jnp.float32),) * 4,
        in_specs=[SMEM] + [VMEM] * 4,
        out_specs=(VMEM,) * 5,
        compiler_params=limit(5),
        cost_estimate=pl.CostEstimate(
            flops=8 * NI * NJ, bytes_accessed=3 * 2**20, transcendentals=2 * NI * NJ
        ),
    )(place, scores0, scores1, known, told)


def swap(x, axis):
    return lax.ppermute(x, axis, [(0, 1), (1, 0)])


def stat_groups():
    def number(z, y, xh, xl, c):
        return (((z * NY + y) * NXH + xh) * NXL + xl) * NC + c

    planes = [
        [number(z, y, xh, xl, 0) for xl in range(NXL) for y in range(NY) for xh in range(NXH)]
        for z in range(NZ)
    ]
    columns = [
        [number(z, y, xh, xl, 1) for xl in range(NXL) for z in range(NZ)]
        for y in range(NY)
        for xh in range(NXH)
    ]
    return planes + columns


def to_plane(x, dz):
    return lax.ppermute(x, "z", [(z, (z + dz) % NZ) for z in range(NZ)])


def largest(x):
    return jnp.max(jnp.abs(x), axis=(0, 1)).astype(jnp.float32)


def on_device(view_one, view_two, partner):
    z = lax.axis_index("z")
    uhigh = lax.axis_index("y") * NXH + lax.axis_index("xh")
    xl = lax.axis_index("xl")
    core = lax.axis_index("core")
    place = jnp.stack([core, xl, z, uhigh]).astype(jnp.int32)

    keep = jnp.where(xl == 0, view_two[:HALF], view_two[HALF:])
    give = jnp.where(xl == 0, view_two[HALF:], view_two[:HALF])
    side = swap(give, "xl")
    copies = sixteen_copies(view_one)
    copies, side = lax.optimization_barrier((copies, side))
    here = jnp.where(xl == 0, jnp.stack([keep, side]), jnp.stack([side, keep]))
    pair = jnp.concatenate([here, to_plane(here, 4)], axis=1)
    v2_all, most_v2 = join(
        [
            pair,
            to_plane(pair, 1),
            to_plane(pair, -1),
            to_plane(pair[0], -2),
            to_plane(pair[1], 2),
        ]
    )
    v1_all = lax.all_to_all(copies, PLANE, 0, 0, tiled=True).reshape(NXL, NI, WIDTH)

    own0 = partial_scores(0, v1_all, v2_all)
    other0 = swap(own0, "core")
    own1 = partial_scores(1, v1_all, v2_all)
    other1 = swap(own1, "core")
    most = jnp.concatenate([most_v2, largest(v1_all)[None]])
    most_other = swap(most, "core")

    scores0, first, cols = first_stats(own0, other0)
    scores1, pack = second_stats(place, own1, other1, first, cols, partner, most, most_other)
    seen = lax.all_to_all(
        pack, EVERY, 0, 0, axis_index_groups=stat_groups(), tiled=True
    )
    known = merge_stats(place, seen)
    coupling, give_one, give_two, take_one, take_two = coupling_of(
        place, scores0, scores1, known, swap(known, "core")
    )

    part_two = [
        (
            lax.dot_general(
                coupling, v1_all[x], (((0,), (0,)), ((), ())), preferred_element_type=jnp.float32
            )
            * give_two
        ).astype(jnp.float16)
        for x in range(NXL)
    ]
    coupling, part_two = lax.optimization_barrier((coupling, part_two))

    def group(g):
        return jnp.stack([part[g * GROUP : (g + 1) * GROUP] for part in part_two])

    before, after = to_plane(group(1), -1), to_plane(group(2), 1)
    two0 = to_plane(part_two[0][3 * GROUP :], 2)
    two1 = to_plane(part_two[1][3 * GROUP :], -2)
    part_one = (
        lax.dot_general(
            jnp.broadcast_to(coupling[None], (NXL, NI, NJ)),
            v2_all,
            (((2,), (1,)), ((0,), (0,))),
            preferred_element_type=jnp.float32,
        )
        * give_one
    ).astype(jnp.float16)
    one_parts = lax.all_to_all(part_one.reshape(16, ROWS, WIDTH), PLANE, 0, 0, tiled=True)
    two = jnp.stack([jnp.concatenate([two0[HALF:], two0[:HALF]]), two1])
    joined = sum(part.astype(jnp.float32) for part in (group(0), before, after, two))
    far = to_plane((joined[:, HALF:] * 0.25).astype(jnp.float16), 4)
    total = (joined[:, :HALF] + 4.0 * far.astype(jnp.float32)) * take_two
    stay = jnp.where(xl == 0, total[0], total[1])
    come = swap(jnp.where(xl == 0, total[1], total[0]), "xl")
    grad_one = jnp.sum(one_parts.astype(jnp.float32) * take_one, axis=0)
    come, grad_one = lax.optimization_barrier((come, grad_one))
    grad_two = jnp.where(
        xl == 0, jnp.concatenate([stay, come]), jnp.concatenate([come, stay])
    )
    return (grad_one, grad_two)


def solution(mesh):
    fine = Mesh(mesh.devices.reshape(NZ, NY, NXH, NXL, NC), EVERY)
    users = P(("z", "y", "xh"))
    both = P(("z", "y", "xh"), ("xl", "core"))
    return jax.shard_map(
        on_device,
        mesh=fine,
        in_specs=(both, both, users),
        out_specs=(both, both),
        check_vma=False,
    )
```

```python
import functools
import math

import jax
import jax.numpy as jnp
from jax import lax
from jax.experimental import pallas as pl
from jax.experimental.pallas import tpu as pltpu
from jax.sharding import Mesh
from jax.sharding import PartitionSpec as P

D = 2048
NZ, NY, NXH, NXL, NC = 8, 4, 2, 2, 2
PLANE = ("xl", "xh", "y")
OFFSETS = (0, 4, 2, -2, 1, 3, -1, -3)
GROUP = 128
EVERY = ("z", "y", "xh", "xl", "core")
ROWS = 128
HALF = 64
WIDTH = 512
NI = NY * NXH * ROWS
NJ = NZ * HALF
NP = NI // 2
LANES = 128
SCALE = 2.0 / math.sqrt(D)
VMEM = pl.BlockSpec(memory_space=pltpu.VMEM)
SMEM = pl.BlockSpec(memory_space=pltpu.SMEM)


def limit(mib):
    return pltpu.CompilerParams(vmem_limit_bytes=mib * 1024 * 1024)


def block_of(core, x, u):
    return jnp.where(core == 0, x * 8 + u, u % 4 * 4 + x * 2 + u // 4)


def arrange_kernel(place_ref, v1_ref, o_ref, sems):
    copies = [
        pltpu.make_async_copy(
            v1_ref.at[block_of(place_ref[0], x, u)], o_ref.at[x, u], sems.at[x * 8 + u]
        )
        for x in range(NXL)
        for u in range(8)
    ]
    for copy in copies:
        copy.start()
    for copy in copies:
        copy.wait()


def arranged(place, v1_all):
    return pl.pallas_call(
        arrange_kernel,
        out_shape=jax.ShapeDtypeStruct((NXL, 8, ROWS, WIDTH), v1_all.dtype),
        in_specs=[SMEM, pl.BlockSpec(memory_space=pl.ANY)],
        out_specs=pl.BlockSpec(memory_space=pl.ANY),
        scratch_shapes=[pltpu.SemaphoreType.DMA((16,))],
        compiler_params=limit(1),
        cost_estimate=pl.CostEstimate(flops=0, bytes_accessed=2**22, transcendentals=0),
    )(place, v1_all)


def join_kernel(own, four0, four1, up2, down2, up, down, v2_ref, most_ref):
    v2_ref[:, :HALF, :] = own[...]
    v2_ref[0, HALF : 2 * HALF, :] = four0[...]
    v2_ref[1, HALF : 2 * HALF, :] = four1[...]
    v2_ref[:, 2 * HALF : 3 * HALF, :] = up2[...]
    v2_ref[:, 3 * HALF : 4 * HALF, :] = down2[...]
    v2_ref[:, 4 * HALF : 6 * HALF, :] = up[...]
    v2_ref[:, 6 * HALF :, :] = down[...]
    size = jnp.maximum(jnp.abs(v2_ref[0]), jnp.abs(v2_ref[1])).astype(jnp.float32)
    most_ref[...] = jnp.max(size, axis=0, keepdims=True)


def join(*parts):
    return pl.pallas_call(
        join_kernel,
        out_shape=(
            jax.ShapeDtypeStruct((NXL, NJ, WIDTH), jnp.bfloat16),
            jax.ShapeDtypeStruct((1, WIDTH), jnp.float32),
        ),
        in_specs=[VMEM] * 7,
        out_specs=(VMEM, VMEM),
        compiler_params=limit(4),
        cost_estimate=pl.CostEstimate(flops=2**20, bytes_accessed=2**21, transcendentals=0),
    )(*parts)


def score_kernel(part, place_ref, v1_ref, v2_hbm, s_ref, v2_ref, sems):
    copies = [pltpu.make_async_copy(v2_hbm.at[x], v2_ref.at[x], sems.at[x]) for x in range(NXL)]
    for copy in copies:
        copy.start()
    for copy in copies:
        copy.wait()
    contract = (((1,), (1,)), ((), ()))
    for u in range(NP // ROWS):
        rows = slice(u * ROWS, (u + 1) * ROWS)
        user = part * (NP // ROWS) + u
        s_ref[rows, :] = sum(
            lax.dot_general(
                v1_ref[block_of(place_ref[0], x, user)],
                v2_ref[x],
                contract,
                preferred_element_type=jnp.float32,
            )
            for x in range(NXL)
        )


def partial_scores(part, place, v1_all, v2_all):
    return pl.pallas_call(
        functools.partial(score_kernel, part),
        out_shape=jax.ShapeDtypeStruct((NP, NJ), jnp.float32),
        in_specs=[SMEM, VMEM, pl.BlockSpec(memory_space=pl.ANY)],
        out_specs=VMEM,
        scratch_shapes=[
            pltpu.VMEM((NXL, NJ, WIDTH), jnp.bfloat16),
            pltpu.SemaphoreType.DMA((NXL,)),
        ],
        compiler_params=limit(6),
        cost_estimate=pl.CostEstimate(
            flops=2 * NP * NJ * NXL * WIDTH, bytes_accessed=3 * 2**20, transcendentals=0
        ),
    )(place, v1_all, v2_all)


def diagonal():
    shape = (LANES, LANES)
    return lax.broadcasted_iota(jnp.int32, shape, 0) == lax.broadcasted_iota(jnp.int32, shape, 1)


def placed(z, k):
    plane = lax.rem(z + OFFSETS[k] + NZ, NZ)
    half = plane // 4
    return plane % 4, half, half != k % 2


def turned(row, trade):
    return jnp.where(trade, pltpu.roll(row, HALF, 1), row)


def lane_half():
    return lax.broadcasted_iota(jnp.int32, (1, LANES), 1) // HALF


def block_stats(own_ref, other_ref, s_ref, row_ref, col_highest, col_total):
    eye = diagonal()
    for u in range(NP // LANES):
        rows = slice(u * LANES, (u + 1) * LANES)
        s = SCALE * (own_ref[rows, :] + other_ref[rows, :])
        s_ref[rows, :] = s
        highest = jnp.max(s, axis=1, keepdims=True)
        lse = highest + jnp.log(jnp.sum(jnp.exp(s - highest), axis=1, keepdims=True))
        row_ref[u : u + 1, :] = jnp.sum(jnp.where(eye, lse, 0.0), axis=0, keepdims=True)
        higher = jnp.maximum(col_highest, jnp.max(s, axis=0, keepdims=True))
        col_total = col_total * jnp.exp(col_highest - higher) + jnp.sum(
            jnp.exp(s - higher), axis=0, keepdims=True
        )
        col_highest = higher
    return col_highest, col_total


def first_kernel(own_ref, other_ref, s_ref, row_ref, col_ref):
    highest, total = block_stats(
        own_ref,
        other_ref,
        s_ref,
        row_ref,
        jnp.full((1, NJ), -jnp.inf, jnp.float32),
        jnp.zeros((1, NJ), jnp.float32),
    )
    col_ref[0:1, :] = highest
    col_ref[1:2, :] = total


def first_stats(own, other):
    return pl.pallas_call(
        first_kernel,
        out_shape=(
            jax.ShapeDtypeStruct((NP, NJ), jnp.float32),
            jax.ShapeDtypeStruct((NP // LANES, LANES), jnp.float32),
            jax.ShapeDtypeStruct((2, NJ), jnp.float32),
        ),
        in_specs=[VMEM] * 2,
        out_specs=(VMEM,) * 3,
        compiler_params=limit(4),
        cost_estimate=pl.CostEstimate(
            flops=10 * NP * NJ, bytes_accessed=3 * 2**20, transcendentals=2 * NP * NJ
        ),
    )(own, other)


def second_kernel(
    place_ref,
    own_ref,
    other_ref,
    first_ref,
    col_ref,
    partner_ref,
    most_ref,
    most_other_ref,
    s_ref,
    out_ref,
    pack_ref,
):
    half = NP // LANES
    pack_ref[...] = jnp.zeros_like(pack_ref)
    pack_ref[0, 0:half, :] = first_ref[...]
    col_highest, col_total = block_stats(
        own_ref,
        other_ref,
        s_ref,
        pack_ref.at[0, half : 2 * half, :],
        col_ref[0:1, :],
        col_ref[1:2, :],
    )
    col_lse = col_highest + jnp.log(col_total)
    for k in range(NZ):
        row, half, trade = placed(place_ref[2], k)
        g = k // 2
        here = turned(col_lse[:, g * LANES : (g + 1) * LANES], trade)
        there = pack_ref[1, pl.ds(row, 1), :]
        pack_ref[1, pl.ds(row, 1), :] = jnp.where(lane_half() == half, here, there)
    most = jnp.max(jnp.maximum(most_ref[...], most_other_ref[...]), axis=1, keepdims=True)
    most = jnp.broadcast_to(jnp.maximum(most, 1e-30), (2, LANES))
    pack_ref[0, 8:9, :] = partner_ref[...].astype(jnp.float32)
    pack_ref[0, 9:10, :] = most[0:1, :]
    pack_ref[1, 9:10, :] = most[1:2, :]
    chosen = jnp.where(place_ref[0] == 0, pack_ref[0], pack_ref[1])
    for p in range(16):
        out_ref[p] = chosen


def second_stats(place, own, other, first, cols, partner, most, most_other):
    return pl.pallas_call(
        second_kernel,
        out_shape=(
            jax.ShapeDtypeStruct((NP, NJ), jnp.float32),
            jax.ShapeDtypeStruct((16, 16, LANES), jnp.float32),
        ),
        in_specs=[SMEM] + [VMEM] * 7,
        out_specs=(VMEM, VMEM),
        scratch_shapes=[pltpu.VMEM((2, 16, LANES), jnp.float32)],
        compiler_params=limit(4),
        cost_estimate=pl.CostEstimate(
            flops=10 * NP * NJ, bytes_accessed=3 * 2**20, transcendentals=2 * NP * NJ
        ),
    )(place, own, other, first, cols, partner.reshape(1, ROWS), most, most_other)


def merged(lses):
    top = jnp.max(lses, axis=0)
    return top + jnp.log(jnp.sum(jnp.exp(lses - top[None]), axis=0))


def merge_kernel(place_ref, seen_ref, known_ref, cols_ref):
    core, xl = place_ref[0], place_ref[1]

    @pl.when(core == 0)
    def _():
        known_ref[0:8, :] = merged(seen_ref[:, 0:8, :])
        for u in range(8):
            known_ref[8 + u : 9 + u, :] = seen_ref[u, 8:9, :]

    @pl.when(core != 0)
    def _():
        known_ref[...] = jnp.zeros_like(known_ref)
        cols_ref[...] = merged(seen_ref[pl.ds(xl * NZ, NZ), 0:8, :])
        for g in range(4):
            row0, _, trade0 = placed(place_ref[2], 2 * g)
            row1, _, trade1 = placed(place_ref[2], 2 * g + 1)
            known_ref[g : g + 1, :] = jnp.where(
                lane_half() == 0,
                turned(cols_ref[pl.ds(row0, 1), :], trade0),
                turned(cols_ref[pl.ds(row1, 1), :], trade1),
            )

    known_ref[16:24, :] = jnp.broadcast_to(jnp.max(seen_ref[:, 9:10, :], axis=0), (8, LANES))


def merge_stats(place, seen):
    return pl.pallas_call(
        merge_kernel,
        out_shape=jax.ShapeDtypeStruct((24, LANES), jnp.float32),
        in_specs=[SMEM, VMEM],
        out_specs=VMEM,
        scratch_shapes=[pltpu.VMEM((8, LANES), jnp.float32)],
        compiler_params=limit(2),
        cost_estimate=pl.CostEstimate(flops=10**5, bytes_accessed=2**17, transcendentals=2**14),
    )(place, seen)


def couple_kernel(
    place_ref,
    s0_ref,
    s1_ref,
    known_ref,
    told_ref,
    c_ref,
    give_one_ref,
    give_two_ref,
    take_one_ref,
    take_two_ref,
):
    core, xl, z, uhigh = place_ref[0], place_ref[1], place_ref[2], place_ref[3]
    rows = jnp.where(core == 0, known_ref[...], told_ref[...])
    cols = jnp.where(core == 0, told_ref[...], known_ref[...])
    eye = diagonal()
    lane = lax.broadcasted_iota(jnp.int32, (1, LANES), 1)
    index, col_lse = [], []
    for g in range(4):
        first = lax.rem(z + OFFSETS[2 * g] + NZ, NZ)
        second = lax.rem(z + OFFSETS[2 * g + 1] + NZ, NZ)
        user = jnp.where(lane < HALF, first, second) * (NY * NXH) + uhigh
        inside = jnp.where(lane < HALF, lane, lane - HALF)
        index.append((user * ROWS + xl * HALF + inside).astype(jnp.float32))
        col_lse.append(cols[g : g + 1, :])
    index = jnp.concatenate(index, axis=1)
    col_lse = jnp.concatenate(col_lse, axis=1)
    for u in range(NI // LANES):
        here = slice(u * LANES, (u + 1) * LANES)
        half_ref = s0_ref if u < NP // LANES else s1_ref
        start = u * LANES % NP
        s = half_ref[start : start + LANES, :]
        row_lse = jnp.sum(jnp.where(eye, rows[u : u + 1, :], 0.0), axis=1, keepdims=True)
        partner = jnp.sum(jnp.where(eye, rows[8 + u : 9 + u, :], 0.0), axis=1, keepdims=True)
        both = jnp.exp(s - row_lse) + jnp.exp(s - col_lse)
        positive = (partner == index).astype(jnp.float32)
        c_ref[here, :] = (0.5 * both - positive).astype(jnp.bfloat16)
    most_two = jnp.concatenate([rows[16:17, :]] * 4, axis=1)
    most_one = jnp.concatenate([cols[16:17, :]] * 4, axis=1)
    give_one_ref[...] = 128.0 / most_two
    take_one_ref[...] = most_two / 128.0
    give_two_ref[...] = 64.0 / most_one
    take_two_ref[...] = most_one / 64.0


def coupling_of(place, scores0, scores1, known, told):
    return pl.pallas_call(
        couple_kernel,
        out_shape=(
            jax.ShapeDtypeStruct((NI, NJ), jnp.bfloat16),
        )
        + (jax.ShapeDtypeStruct((1, WIDTH), jnp.float32),) * 4,
        in_specs=[SMEM] + [VMEM] * 4,
        out_specs=(VMEM,) * 5,
        compiler_params=limit(5),
        cost_estimate=pl.CostEstimate(
            flops=8 * NI * NJ, bytes_accessed=3 * 2**20, transcendentals=2 * NI * NJ
        ),
    )(place, scores0, scores1, known, told)


def swap(x, axis):
    return lax.ppermute(x, axis, [(0, 1), (1, 0)])


def number(z, y, xh, xl, c):
    return (((z * NY + y) * NXH + xh) * NXL + xl) * NC + c


def line_groups(turn):
    alongs_y = [
        [number(z, y, xh, xl, turn) for y in range(NY)]
        for z in range(NZ)
        for xl in range(NXL)
        for xh in range(NXH)
    ]
    alongs_x = [
        [number(z, y, xh, xl, 1 - turn) for xl in range(NXL) for xh in range(NXH)]
        for z in range(NZ)
        for y in range(NY)
    ]
    return alongs_y + alongs_x


def spread(x, turn):
    return lax.all_to_all(
        jnp.broadcast_to(x[None], (4,) + x.shape),
        EVERY,
        0,
        0,
        axis_index_groups=line_groups(turn),
        tiled=True,
    )


def stat_groups():
    planes = [
        [number(z, y, xh, xl, 0) for xl in range(NXL) for xh in range(NXH) for y in range(NY)]
        for z in range(NZ)
    ]
    columns = [
        [number(z, y, xh, xl, 1) for xl in range(NXL) for z in range(NZ)]
        for y in range(NY)
        for xh in range(NXH)
    ]
    return planes + columns


def to_plane(x, dz):
    return lax.ppermute(x, "z", [(z, (z + dz) % NZ) for z in range(NZ)])


def largest(x):
    return jnp.max(jnp.abs(x), axis=(0, 1)).astype(jnp.float32)


def on_device(view_one, view_two, partner):
    z = lax.axis_index("z")
    uhigh = lax.axis_index("y") * NXH + lax.axis_index("xh")
    xl = lax.axis_index("xl")
    core = lax.axis_index("core")
    place = jnp.stack([core, xl, z, uhigh]).astype(jnp.int32)

    keep = jnp.where(xl == 0, view_two[:HALF], view_two[HALF:])
    give = jnp.where(xl == 0, view_two[HALF:], view_two[:HALF])
    side = swap(give, "xl")
    lines = spread(view_one, 0)
    here = jnp.where(xl == 0, jnp.stack([keep, side]), jnp.stack([side, keep]))
    up2, down2 = to_plane(here, -2), to_plane(here, 2)
    v1_all = spread(lines, 1).reshape(16, ROWS, WIDTH)
    up = to_plane(jnp.concatenate([here, up2], axis=1), -1)
    down = to_plane(jnp.concatenate([here, down2], axis=1), 1)
    v2_all, most_v2 = join(
        here, to_plane(up2[0], -2), to_plane(down2[1], 2), up2, down2, up, down
    )

    own0 = partial_scores(0, place, v1_all, v2_all)
    other0 = swap(own0, "core")
    own1 = partial_scores(1, place, v1_all, v2_all)
    other1 = swap(own1, "core")
    most = jnp.concatenate([most_v2, largest(v1_all)[None]])
    most_other = swap(most, "core")

    scores0, first, cols = first_stats(own0, other0)
    scores1, pack = second_stats(place, own1, other1, first, cols, partner, most, most_other)
    seen = lax.all_to_all(
        pack, EVERY, 0, 0, axis_index_groups=stat_groups(), tiled=True
    )
    v1_rows = arranged(place, v1_all).reshape(NXL, NI, WIDTH)
    known = merge_stats(place, seen)
    coupling, give_one, give_two, take_one, take_two = coupling_of(
        place, scores0, scores1, known, swap(known, "core")
    )

    part_one = (
        lax.dot_general(
            jnp.broadcast_to(coupling[None], (NXL, NI, NJ)),
            v2_all,
            (((2,), (1,)), ((0,), (0,))),
            preferred_element_type=jnp.float32,
        )
        * give_one
    ).astype(jnp.float16)
    coupling, part_one = lax.optimization_barrier((coupling, part_one))
    one_parts = lax.all_to_all(part_one.reshape(16, ROWS, WIDTH), PLANE, 0, 0, tiled=True)
    part_two = [
        (
            lax.dot_general(
                coupling, v1_rows[x], (((0,), (0,)), ((), ())), preferred_element_type=jnp.float32
            )
            * give_two
        ).astype(jnp.float16)
        for x in range(NXL)
    ]

    def blocks(start, stop):
        return jnp.stack([part[start * HALF : stop * HALF] for part in part_two])

    from_below, from_above = to_plane(blocks(4, 6), 1), to_plane(blocks(6, 8), -1)
    four0 = to_plane(part_two[0][HALF : 2 * HALF], 2)
    four1 = to_plane(part_two[1][HALF : 2 * HALF], -2)
    wide = [x.astype(jnp.float32) for x in (from_below, from_above, four0, four1)]
    up2 = blocks(2, 3).astype(jnp.float32) + wide[0][:, HALF:]
    up2 = jnp.stack([up2[0] + wide[2], up2[1]])
    down2 = blocks(3, 4).astype(jnp.float32) + wide[1][:, HALF:]
    down2 = jnp.stack([down2[0], down2[1] + wide[3]])
    from_up = to_plane((up2 * 0.25).astype(jnp.float16), 2)
    from_down = to_plane((down2 * 0.25).astype(jnp.float16), -2)
    total = blocks(0, 1).astype(jnp.float32) + wide[0][:, :HALF] + wide[1][:, :HALF]
    total = total + 4.0 * (from_up.astype(jnp.float32) + from_down.astype(jnp.float32))
    total = total * take_two
    stay = jnp.where(xl == 0, total[0], total[1])
    come = swap(jnp.where(xl == 0, total[1], total[0]), "xl")
    grad_one = jnp.sum(one_parts.astype(jnp.float32) * take_one, axis=0)
    come, grad_one = lax.optimization_barrier((come, grad_one))
    grad_two = jnp.where(
        xl == 0, jnp.concatenate([stay, come]), jnp.concatenate([come, stay])
    )
    return (grad_one, grad_two)


def solution(mesh):
    fine = Mesh(mesh.devices.reshape(NZ, NY, NXH, NXL, NC), EVERY)
    users = P(("z", "y", "xh"))
    both = P(("z", "y", "xh"), ("xl", "core"))
    return jax.shard_map(
        on_device,
        mesh=fine,
        in_specs=(both, both, users),
        out_specs=(both, both),
        check_vma=False,
    )
```

```python
import functools
import math

import jax
import jax.numpy as jnp
from jax import lax
from jax.experimental import pallas as pl
from jax.experimental.pallas import tpu as pltpu
from jax.sharding import Mesh
from jax.sharding import PartitionSpec as P

D = 2048
NZ, NY, NXH, NXL, NC = 8, 4, 2, 2, 2
PLANE = ("xl", "xh", "y")
OFFSETS = (0, 4, 2, -2, 1, 3, -1, -3)
GROUP = 128
EVERY = ("z", "y", "xh", "xl", "core")
ROWS = 128
HALF = 64
WIDTH = 512
NI = NY * NXH * ROWS
NJ = NZ * HALF
NP = NI // 2
LANES = 128
SCALE = 2.0 / math.sqrt(D)
VMEM = pl.BlockSpec(memory_space=pltpu.VMEM)
SMEM = pl.BlockSpec(memory_space=pltpu.SMEM)


def limit(mib):
    return pltpu.CompilerParams(vmem_limit_bytes=mib * 1024 * 1024)


def block_of(core, x, u):
    return jnp.where(core == 0, x * 8 + u, u % 4 * 4 + x * 2 + u // 4)


def arrange_kernel(place_ref, v1_ref, *o_refs):
    for x in range(NXL):
        for u in range(8):
            o_refs[x][u * ROWS : (u + 1) * ROWS, :] = v1_ref[block_of(place_ref[0], x, u)]


def arranged(place, v1_all):
    return pl.pallas_call(
        arrange_kernel,
        out_shape=(jax.ShapeDtypeStruct((NI, WIDTH), v1_all.dtype),) * NXL,
        in_specs=[SMEM, VMEM],
        out_specs=(VMEM,) * NXL,
        compiler_params=limit(5),
        cost_estimate=pl.CostEstimate(flops=0, bytes_accessed=2**22, transcendentals=0),
    )(place, v1_all)


def join_kernel(own, four0, four1, up2, down2, up, down, v2_ref, most_ref):
    v2_ref[:, :HALF, :] = own[...]
    v2_ref[0, HALF : 2 * HALF, :] = four0[...]
    v2_ref[1, HALF : 2 * HALF, :] = four1[...]
    v2_ref[:, 2 * HALF : 3 * HALF, :] = up2[...]
    v2_ref[:, 3 * HALF : 4 * HALF, :] = down2[...]
    v2_ref[:, 4 * HALF : 6 * HALF, :] = up[...]
    v2_ref[:, 6 * HALF :, :] = down[...]
    size = jnp.maximum(jnp.abs(v2_ref[0]), jnp.abs(v2_ref[1])).astype(jnp.float32)
    most_ref[...] = jnp.max(size, axis=0, keepdims=True)


def join(*parts):
    return pl.pallas_call(
        join_kernel,
        out_shape=(
            jax.ShapeDtypeStruct((NXL, NJ, WIDTH), jnp.bfloat16),
            jax.ShapeDtypeStruct((1, WIDTH), jnp.float32),
        ),
        in_specs=[VMEM] * 7,
        out_specs=(VMEM, VMEM),
        compiler_params=limit(4),
        cost_estimate=pl.CostEstimate(flops=2**20, bytes_accessed=2**21, transcendentals=0),
    )(*parts)


def score_kernel(part, place_ref, v1_ref, v2_ref, s_ref):
    users = range(part * (NP // ROWS), (part + 1) * (NP // ROWS))
    contract = (((1,), (1,)), ((), ()))
    s_ref[...] = sum(
        lax.dot_general(
            jnp.concatenate([v1_ref[block_of(place_ref[0], x, u)] for u in users]),
            v2_ref[x],
            contract,
            preferred_element_type=jnp.float32,
        )
        for x in range(NXL)
    )


def partial_scores(part, place, v1_all, v2_all):
    return pl.pallas_call(
        functools.partial(score_kernel, part),
        out_shape=jax.ShapeDtypeStruct((NP, NJ), jnp.float32),
        in_specs=[SMEM, VMEM, VMEM],
        out_specs=VMEM,
        compiler_params=limit(6),
        cost_estimate=pl.CostEstimate(
            flops=2 * NP * NJ * NXL * WIDTH, bytes_accessed=3 * 2**20, transcendentals=0
        ),
    )(place, v1_all, v2_all)


def diagonal():
    shape = (LANES, LANES)
    return lax.broadcasted_iota(jnp.int32, shape, 0) == lax.broadcasted_iota(jnp.int32, shape, 1)


def placed(z, k):
    plane = lax.rem(z + OFFSETS[k] + NZ, NZ)
    half = plane // 4
    return plane % 4, half, half != k % 2


def turned(row, trade):
    return jnp.where(trade, pltpu.roll(row, HALF, 1), row)


def lane_half():
    return lax.broadcasted_iota(jnp.int32, (1, LANES), 1) // HALF


def block_stats(own_ref, other_ref, s_ref, row_ref, col_highest, col_total):
    eye = diagonal()
    for u in range(NP // LANES):
        rows = slice(u * LANES, (u + 1) * LANES)
        s = SCALE * (own_ref[rows, :] + other_ref[rows, :])
        s_ref[rows, :] = s
        highest = jnp.max(s, axis=1, keepdims=True)
        lse = highest + jnp.log(jnp.sum(jnp.exp(s - highest), axis=1, keepdims=True))
        row_ref[u : u + 1, :] = jnp.sum(jnp.where(eye, lse, 0.0), axis=0, keepdims=True)
        higher = jnp.maximum(col_highest, jnp.max(s, axis=0, keepdims=True))
        col_total = col_total * jnp.exp(col_highest - higher) + jnp.sum(
            jnp.exp(s - higher), axis=0, keepdims=True
        )
        col_highest = higher
    return col_highest, col_total


def first_kernel(own_ref, other_ref, s_ref, row_ref, col_ref):
    highest, total = block_stats(
        own_ref,
        other_ref,
        s_ref,
        row_ref,
        jnp.full((1, NJ), -jnp.inf, jnp.float32),
        jnp.zeros((1, NJ), jnp.float32),
    )
    col_ref[0:1, :] = highest
    col_ref[1:2, :] = total


def first_stats(own, other):
    return pl.pallas_call(
        first_kernel,
        out_shape=(
            jax.ShapeDtypeStruct((NP, NJ), jnp.float32),
            jax.ShapeDtypeStruct((NP // LANES, LANES), jnp.float32),
            jax.ShapeDtypeStruct((2, NJ), jnp.float32),
        ),
        in_specs=[VMEM] * 2,
        out_specs=(VMEM,) * 3,
        compiler_params=limit(4),
        cost_estimate=pl.CostEstimate(
            flops=10 * NP * NJ, bytes_accessed=3 * 2**20, transcendentals=2 * NP * NJ
        ),
    )(own, other)


def second_kernel(
    place_ref,
    own_ref,
    other_ref,
    first_ref,
    col_ref,
    partner_ref,
    most_ref,
    most_other_ref,
    s_ref,
    out_ref,
    pack_ref,
):
    half = NP // LANES
    pack_ref[...] = jnp.zeros_like(pack_ref)
    pack_ref[0, 0:half, :] = first_ref[...]
    col_highest, col_total = block_stats(
        own_ref,
        other_ref,
        s_ref,
        pack_ref.at[0, half : 2 * half, :],
        col_ref[0:1, :],
        col_ref[1:2, :],
    )
    col_lse = col_highest + jnp.log(col_total)
    for k in range(NZ):
        row, half, trade = placed(place_ref[2], k)
        g = k // 2
        here = turned(col_lse[:, g * LANES : (g + 1) * LANES], trade)
        there = pack_ref[1, pl.ds(row, 1), :]
        pack_ref[1, pl.ds(row, 1), :] = jnp.where(lane_half() == half, here, there)
    most = jnp.max(jnp.maximum(most_ref[...], most_other_ref[...]), axis=1, keepdims=True)
    most = jnp.broadcast_to(jnp.maximum(most, 1e-30), (2, LANES))
    pack_ref[0, 8:9, :] = partner_ref[...].astype(jnp.float32)
    pack_ref[0, 9:10, :] = most[0:1, :]
    pack_ref[1, 9:10, :] = most[1:2, :]
    chosen = jnp.where(place_ref[0] == 0, pack_ref[0], pack_ref[1])
    for p in range(16):
        out_ref[p] = chosen


def second_stats(place, own, other, first, cols, partner, most, most_other):
    return pl.pallas_call(
        second_kernel,
        out_shape=(
            jax.ShapeDtypeStruct((NP, NJ), jnp.float32),
            jax.ShapeDtypeStruct((16, 16, LANES), jnp.float32),
        ),
        in_specs=[SMEM] + [VMEM] * 7,
        out_specs=(VMEM, VMEM),
        scratch_shapes=[pltpu.VMEM((2, 16, LANES), jnp.float32)],
        compiler_params=limit(4),
        cost_estimate=pl.CostEstimate(
            flops=10 * NP * NJ, bytes_accessed=3 * 2**20, transcendentals=2 * NP * NJ
        ),
    )(place, own, other, first, cols, partner.reshape(1, ROWS), most, most_other)


def merged(lses):
    top = jnp.max(lses, axis=0)
    return top + jnp.log(jnp.sum(jnp.exp(lses - top[None]), axis=0))


def merge_kernel(place_ref, seen_ref, known_ref, cols_ref):
    core, xl = place_ref[0], place_ref[1]

    @pl.when(core == 0)
    def _():
        known_ref[0:8, :] = merged(seen_ref[:, 0:8, :])
        for u in range(8):
            known_ref[8 + u : 9 + u, :] = seen_ref[u, 8:9, :]

    @pl.when(core != 0)
    def _():
        known_ref[...] = jnp.zeros_like(known_ref)
        cols_ref[...] = merged(seen_ref[pl.ds(xl * NZ, NZ), 0:8, :])
        for g in range(4):
            row0, _, trade0 = placed(place_ref[2], 2 * g)
            row1, _, trade1 = placed(place_ref[2], 2 * g + 1)
            known_ref[g : g + 1, :] = jnp.where(
                lane_half() == 0,
                turned(cols_ref[pl.ds(row0, 1), :], trade0),
                turned(cols_ref[pl.ds(row1, 1), :], trade1),
            )

    known_ref[16:24, :] = jnp.broadcast_to(jnp.max(seen_ref[:, 9:10, :], axis=0), (8, LANES))


def merge_stats(place, seen):
    return pl.pallas_call(
        merge_kernel,
        out_shape=jax.ShapeDtypeStruct((24, LANES), jnp.float32),
        in_specs=[SMEM, VMEM],
        out_specs=VMEM,
        scratch_shapes=[pltpu.VMEM((8, LANES), jnp.float32)],
        compiler_params=limit(2),
        cost_estimate=pl.CostEstimate(flops=10**5, bytes_accessed=2**17, transcendentals=2**14),
    )(place, seen)


def couple_kernel(
    place_ref,
    s0_ref,
    s1_ref,
    known_ref,
    told_ref,
    c_ref,
    give_one_ref,
    give_two_ref,
    take_one_ref,
    take_two_ref,
):
    core, xl, z, uhigh = place_ref[0], place_ref[1], place_ref[2], place_ref[3]
    rows = jnp.where(core == 0, known_ref[...], told_ref[...])
    cols = jnp.where(core == 0, told_ref[...], known_ref[...])
    eye = diagonal()
    lane = lax.broadcasted_iota(jnp.int32, (1, LANES), 1)
    index, col_lse = [], []
    for g in range(4):
        first = lax.rem(z + OFFSETS[2 * g] + NZ, NZ)
        second = lax.rem(z + OFFSETS[2 * g + 1] + NZ, NZ)
        user = jnp.where(lane < HALF, first, second) * (NY * NXH) + uhigh
        inside = jnp.where(lane < HALF, lane, lane - HALF)
        index.append((user * ROWS + xl * HALF + inside).astype(jnp.float32))
        col_lse.append(cols[g : g + 1, :])
    index = jnp.concatenate(index, axis=1)
    col_lse = jnp.concatenate(col_lse, axis=1)
    for u in range(NI // LANES):
        here = slice(u * LANES, (u + 1) * LANES)
        half_ref = s0_ref if u < NP // LANES else s1_ref
        start = u * LANES % NP
        s = half_ref[start : start + LANES, :]
        row_lse = jnp.sum(jnp.where(eye, rows[u : u + 1, :], 0.0), axis=1, keepdims=True)
        partner = jnp.sum(jnp.where(eye, rows[8 + u : 9 + u, :], 0.0), axis=1, keepdims=True)
        both = jnp.exp(s - row_lse) + jnp.exp(s - col_lse)
        positive = (partner == index).astype(jnp.float32)
        c_ref[here, :] = (0.5 * both - positive).astype(jnp.bfloat16)
    most_two = jnp.concatenate([rows[16:17, :]] * 4, axis=1)
    most_one = jnp.concatenate([cols[16:17, :]] * 4, axis=1)
    give_one_ref[...] = 128.0 / most_two
    take_one_ref[...] = most_two / 128.0
    give_two_ref[...] = 64.0 / most_one
    take_two_ref[...] = most_one / 64.0


def coupling_of(place, scores0, scores1, known, told):
    return pl.pallas_call(
        couple_kernel,
        out_shape=(
            jax.ShapeDtypeStruct((NI, NJ), jnp.bfloat16),
        )
        + (jax.ShapeDtypeStruct((1, WIDTH), jnp.float32),) * 4,
        in_specs=[SMEM] + [VMEM] * 4,
        out_specs=(VMEM,) * 5,
        compiler_params=limit(5),
        cost_estimate=pl.CostEstimate(
            flops=8 * NI * NJ, bytes_accessed=3 * 2**20, transcendentals=2 * NI * NJ
        ),
    )(place, scores0, scores1, known, told)


def swap(x, axis):
    return lax.ppermute(x, axis, [(0, 1), (1, 0)])


def number(z, y, xh, xl, c):
    return (((z * NY + y) * NXH + xh) * NXL + xl) * NC + c


def line_groups(turn):
    alongs_y = [
        [number(z, y, xh, xl, turn) for y in range(NY)]
        for z in range(NZ)
        for xl in range(NXL)
        for xh in range(NXH)
    ]
    alongs_x = [
        [number(z, y, xh, xl, 1 - turn) for xl in range(NXL) for xh in range(NXH)]
        for z in range(NZ)
        for y in range(NY)
    ]
    return alongs_y + alongs_x


def spread(x, turn):
    return lax.all_to_all(
        jnp.broadcast_to(x[None], (4,) + x.shape),
        EVERY,
        0,
        0,
        axis_index_groups=line_groups(turn),
        tiled=True,
    )


def stat_groups():
    planes = [
        [number(z, y, xh, xl, 0) for xl in range(NXL) for xh in range(NXH) for y in range(NY)]
        for z in range(NZ)
    ]
    columns = [
        [number(z, y, xh, xl, 1) for xl in range(NXL) for z in range(NZ)]
        for y in range(NY)
        for xh in range(NXH)
    ]
    return planes + columns


def to_plane(x, dz):
    return lax.ppermute(x, "z", [(z, (z + dz) % NZ) for z in range(NZ)])


def largest(x):
    return jnp.max(jnp.abs(x), axis=(0, 1)).astype(jnp.float32)


def on_device(view_one, view_two, partner):
    z = lax.axis_index("z")
    uhigh = lax.axis_index("y") * NXH + lax.axis_index("xh")
    xl = lax.axis_index("xl")
    core = lax.axis_index("core")
    place = jnp.stack([core, xl, z, uhigh]).astype(jnp.int32)

    keep = jnp.where(xl == 0, view_two[:HALF], view_two[HALF:])
    give = jnp.where(xl == 0, view_two[HALF:], view_two[:HALF])
    side = swap(give, "xl")
    lines = spread(view_one, 0)
    lines, side = lax.optimization_barrier((lines, side))
    here = jnp.where(xl == 0, jnp.stack([keep, side]), jnp.stack([side, keep]))
    up2, down2 = to_plane(here, -2), to_plane(here, 2)
    v1_all = spread(lines, 1).reshape(16, ROWS, WIDTH)
    up = to_plane(jnp.concatenate([here, up2], axis=1), -1)
    down = to_plane(jnp.concatenate([here, down2], axis=1), 1)
    v2_all, most_v2 = join(
        here, to_plane(up2[0], -2), to_plane(down2[1], 2), up2, down2, up, down
    )

    own0 = partial_scores(0, place, v1_all, v2_all)
    other0 = swap(own0, "core")
    own1 = partial_scores(1, place, v1_all, v2_all)
    other1 = swap(own1, "core")
    most = jnp.concatenate([most_v2, largest(v1_all)[None]])
    most_other = swap(most, "core")

    scores0, first, cols = first_stats(own0, other0)
    scores1, pack = second_stats(place, own1, other1, first, cols, partner, most, most_other)
    seen = lax.all_to_all(
        pack, EVERY, 0, 0, axis_index_groups=stat_groups(), tiled=True
    )
    v1_rows = arranged(place, v1_all)
    known = merge_stats(place, seen)
    coupling, give_one, give_two, take_one, take_two = coupling_of(
        place, scores0, scores1, known, swap(known, "core")
    )

    part_one = (
        lax.dot_general(
            jnp.broadcast_to(coupling[None], (NXL, NI, NJ)),
            v2_all,
            (((2,), (1,)), ((0,), (0,))),
            preferred_element_type=jnp.float32,
        )
        * give_one
    ).astype(jnp.float16)
    coupling, part_one = lax.optimization_barrier((coupling, part_one))
    one_parts = lax.all_to_all(part_one.reshape(16, ROWS, WIDTH), PLANE, 0, 0, tiled=True)
    part_two = [
        (
            lax.dot_general(
                coupling, v1_rows[x], (((0,), (0,)), ((), ())), preferred_element_type=jnp.float32
            )
            * give_two
        ).astype(jnp.float16)
        for x in range(NXL)
    ]

    def blocks(start, stop):
        return jnp.stack([part[start * HALF : stop * HALF] for part in part_two])

    from_below, from_above = to_plane(blocks(4, 6), 1), to_plane(blocks(6, 8), -1)
    four0 = to_plane(part_two[0][HALF : 2 * HALF], 2)
    four1 = to_plane(part_two[1][HALF : 2 * HALF], -2)
    wide = [x.astype(jnp.float32) for x in (from_below, from_above, four0, four1)]
    up2 = blocks(2, 3).astype(jnp.float32) + wide[0][:, HALF:]
    up2 = jnp.stack([up2[0] + wide[2], up2[1]])
    down2 = blocks(3, 4).astype(jnp.float32) + wide[1][:, HALF:]
    down2 = jnp.stack([down2[0], down2[1] + wide[3]])
    from_up = to_plane((up2 * 0.25).astype(jnp.float16), 2)
    from_down = to_plane((down2 * 0.25).astype(jnp.float16), -2)
    total = blocks(0, 1).astype(jnp.float32) + wide[0][:, :HALF] + wide[1][:, :HALF]
    total = total + 4.0 * (from_up.astype(jnp.float32) + from_down.astype(jnp.float32))
    total = total * take_two
    stay = jnp.where(xl == 0, total[0], total[1])
    come = swap(jnp.where(xl == 0, total[1], total[0]), "xl")
    grad_one = jnp.sum(one_parts.astype(jnp.float32) * take_one, axis=0)
    come, grad_one = lax.optimization_barrier((come, grad_one))
    grad_two = jnp.where(
        xl == 0, jnp.concatenate([stay, come]), jnp.concatenate([come, stay])
    )
    return (grad_one, grad_two)


def solution(mesh):
    fine = Mesh(mesh.devices.reshape(NZ, NY, NXH, NXL, NC), EVERY)
    users = P(("z", "y", "xh"))
    both = P(("z", "y", "xh"), ("xl", "core"))
    return jax.shard_map(
        on_device,
        mesh=fine,
        in_specs=(both, both, users),
        out_specs=(both, both),
        check_vma=False,
    )
```

```python
import functools
import math

import jax
import jax.numpy as jnp
from jax import lax
from jax.experimental import pallas as pl
from jax.experimental.pallas import tpu as pltpu
from jax.sharding import Mesh
from jax.sharding import PartitionSpec as P

D = 2048
NZ, NY, NXH, NXL, NC = 8, 4, 2, 2, 2
PLANE = ("xl", "xh", "y")
OFFSETS = (0, 4, 2, -2, 1, 3, -1, -3)
GROUP = 128
EVERY = ("z", "y", "xh", "xl", "core")
ROWS = 128
HALF = 64
WIDTH = 512
NI = NY * NXH * ROWS
NJ = NZ * HALF
NP = NI // 2
LANES = 128
SCALE = 2.0 / math.sqrt(D)
VMEM = pl.BlockSpec(memory_space=pltpu.VMEM)
SMEM = pl.BlockSpec(memory_space=pltpu.SMEM)


def limit(mib):
    return pltpu.CompilerParams(vmem_limit_bytes=mib * 1024 * 1024)


def block_of(core, x, u):
    return jnp.where(core == 0, x * 8 + u, u % 4 * 4 + x * 2 + u // 4)


def arrange_kernel(place_ref, v1_ref, *o_refs):
    for x in range(NXL):
        for u in range(8):
            o_refs[x][u * ROWS : (u + 1) * ROWS, :] = v1_ref[block_of(place_ref[0], x, u)]


def arranged(place, v1_all):
    return pl.pallas_call(
        arrange_kernel,
        out_shape=(jax.ShapeDtypeStruct((NI, WIDTH), v1_all.dtype),) * NXL,
        in_specs=[SMEM, VMEM],
        out_specs=(VMEM,) * NXL,
        compiler_params=limit(5),
        cost_estimate=pl.CostEstimate(flops=0, bytes_accessed=2**22, transcendentals=0),
    )(place, v1_all)


def join_kernel(own, four0, four1, up2, down2, up, down, v2_ref, most_ref):
    v2_ref[:, :HALF, :] = own[...]
    v2_ref[0, HALF : 2 * HALF, :] = four0[...]
    v2_ref[1, HALF : 2 * HALF, :] = four1[...]
    v2_ref[:, 2 * HALF : 3 * HALF, :] = up2[...]
    v2_ref[:, 3 * HALF : 4 * HALF, :] = down2[...]
    v2_ref[:, 4 * HALF : 6 * HALF, :] = up[...]
    v2_ref[:, 6 * HALF :, :] = down[...]
    size = jnp.maximum(jnp.abs(v2_ref[0]), jnp.abs(v2_ref[1])).astype(jnp.float32)
    most_ref[...] = jnp.max(size, axis=0, keepdims=True)


def join(*parts):
    return pl.pallas_call(
        join_kernel,
        out_shape=(
            jax.ShapeDtypeStruct((NXL, NJ, WIDTH), jnp.bfloat16),
            jax.ShapeDtypeStruct((1, WIDTH), jnp.float32),
        ),
        in_specs=[VMEM] * 7,
        out_specs=(VMEM, VMEM),
        compiler_params=limit(4),
        cost_estimate=pl.CostEstimate(flops=12 * 2**30, bytes_accessed=2**21, transcendentals=0),
    )(*parts)


def score_kernel(part, place_ref, v1_ref, v2_ref, s_ref):
    users = range(part * (NP // ROWS), (part + 1) * (NP // ROWS))
    contract = (((1,), (1,)), ((), ()))
    s_ref[...] = sum(
        lax.dot_general(
            jnp.concatenate([v1_ref[block_of(place_ref[0], x, u)] for u in users]),
            v2_ref[x],
            contract,
            preferred_element_type=jnp.float32,
        )
        for x in range(NXL)
    )


def partial_scores(part, place, v1_all, v2_all):
    return pl.pallas_call(
        functools.partial(score_kernel, part),
        out_shape=jax.ShapeDtypeStruct((NP, NJ), jnp.float32),
        in_specs=[SMEM, VMEM, VMEM],
        out_specs=VMEM,
        compiler_params=limit(6),
        cost_estimate=pl.CostEstimate(
            flops=2 * NP * NJ * NXL * WIDTH, bytes_accessed=3 * 2**20, transcendentals=0
        ),
    )(place, v1_all, v2_all)


def diagonal():
    shape = (LANES, LANES)
    return lax.broadcasted_iota(jnp.int32, shape, 0) == lax.broadcasted_iota(jnp.int32, shape, 1)


def placed(z, k):
    plane = lax.rem(z + OFFSETS[k] + NZ, NZ)
    half = plane // 4
    return plane % 4, half, half != k % 2


def turned(row, trade):
    return jnp.where(trade, pltpu.roll(row, HALF, 1), row)


def lane_half():
    return lax.broadcasted_iota(jnp.int32, (1, LANES), 1) // HALF


def block_stats(own_ref, other_ref, s_ref, row_ref, col_highest, col_total):
    eye = diagonal()
    for u in range(NP // LANES):
        rows = slice(u * LANES, (u + 1) * LANES)
        s = SCALE * (own_ref[rows, :] + other_ref[rows, :])
        s_ref[rows, :] = s
        highest = jnp.max(s, axis=1, keepdims=True)
        lse = highest + jnp.log(jnp.sum(jnp.exp(s - highest), axis=1, keepdims=True))
        row_ref[u : u + 1, :] = jnp.sum(jnp.where(eye, lse, 0.0), axis=0, keepdims=True)
        higher = jnp.maximum(col_highest, jnp.max(s, axis=0, keepdims=True))
        col_total = col_total * jnp.exp(col_highest - higher) + jnp.sum(
            jnp.exp(s - higher), axis=0, keepdims=True
        )
        col_highest = higher
    return col_highest, col_total


def first_kernel(own_ref, other_ref, s_ref, row_ref, col_ref):
    highest, total = block_stats(
        own_ref,
        other_ref,
        s_ref,
        row_ref,
        jnp.full((1, NJ), -jnp.inf, jnp.float32),
        jnp.zeros((1, NJ), jnp.float32),
    )
    col_ref[0:1, :] = highest
    col_ref[1:2, :] = total


def first_stats(own, other):
    return pl.pallas_call(
        first_kernel,
        out_shape=(
            jax.ShapeDtypeStruct((NP, NJ), jnp.float32),
            jax.ShapeDtypeStruct((NP // LANES, LANES), jnp.float32),
            jax.ShapeDtypeStruct((2, NJ), jnp.float32),
        ),
        in_specs=[VMEM] * 2,
        out_specs=(VMEM,) * 3,
        compiler_params=limit(4),
        cost_estimate=pl.CostEstimate(
            flops=10 * NP * NJ, bytes_accessed=3 * 2**20, transcendentals=2 * NP * NJ
        ),
    )(own, other)


def second_kernel(
    place_ref,
    own_ref,
    other_ref,
    first_ref,
    col_ref,
    partner_ref,
    most_ref,
    most_other_ref,
    s_ref,
    out_ref,
    pack_ref,
):
    half = NP // LANES
    pack_ref[...] = jnp.zeros_like(pack_ref)
    pack_ref[0, 0:half, :] = first_ref[...]
    col_highest, col_total = block_stats(
        own_ref,
        other_ref,
        s_ref,
        pack_ref.at[0, half : 2 * half, :],
        col_ref[0:1, :],
        col_ref[1:2, :],
    )
    col_lse = col_highest + jnp.log(col_total)
    for k in range(NZ):
        row, half, trade = placed(place_ref[2], k)
        g = k // 2
        here = turned(col_lse[:, g * LANES : (g + 1) * LANES], trade)
        there = pack_ref[1, pl.ds(row, 1), :]
        pack_ref[1, pl.ds(row, 1), :] = jnp.where(lane_half() == half, here, there)
    most = jnp.max(jnp.maximum(most_ref[...], most_other_ref[...]), axis=1, keepdims=True)
    most = jnp.broadcast_to(jnp.maximum(most, 1e-30), (2, LANES))
    pack_ref[0, 8:9, :] = partner_ref[...].astype(jnp.float32)
    pack_ref[0, 9:10, :] = most[0:1, :]
    pack_ref[1, 9:10, :] = most[1:2, :]
    chosen = jnp.where(place_ref[0] == 0, pack_ref[0], pack_ref[1])
    for p in range(16):
        out_ref[p] = chosen


def second_stats(place, own, other, first, cols, partner, most, most_other):
    return pl.pallas_call(
        second_kernel,
        out_shape=(
            jax.ShapeDtypeStruct((NP, NJ), jnp.float32),
            jax.ShapeDtypeStruct((16, 16, LANES), jnp.float32),
        ),
        in_specs=[SMEM] + [VMEM] * 7,
        out_specs=(VMEM, VMEM),
        scratch_shapes=[pltpu.VMEM((2, 16, LANES), jnp.float32)],
        compiler_params=limit(4),
        cost_estimate=pl.CostEstimate(
            flops=10 * NP * NJ, bytes_accessed=3 * 2**20, transcendentals=2 * NP * NJ
        ),
    )(place, own, other, first, cols, partner.reshape(1, ROWS), most, most_other)


def merged(lses):
    top = jnp.max(lses, axis=0)
    return top + jnp.log(jnp.sum(jnp.exp(lses - top[None]), axis=0))


def merge_kernel(place_ref, seen_ref, known_ref, cols_ref):
    core, xl = place_ref[0], place_ref[1]

    @pl.when(core == 0)
    def _():
        known_ref[0:8, :] = merged(seen_ref[:, 0:8, :])
        for u in range(8):
            known_ref[8 + u : 9 + u, :] = seen_ref[u, 8:9, :]

    @pl.when(core != 0)
    def _():
        known_ref[...] = jnp.zeros_like(known_ref)
        cols_ref[...] = merged(seen_ref[pl.ds(xl * NZ, NZ), 0:8, :])
        for g in range(4):
            row0, _, trade0 = placed(place_ref[2], 2 * g)
            row1, _, trade1 = placed(place_ref[2], 2 * g + 1)
            known_ref[g : g + 1, :] = jnp.where(
                lane_half() == 0,
                turned(cols_ref[pl.ds(row0, 1), :], trade0),
                turned(cols_ref[pl.ds(row1, 1), :], trade1),
            )

    known_ref[16:24, :] = jnp.broadcast_to(jnp.max(seen_ref[:, 9:10, :], axis=0), (8, LANES))


def merge_stats(place, seen):
    return pl.pallas_call(
        merge_kernel,
        out_shape=jax.ShapeDtypeStruct((24, LANES), jnp.float32),
        in_specs=[SMEM, VMEM],
        out_specs=VMEM,
        scratch_shapes=[pltpu.VMEM((8, LANES), jnp.float32)],
        compiler_params=limit(2),
        cost_estimate=pl.CostEstimate(flops=10**5, bytes_accessed=2**17, transcendentals=2**14),
    )(place, seen)


def couple_kernel(
    place_ref,
    s0_ref,
    s1_ref,
    known_ref,
    told_ref,
    c_ref,
    give_one_ref,
    give_two_ref,
    take_one_ref,
    take_two_ref,
):
    core, xl, z, uhigh = place_ref[0], place_ref[1], place_ref[2], place_ref[3]
    rows = jnp.where(core == 0, known_ref[...], told_ref[...])
    cols = jnp.where(core == 0, told_ref[...], known_ref[...])
    eye = diagonal()
    lane = lax.broadcasted_iota(jnp.int32, (1, LANES), 1)
    index, col_lse = [], []
    for g in range(4):
        first = lax.rem(z + OFFSETS[2 * g] + NZ, NZ)
        second = lax.rem(z + OFFSETS[2 * g + 1] + NZ, NZ)
        user = jnp.where(lane < HALF, first, second) * (NY * NXH) + uhigh
        inside = jnp.where(lane < HALF, lane, lane - HALF)
        index.append((user * ROWS + xl * HALF + inside).astype(jnp.float32))
        col_lse.append(cols[g : g + 1, :])
    index = jnp.concatenate(index, axis=1)
    col_lse = jnp.concatenate(col_lse, axis=1)
    for u in range(NI // LANES):
        here = slice(u * LANES, (u + 1) * LANES)
        half_ref = s0_ref if u < NP // LANES else s1_ref
        start = u * LANES % NP
        s = half_ref[start : start + LANES, :]
        row_lse = jnp.sum(jnp.where(eye, rows[u : u + 1, :], 0.0), axis=1, keepdims=True)
        partner = jnp.sum(jnp.where(eye, rows[8 + u : 9 + u, :], 0.0), axis=1, keepdims=True)
        both = jnp.exp(s - row_lse) + jnp.exp(s - col_lse)
        positive = (partner == index).astype(jnp.float32)
        c_ref[here, :] = (0.5 * both - positive).astype(jnp.bfloat16)
    most_two = jnp.concatenate([rows[16:17, :]] * 4, axis=1)
    most_one = jnp.concatenate([cols[16:17, :]] * 4, axis=1)
    give_one_ref[...] = 128.0 / most_two
    take_one_ref[...] = most_two / 128.0
    give_two_ref[...] = 64.0 / most_one
    take_two_ref[...] = most_one / 64.0


def coupling_of(place, scores0, scores1, known, told):
    return pl.pallas_call(
        couple_kernel,
        out_shape=(
            jax.ShapeDtypeStruct((NI, NJ), jnp.bfloat16),
        )
        + (jax.ShapeDtypeStruct((1, WIDTH), jnp.float32),) * 4,
        in_specs=[SMEM] + [VMEM] * 4,
        out_specs=(VMEM,) * 5,
        compiler_params=limit(5),
        cost_estimate=pl.CostEstimate(
            flops=8 * NI * NJ, bytes_accessed=3 * 2**20, transcendentals=2 * NI * NJ
        ),
    )(place, scores0, scores1, known, told)


def swap(x, axis):
    return lax.ppermute(x, axis, [(0, 1), (1, 0)])


def number(z, y, xh, xl, c):
    return (((z * NY + y) * NXH + xh) * NXL + xl) * NC + c


def line_groups(turn):
    alongs_y = [
        [number(z, y, xh, xl, turn) for y in range(NY)]
        for z in range(NZ)
        for xl in range(NXL)
        for xh in range(NXH)
    ]
    alongs_x = [
        [number(z, y, xh, xl, 1 - turn) for xl in range(NXL) for xh in range(NXH)]
        for z in range(NZ)
        for y in range(NY)
    ]
    return alongs_y + alongs_x


def spread(x, turn):
    return lax.all_to_all(
        jnp.broadcast_to(x[None], (4,) + x.shape),
        EVERY,
        0,
        0,
        axis_index_groups=line_groups(turn),
        tiled=True,
    )


def stat_groups():
    planes = [
        [number(z, y, xh, xl, 0) for xl in range(NXL) for xh in range(NXH) for y in range(NY)]
        for z in range(NZ)
    ]
    columns = [
        [number(z, y, xh, xl, 1) for xl in range(NXL) for z in range(NZ)]
        for y in range(NY)
        for xh in range(NXH)
    ]
    return planes + columns


def to_plane(x, dz):
    return lax.ppermute(x, "z", [(z, (z + dz) % NZ) for z in range(NZ)])


def largest(x):
    return jnp.max(jnp.abs(x), axis=(0, 1)).astype(jnp.float32)


def on_device(view_one, view_two, partner):
    z = lax.axis_index("z")
    uhigh = lax.axis_index("y") * NXH + lax.axis_index("xh")
    xl = lax.axis_index("xl")
    core = lax.axis_index("core")
    place = jnp.stack([core, xl, z, uhigh]).astype(jnp.int32)

    keep = jnp.where(xl == 0, view_two[:HALF], view_two[HALF:])
    give = jnp.where(xl == 0, view_two[HALF:], view_two[:HALF])
    side = swap(give, "xl")
    lines = spread(view_one, 0)
    lines, side = lax.optimization_barrier((lines, side))
    here = jnp.where(xl == 0, jnp.stack([keep, side]), jnp.stack([side, keep]))
    up2, down2 = to_plane(here, -2), to_plane(here, 2)
    v1_all = spread(lines, 1).reshape(16, ROWS, WIDTH)
    up = to_plane(jnp.concatenate([here, up2], axis=1), -1)
    down = to_plane(jnp.concatenate([here, down2], axis=1), 1)
    v2_all, most_v2 = join(
        here, to_plane(up2[0], -2), to_plane(down2[1], 2), up2, down2, up, down
    )

    own0 = partial_scores(0, place, v1_all, v2_all)
    other0 = swap(own0, "core")
    own1 = partial_scores(1, place, v1_all, v2_all)
    other1 = swap(own1, "core")
    most = jnp.concatenate([most_v2, largest(v1_all)[None]])
    most_other = swap(most, "core")

    v1_rows = arranged(place, v1_all)
    other0, v1_rows = lax.optimization_barrier((other0, v1_rows))
    scores0, first, cols = first_stats(own0, other0)
    scores1, pack = second_stats(place, own1, other1, first, cols, partner, most, most_other)
    seen = lax.all_to_all(
        pack, EVERY, 0, 0, axis_index_groups=stat_groups(), tiled=True
    )
    known = merge_stats(place, seen)
    coupling, give_one, give_two, take_one, take_two = coupling_of(
        place, scores0, scores1, known, swap(known, "core")
    )

    part_one = (
        lax.dot_general(
            jnp.broadcast_to(coupling[None], (NXL, NI, NJ)),
            v2_all,
            (((2,), (1,)), ((0,), (0,))),
            preferred_element_type=jnp.float32,
        )
        * give_one
    ).astype(jnp.float16)
    coupling, part_one = lax.optimization_barrier((coupling, part_one))
    one_parts = lax.all_to_all(part_one.reshape(16, ROWS, WIDTH), PLANE, 0, 0, tiled=True)
    part_two = [
        (
            lax.dot_general(
                coupling, v1_rows[x], (((0,), (0,)), ((), ())), preferred_element_type=jnp.float32
            )
            * give_two
        ).astype(jnp.float16)
        for x in range(NXL)
    ]

    def blocks(start, stop):
        return jnp.stack([part[start * HALF : stop * HALF] for part in part_two])

    from_below, from_above = to_plane(blocks(4, 6), 1), to_plane(blocks(6, 8), -1)
    four0 = to_plane(part_two[0][HALF : 2 * HALF], 2)
    four1 = to_plane(part_two[1][HALF : 2 * HALF], -2)
    wide = [x.astype(jnp.float32) for x in (from_below, from_above, four0, four1)]
    up2 = blocks(2, 3).astype(jnp.float32) + wide[0][:, HALF:]
    up2 = jnp.stack([up2[0] + wide[2], up2[1]])
    down2 = blocks(3, 4).astype(jnp.float32) + wide[1][:, HALF:]
    down2 = jnp.stack([down2[0], down2[1] + wide[3]])
    from_up = to_plane((up2 * 0.25).astype(jnp.float16), 2)
    from_down = to_plane((down2 * 0.25).astype(jnp.float16), -2)
    total = blocks(0, 1).astype(jnp.float32) + wide[0][:, :HALF] + wide[1][:, :HALF]
    total = total + 4.0 * (from_up.astype(jnp.float32) + from_down.astype(jnp.float32))
    total = total * take_two
    stay = jnp.where(xl == 0, total[0], total[1])
    come = swap(jnp.where(xl == 0, total[1], total[0]), "xl")
    grad_one = jnp.sum(one_parts.astype(jnp.float32) * take_one, axis=0)
    come, grad_one = lax.optimization_barrier((come, grad_one))
    grad_two = jnp.where(
        xl == 0, jnp.concatenate([stay, come]), jnp.concatenate([come, stay])
    )
    return (grad_one, grad_two)


def solution(mesh):
    fine = Mesh(mesh.devices.reshape(NZ, NY, NXH, NXL, NC), EVERY)
    users = P(("z", "y", "xh"))
    both = P(("z", "y", "xh"), ("xl", "core"))
    return jax.shard_map(
        on_device,
        mesh=fine,
        in_specs=(both, both, users),
        out_specs=(both, both),
        check_vma=False,
    )
```

```python
import functools
import math

import jax
import jax.numpy as jnp
from jax import lax
from jax.experimental import pallas as pl
from jax.experimental.pallas import tpu as pltpu
from jax.sharding import Mesh
from jax.sharding import PartitionSpec as P

D = 2048
NZ, NY, NXH, NXL, NC = 8, 4, 2, 2, 2
PLANE = ("xl", "xh", "y")
OFFSETS = (0, 4, 2, -2, 1, 3, -1, -3)
GROUP = 128
EVERY = ("z", "y", "xh", "xl", "core")
ROWS = 128
HALF = 64
WIDTH = 512
NI = NY * NXH * ROWS
NJ = NZ * HALF
NP = NI // 2
LANES = 128
SCALE = 2.0 / math.sqrt(D)
VMEM = pl.BlockSpec(memory_space=pltpu.VMEM)
SMEM = pl.BlockSpec(memory_space=pltpu.SMEM)


def limit(mib):
    return pltpu.CompilerParams(vmem_limit_bytes=mib * 1024 * 1024)


def block_of(core, x, u):
    return jnp.where(core == 0, x * 8 + u, u % 4 * 4 + x * 2 + u // 4)


def arrange_kernel(place_ref, v1_ref, *o_refs):
    for x in range(NXL):
        for u in range(8):
            o_refs[x][u * ROWS : (u + 1) * ROWS, :] = v1_ref[block_of(place_ref[0], x, u)]


def arranged(place, v1_all):
    return pl.pallas_call(
        arrange_kernel,
        out_shape=(jax.ShapeDtypeStruct((NI, WIDTH), v1_all.dtype),) * NXL,
        in_specs=[SMEM, VMEM],
        out_specs=(VMEM,) * NXL,
        compiler_params=limit(5),
        cost_estimate=pl.CostEstimate(flops=0, bytes_accessed=2**22, transcendentals=0),
    )(place, v1_all)


def join_kernel(own, four0, four1, up2, down2, up, down, v2_ref, most_ref):
    v2_ref[:, :HALF, :] = own[...]
    v2_ref[0, HALF : 2 * HALF, :] = four0[...]
    v2_ref[1, HALF : 2 * HALF, :] = four1[...]
    v2_ref[:, 2 * HALF : 3 * HALF, :] = up2[...]
    v2_ref[:, 3 * HALF : 4 * HALF, :] = down2[...]
    v2_ref[:, 4 * HALF : 6 * HALF, :] = up[...]
    v2_ref[:, 6 * HALF :, :] = down[...]
    size = jnp.maximum(jnp.abs(v2_ref[0]), jnp.abs(v2_ref[1])).astype(jnp.float32)
    most_ref[...] = jnp.max(size, axis=0, keepdims=True)


def join(*parts):
    return pl.pallas_call(
        join_kernel,
        out_shape=(
            jax.ShapeDtypeStruct((NXL, NJ, WIDTH), jnp.bfloat16),
            jax.ShapeDtypeStruct((1, WIDTH), jnp.float32),
        ),
        in_specs=[VMEM] * 7,
        out_specs=(VMEM, VMEM),
        compiler_params=limit(4),
        cost_estimate=pl.CostEstimate(flops=12 * 2**30, bytes_accessed=2**21, transcendentals=0),
    )(*parts)


def score_kernel(part, place_ref, v1_ref, v2_ref, s_ref):
    users = range(part * (NP // ROWS), (part + 1) * (NP // ROWS))
    contract = (((1,), (1,)), ((), ()))
    s_ref[...] = sum(
        lax.dot_general(
            jnp.concatenate([v1_ref[block_of(place_ref[0], x, u)] for u in users]),
            v2_ref[x],
            contract,
            preferred_element_type=jnp.float32,
        )
        for x in range(NXL)
    )


def partial_scores(part, place, v1_all, v2_all):
    return pl.pallas_call(
        functools.partial(score_kernel, part),
        out_shape=jax.ShapeDtypeStruct((NP, NJ), jnp.float32),
        in_specs=[SMEM, VMEM, VMEM],
        out_specs=VMEM,
        compiler_params=limit(6),
        cost_estimate=pl.CostEstimate(
            flops=2 * NP * NJ * NXL * WIDTH, bytes_accessed=3 * 2**20, transcendentals=0
        ),
    )(place, v1_all, v2_all)


def diagonal():
    shape = (LANES, LANES)
    return lax.broadcasted_iota(jnp.int32, shape, 0) == lax.broadcasted_iota(jnp.int32, shape, 1)


def placed(z, k):
    plane = lax.rem(z + OFFSETS[k] + NZ, NZ)
    half = plane // 4
    return plane % 4, half, half != k % 2


def turned(row, trade):
    return jnp.where(trade, pltpu.roll(row, HALF, 1), row)


def lane_half():
    return lax.broadcasted_iota(jnp.int32, (1, LANES), 1) // HALF


def block_stats(own_ref, other_ref, s_ref, row_ref, col_highest, col_total):
    eye = diagonal()
    for u in range(NP // LANES):
        rows = slice(u * LANES, (u + 1) * LANES)
        s = SCALE * (own_ref[rows, :] + other_ref[rows, :])
        s_ref[rows, :] = s
        highest = jnp.max(s, axis=1, keepdims=True)
        lse = highest + jnp.log(jnp.sum(jnp.exp(s - highest), axis=1, keepdims=True))
        row_ref[u : u + 1, :] = jnp.sum(jnp.where(eye, lse, 0.0), axis=0, keepdims=True)
        higher = jnp.maximum(col_highest, jnp.max(s, axis=0, keepdims=True))
        col_total = col_total * jnp.exp(col_highest - higher) + jnp.sum(
            jnp.exp(s - higher), axis=0, keepdims=True
        )
        col_highest = higher
    return col_highest, col_total


def first_kernel(own_ref, other_ref, s_ref, row_ref, col_ref):
    highest, total = block_stats(
        own_ref,
        other_ref,
        s_ref,
        row_ref,
        jnp.full((1, NJ), -jnp.inf, jnp.float32),
        jnp.zeros((1, NJ), jnp.float32),
    )
    col_ref[0:1, :] = highest
    col_ref[1:2, :] = total


def first_stats(own, other):
    return pl.pallas_call(
        first_kernel,
        out_shape=(
            jax.ShapeDtypeStruct((NP, NJ), jnp.float32),
            jax.ShapeDtypeStruct((NP // LANES, LANES), jnp.float32),
            jax.ShapeDtypeStruct((2, NJ), jnp.float32),
        ),
        in_specs=[VMEM] * 2,
        out_specs=(VMEM,) * 3,
        compiler_params=limit(4),
        cost_estimate=pl.CostEstimate(
            flops=10 * NP * NJ, bytes_accessed=3 * 2**20, transcendentals=2 * NP * NJ
        ),
    )(own, other)


def second_kernel(
    place_ref,
    own_ref,
    other_ref,
    first_ref,
    col_ref,
    partner_ref,
    most_ref,
    most_other_ref,
    s_ref,
    out_ref,
    pack_ref,
):
    half = NP // LANES
    pack_ref[...] = jnp.zeros_like(pack_ref)
    pack_ref[0, 0:half, :] = first_ref[...]
    col_highest, col_total = block_stats(
        own_ref,
        other_ref,
        s_ref,
        pack_ref.at[0, half : 2 * half, :],
        col_ref[0:1, :],
        col_ref[1:2, :],
    )
    col_lse = col_highest + jnp.log(col_total)
    for k in range(NZ):
        row, half, trade = placed(place_ref[2], k)
        g = k // 2
        here = turned(col_lse[:, g * LANES : (g + 1) * LANES], trade)
        there = pack_ref[1, pl.ds(row, 1), :]
        pack_ref[1, pl.ds(row, 1), :] = jnp.where(lane_half() == half, here, there)
    most = jnp.max(jnp.maximum(most_ref[...], most_other_ref[...]), axis=1, keepdims=True)
    most = jnp.broadcast_to(jnp.maximum(most, 1e-30), (2, LANES))
    pack_ref[0, 8:9, :] = partner_ref[...].astype(jnp.float32)
    pack_ref[0, 9:10, :] = most[0:1, :]
    pack_ref[1, 9:10, :] = most[1:2, :]
    chosen = jnp.where(place_ref[0] == 0, pack_ref[0], pack_ref[1])
    for p in range(16):
        out_ref[p] = chosen


def second_stats(place, own, other, first, cols, partner, most, most_other):
    return pl.pallas_call(
        second_kernel,
        out_shape=(
            jax.ShapeDtypeStruct((NP, NJ), jnp.float32),
            jax.ShapeDtypeStruct((16, 16, LANES), jnp.float32),
        ),
        in_specs=[SMEM] + [VMEM] * 7,
        out_specs=(VMEM, VMEM),
        scratch_shapes=[pltpu.VMEM((2, 16, LANES), jnp.float32)],
        compiler_params=limit(4),
        cost_estimate=pl.CostEstimate(
            flops=10 * NP * NJ, bytes_accessed=3 * 2**20, transcendentals=2 * NP * NJ
        ),
    )(place, own, other, first, cols, partner.reshape(1, ROWS), most, most_other)


def merged(lses):
    top = jnp.max(lses, axis=0)
    return top + jnp.log(jnp.sum(jnp.exp(lses - top[None]), axis=0))


def merge_kernel(place_ref, seen_ref, known_ref, cols_ref):
    core, xl = place_ref[0], place_ref[1]

    @pl.when(core == 0)
    def _():
        known_ref[0:8, :] = merged(seen_ref[:, 0:8, :])
        for u in range(8):
            known_ref[8 + u : 9 + u, :] = seen_ref[u, 8:9, :]

    @pl.when(core != 0)
    def _():
        known_ref[...] = jnp.zeros_like(known_ref)
        cols_ref[...] = merged(seen_ref[pl.ds(xl * NZ, NZ), 0:8, :])
        for g in range(4):
            row0, _, trade0 = placed(place_ref[2], 2 * g)
            row1, _, trade1 = placed(place_ref[2], 2 * g + 1)
            known_ref[g : g + 1, :] = jnp.where(
                lane_half() == 0,
                turned(cols_ref[pl.ds(row0, 1), :], trade0),
                turned(cols_ref[pl.ds(row1, 1), :], trade1),
            )

    known_ref[16:24, :] = jnp.broadcast_to(jnp.max(seen_ref[:, 9:10, :], axis=0), (8, LANES))


def merge_stats(place, seen):
    return pl.pallas_call(
        merge_kernel,
        out_shape=jax.ShapeDtypeStruct((24, LANES), jnp.float32),
        in_specs=[SMEM, VMEM],
        out_specs=VMEM,
        scratch_shapes=[pltpu.VMEM((8, LANES), jnp.float32)],
        compiler_params=limit(2),
        cost_estimate=pl.CostEstimate(flops=10**5, bytes_accessed=2**17, transcendentals=2**14),
    )(place, seen)


def couple_kernel(
    place_ref,
    s0_ref,
    s1_ref,
    known_ref,
    told_ref,
    c_ref,
    give_one_ref,
    give_two_ref,
    take_one_ref,
    take_two_ref,
):
    core, xl, z, uhigh = place_ref[0], place_ref[1], place_ref[2], place_ref[3]
    rows = jnp.where(core == 0, known_ref[...], told_ref[...])
    cols = jnp.where(core == 0, told_ref[...], known_ref[...])
    eye = diagonal()
    lane = lax.broadcasted_iota(jnp.int32, (1, LANES), 1)
    index, col_lse = [], []
    for g in range(4):
        first = lax.rem(z + OFFSETS[2 * g] + NZ, NZ)
        second = lax.rem(z + OFFSETS[2 * g + 1] + NZ, NZ)
        user = jnp.where(lane < HALF, first, second) * (NY * NXH) + uhigh
        inside = jnp.where(lane < HALF, lane, lane - HALF)
        index.append((user * ROWS + xl * HALF + inside).astype(jnp.float32))
        col_lse.append(cols[g : g + 1, :])
    index = jnp.concatenate(index, axis=1)
    col_lse = jnp.concatenate(col_lse, axis=1)
    for u in range(NI // LANES):
        here = slice(u * LANES, (u + 1) * LANES)
        half_ref = s0_ref if u < NP // LANES else s1_ref
        start = u * LANES % NP
        s = half_ref[start : start + LANES, :]
        row_lse = jnp.sum(jnp.where(eye, rows[u : u + 1, :], 0.0), axis=1, keepdims=True)
        partner = jnp.sum(jnp.where(eye, rows[8 + u : 9 + u, :], 0.0), axis=1, keepdims=True)
        both = jnp.exp(s - row_lse) + jnp.exp(s - col_lse)
        positive = (partner == index).astype(jnp.float32)
        c_ref[here, :] = (0.5 * both - positive).astype(jnp.bfloat16)
    most_two = jnp.concatenate([rows[16:17, :]] * 4, axis=1)
    most_one = jnp.concatenate([cols[16:17, :]] * 4, axis=1)
    give_one_ref[...] = 128.0 / most_two
    take_one_ref[...] = most_two / 128.0
    give_two_ref[...] = 64.0 / most_one
    take_two_ref[...] = most_one / 64.0


def coupling_of(place, scores0, scores1, known, told):
    return pl.pallas_call(
        couple_kernel,
        out_shape=(
            jax.ShapeDtypeStruct((NI, NJ), jnp.bfloat16),
        )
        + (jax.ShapeDtypeStruct((1, WIDTH), jnp.float32),) * 4,
        in_specs=[SMEM] + [VMEM] * 4,
        out_specs=(VMEM,) * 5,
        compiler_params=limit(5),
        cost_estimate=pl.CostEstimate(
            flops=8 * NI * NJ, bytes_accessed=3 * 2**20, transcendentals=2 * NI * NJ
        ),
    )(place, scores0, scores1, known, told)


def swap(x, axis):
    return lax.ppermute(x, axis, [(0, 1), (1, 0)])


def number(z, y, xh, xl, c):
    return (((z * NY + y) * NXH + xh) * NXL + xl) * NC + c


def line_groups(turn):
    alongs_y = [
        [number(z, y, xh, xl, turn) for y in range(NY)]
        for z in range(NZ)
        for xl in range(NXL)
        for xh in range(NXH)
    ]
    alongs_x = [
        [number(z, y, xh, xl, 1 - turn) for xl in range(NXL) for xh in range(NXH)]
        for z in range(NZ)
        for y in range(NY)
    ]
    return alongs_y + alongs_x


def spread(x, turn):
    return lax.all_to_all(
        jnp.broadcast_to(x[None], (4,) + x.shape),
        EVERY,
        0,
        0,
        axis_index_groups=line_groups(turn),
        tiled=True,
    )


def stat_groups():
    planes = [
        [number(z, y, xh, xl, 0) for xl in range(NXL) for xh in range(NXH) for y in range(NY)]
        for z in range(NZ)
    ]
    columns = [
        [number(z, y, xh, xl, 1) for xl in range(NXL) for z in range(NZ)]
        for y in range(NY)
        for xh in range(NXH)
    ]
    return planes + columns


def to_plane(x, dz):
    return lax.ppermute(x, "z", [(z, (z + dz) % NZ) for z in range(NZ)])


def largest(x):
    return jnp.max(jnp.abs(x), axis=(0, 1)).astype(jnp.float32)


def on_device(view_one, view_two, partner):
    z = lax.axis_index("z")
    uhigh = lax.axis_index("y") * NXH + lax.axis_index("xh")
    xl = lax.axis_index("xl")
    core = lax.axis_index("core")
    place = jnp.stack([core, xl, z, uhigh]).astype(jnp.int32)

    keep = jnp.where(xl == 0, view_two[:HALF], view_two[HALF:])
    give = jnp.where(xl == 0, view_two[HALF:], view_two[:HALF])
    side = swap(give, "xl")
    lines = spread(view_one, 0)
    lines, side = lax.optimization_barrier((lines, side))
    here = jnp.where(xl == 0, jnp.stack([keep, side]), jnp.stack([side, keep]))
    up2, down2 = to_plane(here, -2), to_plane(here, 2)
    v1_all = spread(lines, 1).reshape(16, ROWS, WIDTH)
    up = to_plane(jnp.concatenate([here, up2], axis=1), -1)
    down = to_plane(jnp.concatenate([here, down2], axis=1), 1)
    v2_all, most_v2 = join(
        here, to_plane(up2[0], -2), to_plane(down2[1], 2), up2, down2, up, down
    )

    own0 = partial_scores(0, place, v1_all, v2_all)
    other0 = swap(own0, "core")
    own1 = partial_scores(1, place, v1_all, v2_all)
    other1 = swap(own1, "core")
    most = jnp.concatenate([most_v2, largest(v1_all)[None]])
    most_other = swap(most, "core")

    scores0, first, cols = first_stats(own0, other0)
    scores1, pack = second_stats(place, own1, other1, first, cols, partner, most, most_other)
    seen = lax.all_to_all(
        pack, EVERY, 0, 0, axis_index_groups=stat_groups(), tiled=True
    )
    v1_rows = arranged(place, v1_all)
    known = merge_stats(place, seen)
    coupling, give_one, give_two, take_one, take_two = coupling_of(
        place, scores0, scores1, known, swap(known, "core")
    )

    part_one = (
        lax.dot_general(
            jnp.broadcast_to(coupling[None], (NXL, NI, NJ)),
            v2_all,
            (((2,), (1,)), ((0,), (0,))),
            preferred_element_type=jnp.float32,
        )
        * give_one
    ).astype(jnp.float16)
    coupling, part_one = lax.optimization_barrier((coupling, part_one))
    one_parts = lax.all_to_all(part_one.reshape(16, ROWS, WIDTH), PLANE, 0, 0, tiled=True)
    part_two = [
        (
            lax.dot_general(
                coupling, v1_rows[x], (((0,), (0,)), ((), ())), preferred_element_type=jnp.float32
            )
            * give_two
        ).astype(jnp.float16)
        for x in range(NXL)
    ]

    def blocks(start, stop):
        return jnp.stack([part[start * HALF : stop * HALF] for part in part_two])

    from_below, from_above = to_plane(blocks(4, 6), 1), to_plane(blocks(6, 8), -1)
    four0 = to_plane(part_two[0][HALF : 2 * HALF], 2)
    four1 = to_plane(part_two[1][HALF : 2 * HALF], -2)
    wide = [x.astype(jnp.float32) for x in (from_below, from_above, four0, four1)]
    up2 = blocks(2, 3).astype(jnp.float32) + wide[0][:, HALF:]
    up2 = jnp.stack([up2[0] + wide[2], up2[1]])
    down2 = blocks(3, 4).astype(jnp.float32) + wide[1][:, HALF:]
    down2 = jnp.stack([down2[0], down2[1] + wide[3]])
    from_up = to_plane((up2 * 0.25).astype(jnp.float16), 2)
    from_down = to_plane((down2 * 0.25).astype(jnp.float16), -2)
    total = blocks(0, 1).astype(jnp.float32) + wide[0][:, :HALF] + wide[1][:, :HALF]
    total = total + 4.0 * (from_up.astype(jnp.float32) + from_down.astype(jnp.float32))
    stay = jnp.where(xl == 0, total[0], total[1])
    leave = jnp.where(xl == 0, total[1], total[0])
    come = swap((leave * 0.125).astype(jnp.float16), "xl")
    grad_one = jnp.sum(one_parts.astype(jnp.float32) * take_one, axis=0)
    come, grad_one = lax.optimization_barrier((come, grad_one))
    come = 8.0 * come.astype(jnp.float32)
    grad_two = take_two * jnp.where(
        xl == 0, jnp.concatenate([stay, come]), jnp.concatenate([come, stay])
    )
    return (grad_one, grad_two)


def solution(mesh):
    fine = Mesh(mesh.devices.reshape(NZ, NY, NXH, NXL, NC), EVERY)
    users = P(("z", "y", "xh"))
    both = P(("z", "y", "xh"), ("xl", "core"))
    return jax.shard_map(
        on_device,
        mesh=fine,
        in_specs=(both, both, users),
        out_specs=(both, both),
        check_vma=False,
    )
```

```python
import functools
import math

import jax
import jax.numpy as jnp
from jax import lax
from jax.experimental import pallas as pl
from jax.experimental.pallas import tpu as pltpu
from jax.sharding import Mesh
from jax.sharding import PartitionSpec as P

D = 2048
NZ, NY, NXH, NXL, NC = 8, 4, 2, 2, 2
PLANE = ("xl", "xh", "y")
OFFSETS = (0, 4, 2, -2, 1, 3, -1, -3)
GROUP = 128
EVERY = ("z", "y", "xh", "xl", "core")
ROWS = 128
HALF = 64
WIDTH = 512
NI = NY * NXH * ROWS
NJ = NZ * HALF
NP = NI // 2
LANES = 128
SCALE = 2.0 / math.sqrt(D)
VMEM = pl.BlockSpec(memory_space=pltpu.VMEM)
SMEM = pl.BlockSpec(memory_space=pltpu.SMEM)


def limit(mib):
    return pltpu.CompilerParams(vmem_limit_bytes=mib * 1024 * 1024)


def block_of(core, x, u):
    return jnp.where(core == 0, x * 8 + u, u % 4 * 4 + x * 2 + u // 4)


def arrange_kernel(place_ref, v1_ref, *o_refs):
    for x in range(NXL):
        for u in range(8):
            o_refs[x][u * ROWS : (u + 1) * ROWS, :] = v1_ref[block_of(place_ref[0], x, u)]


def arranged(place, v1_all):
    return pl.pallas_call(
        arrange_kernel,
        out_shape=(jax.ShapeDtypeStruct((NI, WIDTH), v1_all.dtype),) * NXL,
        in_specs=[SMEM, VMEM],
        out_specs=(VMEM,) * NXL,
        compiler_params=limit(5),
        cost_estimate=pl.CostEstimate(flops=0, bytes_accessed=2**22, transcendentals=0),
    )(place, v1_all)


def number_kernel(partner_ref, o_ref):
    o_ref[...] = partner_ref[...].astype(jnp.float32)


def numbers(partner):
    return pl.pallas_call(
        number_kernel,
        out_shape=jax.ShapeDtypeStruct((1, ROWS), jnp.float32),
        in_specs=[VMEM],
        out_specs=VMEM,
        compiler_params=limit(1),
        cost_estimate=pl.CostEstimate(flops=8 * 2**30, bytes_accessed=2**10, transcendentals=0),
    )(partner.reshape(1, ROWS))


def join_kernel(own, four0, four1, up2, down2, up, down, v2_ref, most_ref):
    v2_ref[:, :HALF, :] = own[...]
    v2_ref[0, HALF : 2 * HALF, :] = four0[...]
    v2_ref[1, HALF : 2 * HALF, :] = four1[...]
    v2_ref[:, 2 * HALF : 3 * HALF, :] = up2[...]
    v2_ref[:, 3 * HALF : 4 * HALF, :] = down2[...]
    v2_ref[:, 4 * HALF : 6 * HALF, :] = up[...]
    v2_ref[:, 6 * HALF :, :] = down[...]
    size = jnp.maximum(jnp.abs(v2_ref[0]), jnp.abs(v2_ref[1])).astype(jnp.float32)
    most_ref[...] = jnp.max(size, axis=0, keepdims=True)


def join(*parts):
    return pl.pallas_call(
        join_kernel,
        out_shape=(
            jax.ShapeDtypeStruct((NXL, NJ, WIDTH), jnp.bfloat16),
            jax.ShapeDtypeStruct((1, WIDTH), jnp.float32),
        ),
        in_specs=[VMEM] * 7,
        out_specs=(VMEM, VMEM),
        compiler_params=limit(4),
        cost_estimate=pl.CostEstimate(flops=12 * 2**30, bytes_accessed=2**21, transcendentals=0),
    )(*parts)


def score_kernel(part, place_ref, v1_ref, v2_ref, s_ref):
    users = range(part * (NP // ROWS), (part + 1) * (NP // ROWS))
    contract = (((1,), (1,)), ((), ()))
    s_ref[...] = sum(
        lax.dot_general(
            jnp.concatenate([v1_ref[block_of(place_ref[0], x, u)] for u in users]),
            v2_ref[x],
            contract,
            preferred_element_type=jnp.float32,
        )
        for x in range(NXL)
    )


def partial_scores(part, place, v1_all, v2_all):
    return pl.pallas_call(
        functools.partial(score_kernel, part),
        out_shape=jax.ShapeDtypeStruct((NP, NJ), jnp.float32),
        in_specs=[SMEM, VMEM, VMEM],
        out_specs=VMEM,
        compiler_params=limit(6),
        cost_estimate=pl.CostEstimate(
            flops=2 * NP * NJ * NXL * WIDTH, bytes_accessed=3 * 2**20, transcendentals=0
        ),
    )(place, v1_all, v2_all)


def diagonal():
    shape = (LANES, LANES)
    return lax.broadcasted_iota(jnp.int32, shape, 0) == lax.broadcasted_iota(jnp.int32, shape, 1)


def placed(z, k):
    plane = lax.rem(z + OFFSETS[k] + NZ, NZ)
    half = plane // 4
    return plane % 4, half, half != k % 2


def turned(row, trade):
    return jnp.where(trade, pltpu.roll(row, HALF, 1), row)


def lane_half():
    return lax.broadcasted_iota(jnp.int32, (1, LANES), 1) // HALF


def block_stats(own_ref, other_ref, s_ref, row_ref, col_highest, col_total):
    eye = diagonal()
    for u in range(NP // LANES):
        rows = slice(u * LANES, (u + 1) * LANES)
        s = SCALE * (own_ref[rows, :] + other_ref[rows, :])
        s_ref[rows, :] = s
        highest = jnp.max(s, axis=1, keepdims=True)
        lse = highest + jnp.log(jnp.sum(jnp.exp(s - highest), axis=1, keepdims=True))
        row_ref[u : u + 1, :] = jnp.sum(jnp.where(eye, lse, 0.0), axis=0, keepdims=True)
        higher = jnp.maximum(col_highest, jnp.max(s, axis=0, keepdims=True))
        col_total = col_total * jnp.exp(col_highest - higher) + jnp.sum(
            jnp.exp(s - higher), axis=0, keepdims=True
        )
        col_highest = higher
    return col_highest, col_total


def first_kernel(own_ref, other_ref, s_ref, row_ref, col_ref):
    highest, total = block_stats(
        own_ref,
        other_ref,
        s_ref,
        row_ref,
        jnp.full((1, NJ), -jnp.inf, jnp.float32),
        jnp.zeros((1, NJ), jnp.float32),
    )
    col_ref[0:1, :] = highest
    col_ref[1:2, :] = total


def first_stats(own, other):
    return pl.pallas_call(
        first_kernel,
        out_shape=(
            jax.ShapeDtypeStruct((NP, NJ), jnp.float32),
            jax.ShapeDtypeStruct((NP // LANES, LANES), jnp.float32),
            jax.ShapeDtypeStruct((2, NJ), jnp.float32),
        ),
        in_specs=[VMEM] * 2,
        out_specs=(VMEM,) * 3,
        compiler_params=limit(4),
        cost_estimate=pl.CostEstimate(
            flops=10 * NP * NJ, bytes_accessed=3 * 2**20, transcendentals=2 * NP * NJ
        ),
    )(own, other)


def second_kernel(
    place_ref,
    own_ref,
    other_ref,
    first_ref,
    col_ref,
    partner_ref,
    most_ref,
    most_other_ref,
    s_ref,
    out_ref,
    pack_ref,
):
    half = NP // LANES
    pack_ref[...] = jnp.zeros_like(pack_ref)
    pack_ref[0, 0:half, :] = first_ref[...]
    col_highest, col_total = block_stats(
        own_ref,
        other_ref,
        s_ref,
        pack_ref.at[0, half : 2 * half, :],
        col_ref[0:1, :],
        col_ref[1:2, :],
    )
    col_lse = col_highest + jnp.log(col_total)
    for k in range(NZ):
        row, half, trade = placed(place_ref[2], k)
        g = k // 2
        here = turned(col_lse[:, g * LANES : (g + 1) * LANES], trade)
        there = pack_ref[1, pl.ds(row, 1), :]
        pack_ref[1, pl.ds(row, 1), :] = jnp.where(lane_half() == half, here, there)
    most = jnp.max(jnp.maximum(most_ref[...], most_other_ref[...]), axis=1, keepdims=True)
    most = jnp.broadcast_to(jnp.maximum(most, 1e-30), (2, LANES))
    pack_ref[0, 8:9, :] = partner_ref[...]
    pack_ref[0, 9:10, :] = most[0:1, :]
    pack_ref[1, 9:10, :] = most[1:2, :]
    chosen = jnp.where(place_ref[0] == 0, pack_ref[0], pack_ref[1])
    for p in range(16):
        out_ref[p] = chosen


def second_stats(place, own, other, first, cols, partner, most, most_other):
    return pl.pallas_call(
        second_kernel,
        out_shape=(
            jax.ShapeDtypeStruct((NP, NJ), jnp.float32),
            jax.ShapeDtypeStruct((16, 16, LANES), jnp.float32),
        ),
        in_specs=[SMEM] + [VMEM] * 7,
        out_specs=(VMEM, VMEM),
        scratch_shapes=[pltpu.VMEM((2, 16, LANES), jnp.float32)],
        compiler_params=limit(4),
        cost_estimate=pl.CostEstimate(
            flops=10 * NP * NJ, bytes_accessed=3 * 2**20, transcendentals=2 * NP * NJ
        ),
    )(place, own, other, first, cols, partner, most, most_other)


def merged(lses):
    top = jnp.max(lses, axis=0)
    return top + jnp.log(jnp.sum(jnp.exp(lses - top[None]), axis=0))


def merge_kernel(place_ref, seen_ref, known_ref, cols_ref):
    core, xl = place_ref[0], place_ref[1]

    @pl.when(core == 0)
    def _():
        known_ref[0:8, :] = merged(seen_ref[:, 0:8, :])
        for u in range(8):
            known_ref[8 + u : 9 + u, :] = seen_ref[u, 8:9, :]

    @pl.when(core != 0)
    def _():
        known_ref[...] = jnp.zeros_like(known_ref)
        cols_ref[...] = merged(seen_ref[pl.ds(xl * NZ, NZ), 0:8, :])
        for g in range(4):
            row0, _, trade0 = placed(place_ref[2], 2 * g)
            row1, _, trade1 = placed(place_ref[2], 2 * g + 1)
            known_ref[g : g + 1, :] = jnp.where(
                lane_half() == 0,
                turned(cols_ref[pl.ds(row0, 1), :], trade0),
                turned(cols_ref[pl.ds(row1, 1), :], trade1),
            )

    known_ref[16:24, :] = jnp.broadcast_to(jnp.max(seen_ref[:, 9:10, :], axis=0), (8, LANES))


def merge_stats(place, seen):
    return pl.pallas_call(
        merge_kernel,
        out_shape=jax.ShapeDtypeStruct((24, LANES), jnp.float32),
        in_specs=[SMEM, VMEM],
        out_specs=VMEM,
        scratch_shapes=[pltpu.VMEM((8, LANES), jnp.float32)],
        compiler_params=limit(2),
        cost_estimate=pl.CostEstimate(flops=10**5, bytes_accessed=2**17, transcendentals=2**14),
    )(place, seen)


def couple_kernel(
    place_ref,
    s0_ref,
    s1_ref,
    known_ref,
    told_ref,
    c_ref,
    give_one_ref,
    give_two_ref,
    take_one_ref,
    take_two_ref,
):
    core, xl, z, uhigh = place_ref[0], place_ref[1], place_ref[2], place_ref[3]
    rows = jnp.where(core == 0, known_ref[...], told_ref[...])
    cols = jnp.where(core == 0, told_ref[...], known_ref[...])
    eye = diagonal()
    lane = lax.broadcasted_iota(jnp.int32, (1, LANES), 1)
    index, col_lse = [], []
    for g in range(4):
        first = lax.rem(z + OFFSETS[2 * g] + NZ, NZ)
        second = lax.rem(z + OFFSETS[2 * g + 1] + NZ, NZ)
        user = jnp.where(lane < HALF, first, second) * (NY * NXH) + uhigh
        inside = jnp.where(lane < HALF, lane, lane - HALF)
        index.append((user * ROWS + xl * HALF + inside).astype(jnp.float32))
        col_lse.append(cols[g : g + 1, :])
    index = jnp.concatenate(index, axis=1)
    col_lse = jnp.concatenate(col_lse, axis=1)
    for u in range(NI // LANES):
        here = slice(u * LANES, (u + 1) * LANES)
        half_ref = s0_ref if u < NP // LANES else s1_ref
        start = u * LANES % NP
        s = half_ref[start : start + LANES, :]
        row_lse = jnp.sum(jnp.where(eye, rows[u : u + 1, :], 0.0), axis=1, keepdims=True)
        partner = jnp.sum(jnp.where(eye, rows[8 + u : 9 + u, :], 0.0), axis=1, keepdims=True)
        both = jnp.exp(s - row_lse) + jnp.exp(s - col_lse)
        positive = (partner == index).astype(jnp.float32)
        c_ref[here, :] = (0.5 * both - positive).astype(jnp.bfloat16)
    most_two = jnp.concatenate([rows[16:17, :]] * 4, axis=1)
    most_one = jnp.concatenate([cols[16:17, :]] * 4, axis=1)
    give_one_ref[...] = 128.0 / most_two
    take_one_ref[...] = most_two / 128.0
    give_two_ref[...] = 64.0 / most_one
    take_two_ref[...] = most_one / 64.0


def coupling_of(place, scores0, scores1, known, told):
    return pl.pallas_call(
        couple_kernel,
        out_shape=(
            jax.ShapeDtypeStruct((NI, NJ), jnp.bfloat16),
        )
        + (jax.ShapeDtypeStruct((1, WIDTH), jnp.float32),) * 4,
        in_specs=[SMEM] + [VMEM] * 4,
        out_specs=(VMEM,) * 5,
        compiler_params=limit(5),
        cost_estimate=pl.CostEstimate(
            flops=8 * NI * NJ, bytes_accessed=3 * 2**20, transcendentals=2 * NI * NJ
        ),
    )(place, scores0, scores1, known, told)


def swap(x, axis):
    return lax.ppermute(x, axis, [(0, 1), (1, 0)])


def number(z, y, xh, xl, c):
    return (((z * NY + y) * NXH + xh) * NXL + xl) * NC + c


def line_groups(turn):
    alongs_y = [
        [number(z, y, xh, xl, turn) for y in range(NY)]
        for z in range(NZ)
        for xl in range(NXL)
        for xh in range(NXH)
    ]
    alongs_x = [
        [number(z, y, xh, xl, 1 - turn) for xl in range(NXL) for xh in range(NXH)]
        for z in range(NZ)
        for y in range(NY)
    ]
    return alongs_y + alongs_x


def spread(x, turn):
    return lax.all_to_all(
        jnp.broadcast_to(x[None], (4,) + x.shape),
        EVERY,
        0,
        0,
        axis_index_groups=line_groups(turn),
        tiled=True,
    )


def stat_groups():
    planes = [
        [number(z, y, xh, xl, 0) for xl in range(NXL) for xh in range(NXH) for y in range(NY)]
        for z in range(NZ)
    ]
    columns = [
        [number(z, y, xh, xl, 1) for xl in range(NXL) for z in range(NZ)]
        for y in range(NY)
        for xh in range(NXH)
    ]
    return planes + columns


def to_plane(x, dz):
    return lax.ppermute(x, "z", [(z, (z + dz) % NZ) for z in range(NZ)])


def largest(x):
    return jnp.max(jnp.abs(x), axis=(0, 1)).astype(jnp.float32)


def on_device(view_one, view_two, partner):
    z = lax.axis_index("z")
    uhigh = lax.axis_index("y") * NXH + lax.axis_index("xh")
    xl = lax.axis_index("xl")
    core = lax.axis_index("core")
    place = jnp.stack([core, xl, z, uhigh]).astype(jnp.int32)

    keep = jnp.where(xl == 0, view_two[:HALF], view_two[HALF:])
    give = jnp.where(xl == 0, view_two[HALF:], view_two[:HALF])
    side = swap(give, "xl")
    lines = spread(view_one, 0)
    partner = numbers(partner)
    lines, side, partner = lax.optimization_barrier((lines, side, partner))
    here = jnp.where(xl == 0, jnp.stack([keep, side]), jnp.stack([side, keep]))
    up2, down2 = to_plane(here, -2), to_plane(here, 2)
    v1_all = spread(lines, 1).reshape(16, ROWS, WIDTH)
    up = to_plane(jnp.concatenate([here, up2], axis=1), -1)
    down = to_plane(jnp.concatenate([here, down2], axis=1), 1)
    v2_all, most_v2 = join(
        here, to_plane(up2[0], -2), to_plane(down2[1], 2), up2, down2, up, down
    )

    own0 = partial_scores(0, place, v1_all, v2_all)
    other0 = swap(own0, "core")
    own1 = partial_scores(1, place, v1_all, v2_all)
    other1 = swap(own1, "core")
    most = jnp.concatenate([most_v2, largest(v1_all)[None]])
    most_other = swap(most, "core")

    scores0, first, cols = first_stats(own0, other0)
    scores1, pack = second_stats(place, own1, other1, first, cols, partner, most, most_other)
    seen = lax.all_to_all(
        pack, EVERY, 0, 0, axis_index_groups=stat_groups(), tiled=True
    )
    v1_rows = arranged(place, v1_all)
    known = merge_stats(place, seen)
    coupling, give_one, give_two, take_one, take_two = coupling_of(
        place, scores0, scores1, known, swap(known, "core")
    )

    part_one = (
        lax.dot_general(
            jnp.broadcast_to(coupling[None], (NXL, NI, NJ)),
            v2_all,
            (((2,), (1,)), ((0,), (0,))),
            preferred_element_type=jnp.float32,
        )
        * give_one
    ).astype(jnp.float16)
    coupling, part_one = lax.optimization_barrier((coupling, part_one))
    one_parts = lax.all_to_all(part_one.reshape(16, ROWS, WIDTH), PLANE, 0, 0, tiled=True)
    part_two = [
        (
            lax.dot_general(
                coupling, v1_rows[x], (((0,), (0,)), ((), ())), preferred_element_type=jnp.float32
            )
            * give_two
        ).astype(jnp.float16)
        for x in range(NXL)
    ]

    def blocks(start, stop):
        return jnp.stack([part[start * HALF : stop * HALF] for part in part_two])

    from_below, from_above = to_plane(blocks(4, 6), 1), to_plane(blocks(6, 8), -1)
    four0 = to_plane(part_two[0][HALF : 2 * HALF], 2)
    four1 = to_plane(part_two[1][HALF : 2 * HALF], -2)
    wide = [x.astype(jnp.float32) for x in (from_below, from_above, four0, four1)]
    up2 = blocks(2, 3).astype(jnp.float32) + wide[0][:, HALF:]
    up2 = jnp.stack([up2[0] + wide[2], up2[1]])
    down2 = blocks(3, 4).astype(jnp.float32) + wide[1][:, HALF:]
    down2 = jnp.stack([down2[0], down2[1] + wide[3]])
    from_up = to_plane((up2 * 0.25).astype(jnp.float16), 2)
    from_down = to_plane((down2 * 0.25).astype(jnp.float16), -2)
    total = blocks(0, 1).astype(jnp.float32) + wide[0][:, :HALF] + wide[1][:, :HALF]
    total = total + 4.0 * (from_up.astype(jnp.float32) + from_down.astype(jnp.float32))
    total = total * take_two
    stay = jnp.where(xl == 0, total[0], total[1])
    come = swap(jnp.where(xl == 0, total[1], total[0]), "xl")
    grad_one = jnp.sum(one_parts.astype(jnp.float32) * take_one, axis=0)
    come, grad_one = lax.optimization_barrier((come, grad_one))
    grad_two = jnp.where(
        xl == 0, jnp.concatenate([stay, come]), jnp.concatenate([come, stay])
    )
    return (grad_one, grad_two)


def solution(mesh):
    fine = Mesh(mesh.devices.reshape(NZ, NY, NXH, NXL, NC), EVERY)
    users = P(("z", "y", "xh"))
    both = P(("z", "y", "xh"), ("xl", "core"))
    return jax.shard_map(
        on_device,
        mesh=fine,
        in_specs=(both, both, users),
        out_specs=(both, both),
        check_vma=False,
    )
```

```python
import functools
import math

import jax
import jax.numpy as jnp
from jax import lax
from jax.experimental import pallas as pl
from jax.experimental.pallas import tpu as pltpu
from jax.sharding import Mesh
from jax.sharding import PartitionSpec as P

D = 2048
NZ, NY, NXH, NXL, NC = 8, 4, 2, 2, 2
PLANE = ("xl", "xh", "y")
OFFSETS = (0, 4, 2, -2, 1, 3, -1, -3)
GROUP = 128
EVERY = ("z", "y", "xh", "xl", "core")
ROWS = 128
HALF = 64
WIDTH = 512
NI = NY * NXH * ROWS
NJ = NZ * HALF
NP = NI // 2
LANES = 128
SCALE = 2.0 / math.sqrt(D)
VMEM = pl.BlockSpec(memory_space=pltpu.VMEM)
SMEM = pl.BlockSpec(memory_space=pltpu.SMEM)


def limit(mib):
    return pltpu.CompilerParams(vmem_limit_bytes=mib * 1024 * 1024)


def block_of(core, x, u):
    return jnp.where(core == 0, x * 8 + u, u % 4 * 4 + x * 2 + u // 4)


def arrange_kernel(place_ref, v1_ref, *o_refs):
    for x in range(NXL):
        for u in range(8):
            o_refs[x][u * ROWS : (u + 1) * ROWS, :] = v1_ref[block_of(place_ref[0], x, u)]


def arranged(place, v1_all):
    return pl.pallas_call(
        arrange_kernel,
        out_shape=(jax.ShapeDtypeStruct((NI, WIDTH), v1_all.dtype),) * NXL,
        in_specs=[SMEM, VMEM],
        out_specs=(VMEM,) * NXL,
        compiler_params=limit(5),
        cost_estimate=pl.CostEstimate(flops=0, bytes_accessed=2**22, transcendentals=0),
    )(place, v1_all)


def number_kernel(partner_ref, o_ref):
    o_ref[...] = partner_ref[...].astype(jnp.float32)


def numbers(partner):
    return pl.pallas_call(
        number_kernel,
        out_shape=jax.ShapeDtypeStruct((1, ROWS), jnp.float32),
        in_specs=[VMEM],
        out_specs=VMEM,
        compiler_params=limit(1),
        cost_estimate=pl.CostEstimate(flops=8 * 2**30, bytes_accessed=2**10, transcendentals=0),
    )(partner.reshape(1, ROWS))


def join_kernel(own, four0, four1, up2, down2, up, down, v2_ref, most_ref):
    v2_ref[:, :HALF, :] = own[...]
    v2_ref[0, HALF : 2 * HALF, :] = four0[...]
    v2_ref[1, HALF : 2 * HALF, :] = four1[...]
    v2_ref[:, 2 * HALF : 3 * HALF, :] = up2[...]
    v2_ref[:, 3 * HALF : 4 * HALF, :] = down2[...]
    v2_ref[:, 4 * HALF : 6 * HALF, :] = up[...]
    v2_ref[:, 6 * HALF :, :] = down[...]
    size = jnp.maximum(jnp.abs(v2_ref[0]), jnp.abs(v2_ref[1])).astype(jnp.float32)
    most_ref[...] = jnp.max(size, axis=0, keepdims=True)


def join(*parts):
    return pl.pallas_call(
        join_kernel,
        out_shape=(
            jax.ShapeDtypeStruct((NXL, NJ, WIDTH), jnp.bfloat16),
            jax.ShapeDtypeStruct((1, WIDTH), jnp.float32),
        ),
        in_specs=[VMEM] * 7,
        out_specs=(VMEM, VMEM),
        compiler_params=limit(4),
        cost_estimate=pl.CostEstimate(flops=10 * 2**30, bytes_accessed=2**21, transcendentals=0),
    )(*parts)


def score_kernel(part, place_ref, v1_ref, v2_ref, s_ref):
    users = range(part * (NP // ROWS), (part + 1) * (NP // ROWS))
    contract = (((1,), (1,)), ((), ()))
    s_ref[...] = sum(
        lax.dot_general(
            jnp.concatenate([v1_ref[block_of(place_ref[0], x, u)] for u in users]),
            v2_ref[x],
            contract,
            preferred_element_type=jnp.float32,
        )
        for x in range(NXL)
    )


def partial_scores(part, place, v1_all, v2_all):
    return pl.pallas_call(
        functools.partial(score_kernel, part),
        out_shape=jax.ShapeDtypeStruct((NP, NJ), jnp.float32),
        in_specs=[SMEM, VMEM, VMEM],
        out_specs=VMEM,
        compiler_params=limit(6),
        cost_estimate=pl.CostEstimate(
            flops=2 * NP * NJ * NXL * WIDTH, bytes_accessed=3 * 2**20, transcendentals=0
        ),
    )(place, v1_all, v2_all)


def diagonal():
    shape = (LANES, LANES)
    return lax.broadcasted_iota(jnp.int32, shape, 0) == lax.broadcasted_iota(jnp.int32, shape, 1)


def placed(z, k):
    plane = lax.rem(z + OFFSETS[k] + NZ, NZ)
    half = plane // 4
    return plane % 4, half, half != k % 2


def turned(row, trade):
    return jnp.where(trade, pltpu.roll(row, HALF, 1), row)


def lane_half():
    return lax.broadcasted_iota(jnp.int32, (1, LANES), 1) // HALF


def block_stats(own_ref, other_ref, s_ref, row_ref, col_highest, col_total):
    eye = diagonal()
    for u in range(NP // LANES):
        rows = slice(u * LANES, (u + 1) * LANES)
        s = SCALE * (own_ref[rows, :] + other_ref[rows, :])
        s_ref[rows, :] = s
        highest = jnp.max(s, axis=1, keepdims=True)
        lse = highest + jnp.log(jnp.sum(jnp.exp(s - highest), axis=1, keepdims=True))
        row_ref[u : u + 1, :] = jnp.sum(jnp.where(eye, lse, 0.0), axis=0, keepdims=True)
        higher = jnp.maximum(col_highest, jnp.max(s, axis=0, keepdims=True))
        col_total = col_total * jnp.exp(col_highest - higher) + jnp.sum(
            jnp.exp(s - higher), axis=0, keepdims=True
        )
        col_highest = higher
    return col_highest, col_total


def first_kernel(own_ref, other_ref, s_ref, row_ref, col_ref):
    highest, total = block_stats(
        own_ref,
        other_ref,
        s_ref,
        row_ref,
        jnp.full((1, NJ), -jnp.inf, jnp.float32),
        jnp.zeros((1, NJ), jnp.float32),
    )
    col_ref[0:1, :] = highest
    col_ref[1:2, :] = total


def first_stats(own, other):
    return pl.pallas_call(
        first_kernel,
        out_shape=(
            jax.ShapeDtypeStruct((NP, NJ), jnp.float32),
            jax.ShapeDtypeStruct((NP // LANES, LANES), jnp.float32),
            jax.ShapeDtypeStruct((2, NJ), jnp.float32),
        ),
        in_specs=[VMEM] * 2,
        out_specs=(VMEM,) * 3,
        compiler_params=limit(4),
        cost_estimate=pl.CostEstimate(
            flops=10 * NP * NJ, bytes_accessed=3 * 2**20, transcendentals=2 * NP * NJ
        ),
    )(own, other)


def second_kernel(
    place_ref,
    own_ref,
    other_ref,
    first_ref,
    col_ref,
    partner_ref,
    most_ref,
    most_other_ref,
    s_ref,
    out_ref,
    pack_ref,
):
    half = NP // LANES
    pack_ref[...] = jnp.zeros_like(pack_ref)
    pack_ref[0, 0:half, :] = first_ref[...]
    col_highest, col_total = block_stats(
        own_ref,
        other_ref,
        s_ref,
        pack_ref.at[0, half : 2 * half, :],
        col_ref[0:1, :],
        col_ref[1:2, :],
    )
    col_lse = col_highest + jnp.log(col_total)
    for k in range(NZ):
        row, half, trade = placed(place_ref[2], k)
        g = k // 2
        here = turned(col_lse[:, g * LANES : (g + 1) * LANES], trade)
        there = pack_ref[1, pl.ds(row, 1), :]
        pack_ref[1, pl.ds(row, 1), :] = jnp.where(lane_half() == half, here, there)
    most = jnp.max(jnp.maximum(most_ref[...], most_other_ref[...]), axis=1, keepdims=True)
    most = jnp.broadcast_to(jnp.maximum(most, 1e-30), (2, LANES))
    pack_ref[0, 8:9, :] = partner_ref[...]
    pack_ref[0, 9:10, :] = most[0:1, :]
    pack_ref[1, 9:10, :] = most[1:2, :]
    chosen = jnp.where(place_ref[0] == 0, pack_ref[0], pack_ref[1])
    for p in range(16):
        out_ref[p] = chosen


def second_stats(place, own, other, first, cols, partner, most, most_other):
    return pl.pallas_call(
        second_kernel,
        out_shape=(
            jax.ShapeDtypeStruct((NP, NJ), jnp.float32),
            jax.ShapeDtypeStruct((16, 16, LANES), jnp.float32),
        ),
        in_specs=[SMEM] + [VMEM] * 7,
        out_specs=(VMEM, VMEM),
        scratch_shapes=[pltpu.VMEM((2, 16, LANES), jnp.float32)],
        compiler_params=limit(4),
        cost_estimate=pl.CostEstimate(
            flops=10 * NP * NJ, bytes_accessed=3 * 2**20, transcendentals=2 * NP * NJ
        ),
    )(place, own, other, first, cols, partner, most, most_other)


def merged(lses):
    top = jnp.max(lses, axis=0)
    return top + jnp.log(jnp.sum(jnp.exp(lses - top[None]), axis=0))


def merge_kernel(place_ref, seen_ref, known_ref, cols_ref):
    core, xl = place_ref[0], place_ref[1]

    @pl.when(core == 0)
    def _():
        known_ref[0:8, :] = merged(seen_ref[:, 0:8, :])
        for u in range(8):
            known_ref[8 + u : 9 + u, :] = seen_ref[u, 8:9, :]

    @pl.when(core != 0)
    def _():
        known_ref[...] = jnp.zeros_like(known_ref)
        cols_ref[...] = merged(seen_ref[pl.ds(xl * NZ, NZ), 0:8, :])
        for g in range(4):
            row0, _, trade0 = placed(place_ref[2], 2 * g)
            row1, _, trade1 = placed(place_ref[2], 2 * g + 1)
            known_ref[g : g + 1, :] = jnp.where(
                lane_half() == 0,
                turned(cols_ref[pl.ds(row0, 1), :], trade0),
                turned(cols_ref[pl.ds(row1, 1), :], trade1),
            )

    known_ref[16:24, :] = jnp.broadcast_to(jnp.max(seen_ref[:, 9:10, :], axis=0), (8, LANES))


def merge_stats(place, seen):
    return pl.pallas_call(
        merge_kernel,
        out_shape=jax.ShapeDtypeStruct((24, LANES), jnp.float32),
        in_specs=[SMEM, VMEM],
        out_specs=VMEM,
        scratch_shapes=[pltpu.VMEM((8, LANES), jnp.float32)],
        compiler_params=limit(2),
        cost_estimate=pl.CostEstimate(flops=10**5, bytes_accessed=2**17, transcendentals=2**14),
    )(place, seen)


def couple_kernel(
    place_ref,
    s0_ref,
    s1_ref,
    known_ref,
    told_ref,
    c_ref,
    give_one_ref,
    give_two_ref,
    take_one_ref,
    take_two_ref,
):
    core, xl, z, uhigh = place_ref[0], place_ref[1], place_ref[2], place_ref[3]
    rows = jnp.where(core == 0, known_ref[...], told_ref[...])
    cols = jnp.where(core == 0, told_ref[...], known_ref[...])
    eye = diagonal()
    lane = lax.broadcasted_iota(jnp.int32, (1, LANES), 1)
    index, col_lse = [], []
    for g in range(4):
        first = lax.rem(z + OFFSETS[2 * g] + NZ, NZ)
        second = lax.rem(z + OFFSETS[2 * g + 1] + NZ, NZ)
        user = jnp.where(lane < HALF, first, second) * (NY * NXH) + uhigh
        inside = jnp.where(lane < HALF, lane, lane - HALF)
        index.append((user * ROWS + xl * HALF + inside).astype(jnp.float32))
        col_lse.append(cols[g : g + 1, :])
    index = jnp.concatenate(index, axis=1)
    col_lse = jnp.concatenate(col_lse, axis=1)
    for u in range(NI // LANES):
        here = slice(u * LANES, (u + 1) * LANES)
        half_ref = s0_ref if u < NP // LANES else s1_ref
        start = u * LANES % NP
        s = half_ref[start : start + LANES, :]
        row_lse = jnp.sum(jnp.where(eye, rows[u : u + 1, :], 0.0), axis=1, keepdims=True)
        partner = jnp.sum(jnp.where(eye, rows[8 + u : 9 + u, :], 0.0), axis=1, keepdims=True)
        both = jnp.exp(s - row_lse) + jnp.exp(s - col_lse)
        positive = (partner == index).astype(jnp.float32)
        c_ref[here, :] = (0.5 * both - positive).astype(jnp.bfloat16)
    most_two = jnp.concatenate([rows[16:17, :]] * 4, axis=1)
    most_one = jnp.concatenate([cols[16:17, :]] * 4, axis=1)
    give_one_ref[...] = 128.0 / most_two
    take_one_ref[...] = most_two / 128.0
    give_two_ref[...] = 64.0 / most_one
    take_two_ref[...] = most_one / 64.0


def coupling_of(place, scores0, scores1, known, told):
    return pl.pallas_call(
        couple_kernel,
        out_shape=(
            jax.ShapeDtypeStruct((NI, NJ), jnp.bfloat16),
        )
        + (jax.ShapeDtypeStruct((1, WIDTH), jnp.float32),) * 4,
        in_specs=[SMEM] + [VMEM] * 4,
        out_specs=(VMEM,) * 5,
        compiler_params=limit(5),
        cost_estimate=pl.CostEstimate(
            flops=8 * NI * NJ, bytes_accessed=3 * 2**20, transcendentals=2 * NI * NJ
        ),
    )(place, scores0, scores1, known, told)


def swap(x, axis):
    return lax.ppermute(x, axis, [(0, 1), (1, 0)])


def number(z, y, xh, xl, c):
    return (((z * NY + y) * NXH + xh) * NXL + xl) * NC + c


def line_groups(turn):
    alongs_y = [
        [number(z, y, xh, xl, turn) for y in range(NY)]
        for z in range(NZ)
        for xl in range(NXL)
        for xh in range(NXH)
    ]
    alongs_x = [
        [number(z, y, xh, xl, 1 - turn) for xl in range(NXL) for xh in range(NXH)]
        for z in range(NZ)
        for y in range(NY)
    ]
    return alongs_y + alongs_x


def spread(x, turn):
    return lax.all_to_all(
        jnp.broadcast_to(x[None], (4,) + x.shape),
        EVERY,
        0,
        0,
        axis_index_groups=line_groups(turn),
        tiled=True,
    )


def stat_groups():
    planes = [
        [number(z, y, xh, xl, 0) for xl in range(NXL) for xh in range(NXH) for y in range(NY)]
        for z in range(NZ)
    ]
    columns = [
        [number(z, y, xh, xl, 1) for xl in range(NXL) for z in range(NZ)]
        for y in range(NY)
        for xh in range(NXH)
    ]
    return planes + columns


def to_plane(x, dz):
    return lax.ppermute(x, "z", [(z, (z + dz) % NZ) for z in range(NZ)])


def largest(x):
    return jnp.max(jnp.abs(x), axis=(0, 1)).astype(jnp.float32)


def on_device(view_one, view_two, partner):
    z = lax.axis_index("z")
    uhigh = lax.axis_index("y") * NXH + lax.axis_index("xh")
    xl = lax.axis_index("xl")
    core = lax.axis_index("core")
    place = jnp.stack([core, xl, z, uhigh]).astype(jnp.int32)

    keep = jnp.where(xl == 0, view_two[:HALF], view_two[HALF:])
    give = jnp.where(xl == 0, view_two[HALF:], view_two[:HALF])
    side = swap(give, "xl")
    lines = spread(view_one, 0)
    partner = numbers(partner)
    side, partner = lax.optimization_barrier((side, partner))
    lines, _ = lax.optimization_barrier((lines, side))
    here = jnp.where(xl == 0, jnp.stack([keep, side]), jnp.stack([side, keep]))
    up2, down2 = to_plane(here, -2), to_plane(here, 2)
    v1_all = spread(lines, 1).reshape(16, ROWS, WIDTH)
    up = to_plane(jnp.concatenate([here, up2], axis=1), -1)
    down = to_plane(jnp.concatenate([here, down2], axis=1), 1)
    v2_all, most_v2 = join(
        here, to_plane(up2[0], -2), to_plane(down2[1], 2), up2, down2, up, down
    )

    own0 = partial_scores(0, place, v1_all, v2_all)
    other0 = swap(own0, "core")
    own1 = partial_scores(1, place, v1_all, v2_all)
    other1 = swap(own1, "core")
    most = jnp.concatenate([most_v2, largest(v1_all)[None]])
    most_other = swap(most, "core")

    scores0, first, cols = first_stats(own0, other0)
    scores1, pack = second_stats(place, own1, other1, first, cols, partner, most, most_other)
    seen = lax.all_to_all(
        pack, EVERY, 0, 0, axis_index_groups=stat_groups(), tiled=True
    )
    v1_rows = arranged(place, v1_all)
    known = merge_stats(place, seen)
    coupling, give_one, give_two, take_one, take_two = coupling_of(
        place, scores0, scores1, known, swap(known, "core")
    )

    part_one = (
        lax.dot_general(
            jnp.broadcast_to(coupling[None], (NXL, NI, NJ)),
            v2_all,
            (((2,), (1,)), ((0,), (0,))),
            preferred_element_type=jnp.float32,
        )
        * give_one
    ).astype(jnp.float16)
    coupling, part_one = lax.optimization_barrier((coupling, part_one))
    one_parts = lax.all_to_all(part_one.reshape(16, ROWS, WIDTH), PLANE, 0, 0, tiled=True)
    part_two = [
        (
            lax.dot_general(
                coupling, v1_rows[x], (((0,), (0,)), ((), ())), preferred_element_type=jnp.float32
            )
            * give_two
        ).astype(jnp.float16)
        for x in range(NXL)
    ]

    def blocks(start, stop):
        return jnp.stack([part[start * HALF : stop * HALF] for part in part_two])

    from_below, from_above = to_plane(blocks(4, 6), 1), to_plane(blocks(6, 8), -1)
    four0 = to_plane(part_two[0][HALF : 2 * HALF], 2)
    four1 = to_plane(part_two[1][HALF : 2 * HALF], -2)
    wide = [x.astype(jnp.float32) for x in (from_below, from_above, four0, four1)]
    up2 = blocks(2, 3).astype(jnp.float32) + wide[0][:, HALF:]
    up2 = jnp.stack([up2[0] + wide[2], up2[1]])
    down2 = blocks(3, 4).astype(jnp.float32) + wide[1][:, HALF:]
    down2 = jnp.stack([down2[0], down2[1] + wide[3]])
    from_up = to_plane((up2 * 0.25).astype(jnp.float16), 2)
    from_down = to_plane((down2 * 0.25).astype(jnp.float16), -2)
    total = blocks(0, 1).astype(jnp.float32) + wide[0][:, :HALF] + wide[1][:, :HALF]
    total = total + 4.0 * (from_up.astype(jnp.float32) + from_down.astype(jnp.float32))
    total = total * take_two
    stay = jnp.where(xl == 0, total[0], total[1])
    come = swap(jnp.where(xl == 0, total[1], total[0]), "xl")
    grad_one = jnp.sum(one_parts.astype(jnp.float32) * take_one, axis=0)
    come, grad_one = lax.optimization_barrier((come, grad_one))
    grad_two = jnp.where(
        xl == 0, jnp.concatenate([stay, come]), jnp.concatenate([come, stay])
    )
    return (grad_one, grad_two)


def solution(mesh):
    fine = Mesh(mesh.devices.reshape(NZ, NY, NXH, NXL, NC), EVERY)
    users = P(("z", "y", "xh"))
    both = P(("z", "y", "xh"), ("xl", "core"))
    return jax.shard_map(
        on_device,
        mesh=fine,
        in_specs=(both, both, users),
        out_specs=(both, both),
        check_vma=False,
    )
```

```python
import functools
import math

import jax
import jax.numpy as jnp
from jax import lax
from jax.experimental import pallas as pl
from jax.experimental.pallas import tpu as pltpu
from jax.sharding import Mesh
from jax.sharding import PartitionSpec as P

D = 2048
NZ, NY, NXH, NXL, NC = 8, 4, 2, 2, 2
PLANE = ("xl", "xh", "y")
OFFSETS = (0, 4, 2, -2, 1, 3, -1, -3)
GROUP = 128
EVERY = ("z", "y", "xh", "xl", "core")
ROWS = 128
HALF = 64
WIDTH = 512
NI = NY * NXH * ROWS
NJ = NZ * HALF
NP = NI // 2
LANES = 128
SCALE = 2.0 / math.sqrt(D)
VMEM = pl.BlockSpec(memory_space=pltpu.VMEM)
SMEM = pl.BlockSpec(memory_space=pltpu.SMEM)


def limit(mib):
    return pltpu.CompilerParams(vmem_limit_bytes=mib * 1024 * 1024)


def block_of(core, x, u):
    return jnp.where(core == 0, x * 8 + u, u % 4 * 4 + x * 2 + u // 4)


def arrange_kernel(place_ref, v1_ref, *o_refs):
    for x in range(NXL):
        for u in range(8):
            o_refs[x][u * ROWS : (u + 1) * ROWS, :] = v1_ref[block_of(place_ref[0], x, u)]


def arranged(place, v1_all):
    return pl.pallas_call(
        arrange_kernel,
        out_shape=(jax.ShapeDtypeStruct((NI, WIDTH), v1_all.dtype),) * NXL,
        in_specs=[SMEM, VMEM],
        out_specs=(VMEM,) * NXL,
        compiler_params=limit(5),
        cost_estimate=pl.CostEstimate(flops=0, bytes_accessed=2**22, transcendentals=0),
    )(place, v1_all)


def number_kernel(partner_ref, o_ref):
    o_ref[...] = partner_ref[...].astype(jnp.float32)


def numbers(partner):
    return pl.pallas_call(
        number_kernel,
        out_shape=jax.ShapeDtypeStruct((1, ROWS), jnp.float32),
        in_specs=[VMEM],
        out_specs=VMEM,
        compiler_params=limit(1),
        cost_estimate=pl.CostEstimate(flops=8 * 2**30, bytes_accessed=2**10, transcendentals=0),
    )(partner.reshape(1, ROWS))


def join_kernel(own, four0, four1, up2, down2, up, down, v2_ref, most_ref):
    v2_ref[:, :HALF, :] = own[...]
    v2_ref[0, HALF : 2 * HALF, :] = four0[...]
    v2_ref[1, HALF : 2 * HALF, :] = four1[...]
    v2_ref[:, 2 * HALF : 3 * HALF, :] = up2[...]
    v2_ref[:, 3 * HALF : 4 * HALF, :] = down2[...]
    v2_ref[:, 4 * HALF : 6 * HALF, :] = up[...]
    v2_ref[:, 6 * HALF :, :] = down[...]
    size = jnp.maximum(jnp.abs(v2_ref[0]), jnp.abs(v2_ref[1])).astype(jnp.float32)
    most_ref[...] = jnp.max(size, axis=0, keepdims=True)


def join(*parts):
    return pl.pallas_call(
        join_kernel,
        out_shape=(
            jax.ShapeDtypeStruct((NXL, NJ, WIDTH), jnp.bfloat16),
            jax.ShapeDtypeStruct((1, WIDTH), jnp.float32),
        ),
        in_specs=[VMEM] * 7,
        out_specs=(VMEM, VMEM),
        compiler_params=limit(4),
        cost_estimate=pl.CostEstimate(flops=10 * 2**30, bytes_accessed=2**21, transcendentals=0),
    )(*parts)


def score_kernel(part, place_ref, v1_ref, v2_ref, s_ref):
    users = range(part * (NP // ROWS), (part + 1) * (NP // ROWS))
    contract = (((1,), (1,)), ((), ()))
    s_ref[...] = sum(
        lax.dot_general(
            jnp.concatenate([v1_ref[block_of(place_ref[0], x, u)] for u in users]),
            v2_ref[x],
            contract,
            preferred_element_type=jnp.float32,
        )
        for x in range(NXL)
    )


def partial_scores(part, place, v1_all, v2_all):
    return pl.pallas_call(
        functools.partial(score_kernel, part),
        out_shape=jax.ShapeDtypeStruct((NP, NJ), jnp.float32),
        in_specs=[SMEM, VMEM, VMEM],
        out_specs=VMEM,
        compiler_params=limit(6),
        cost_estimate=pl.CostEstimate(
            flops=2 * NP * NJ * NXL * WIDTH, bytes_accessed=3 * 2**20, transcendentals=0
        ),
    )(place, v1_all, v2_all)


def diagonal():
    shape = (LANES, LANES)
    return lax.broadcasted_iota(jnp.int32, shape, 0) == lax.broadcasted_iota(jnp.int32, shape, 1)


def placed(z, k):
    plane = lax.rem(z + OFFSETS[k] + NZ, NZ)
    half = plane // 4
    return plane % 4, half, half != k % 2


def turned(row, trade):
    return jnp.where(trade, pltpu.roll(row, HALF, 1), row)


def lane_half():
    return lax.broadcasted_iota(jnp.int32, (1, LANES), 1) // HALF


def block_stats(own_ref, other_ref, s_ref, row_ref, col_highest, col_total):
    eye = diagonal()
    for u in range(NP // LANES):
        rows = slice(u * LANES, (u + 1) * LANES)
        s = SCALE * (own_ref[rows, :] + other_ref[rows, :])
        s_ref[rows, :] = s
        highest = jnp.max(s, axis=1, keepdims=True)
        lse = highest + jnp.log(jnp.sum(jnp.exp(s - highest), axis=1, keepdims=True))
        row_ref[u : u + 1, :] = jnp.sum(jnp.where(eye, lse, 0.0), axis=0, keepdims=True)
        higher = jnp.maximum(col_highest, jnp.max(s, axis=0, keepdims=True))
        col_total = col_total * jnp.exp(col_highest - higher) + jnp.sum(
            jnp.exp(s - higher), axis=0, keepdims=True
        )
        col_highest = higher
    return col_highest, col_total


def first_kernel(own_ref, other_ref, s_ref, row_ref, col_ref):
    highest, total = block_stats(
        own_ref,
        other_ref,
        s_ref,
        row_ref,
        jnp.full((1, NJ), -jnp.inf, jnp.float32),
        jnp.zeros((1, NJ), jnp.float32),
    )
    col_ref[0:1, :] = highest
    col_ref[1:2, :] = total


def first_stats(own, other):
    return pl.pallas_call(
        first_kernel,
        out_shape=(
            jax.ShapeDtypeStruct((NP, NJ), jnp.float32),
            jax.ShapeDtypeStruct((NP // LANES, LANES), jnp.float32),
            jax.ShapeDtypeStruct((2, NJ), jnp.float32),
        ),
        in_specs=[VMEM] * 2,
        out_specs=(VMEM,) * 3,
        compiler_params=limit(4),
        cost_estimate=pl.CostEstimate(
            flops=10 * NP * NJ, bytes_accessed=3 * 2**20, transcendentals=2 * NP * NJ
        ),
    )(own, other)


def second_kernel(
    place_ref,
    own_ref,
    other_ref,
    first_ref,
    col_ref,
    partner_ref,
    most_ref,
    most_other_ref,
    s_ref,
    out_ref,
    pack_ref,
):
    half = NP // LANES
    pack_ref[...] = jnp.zeros_like(pack_ref)
    pack_ref[0, 0:half, :] = first_ref[...]
    col_highest, col_total = block_stats(
        own_ref,
        other_ref,
        s_ref,
        pack_ref.at[0, half : 2 * half, :],
        col_ref[0:1, :],
        col_ref[1:2, :],
    )
    col_lse = col_highest + jnp.log(col_total)
    for k in range(NZ):
        row, half, trade = placed(place_ref[2], k)
        g = k // 2
        here = turned(col_lse[:, g * LANES : (g + 1) * LANES], trade)
        there = pack_ref[1, pl.ds(row, 1), :]
        pack_ref[1, pl.ds(row, 1), :] = jnp.where(lane_half() == half, here, there)
    most = jnp.max(jnp.maximum(most_ref[...], most_other_ref[...]), axis=1, keepdims=True)
    most = jnp.broadcast_to(jnp.maximum(most, 1e-30), (2, LANES))
    pack_ref[0, 8:9, :] = partner_ref[...]
    pack_ref[0, 9:10, :] = most[0:1, :]
    pack_ref[1, 9:10, :] = most[1:2, :]
    chosen = jnp.where(place_ref[0] == 0, pack_ref[0], pack_ref[1])
    for p in range(16):
        out_ref[p] = chosen


def second_stats(place, own, other, first, cols, partner, most, most_other):
    return pl.pallas_call(
        second_kernel,
        out_shape=(
            jax.ShapeDtypeStruct((NP, NJ), jnp.float32),
            jax.ShapeDtypeStruct((16, 16, LANES), jnp.float32),
        ),
        in_specs=[SMEM] + [VMEM] * 7,
        out_specs=(VMEM, VMEM),
        scratch_shapes=[pltpu.VMEM((2, 16, LANES), jnp.float32)],
        compiler_params=limit(4),
        cost_estimate=pl.CostEstimate(
            flops=10 * NP * NJ, bytes_accessed=3 * 2**20, transcendentals=2 * NP * NJ
        ),
    )(place, own, other, first, cols, partner, most, most_other)


def merged(lses):
    top = jnp.max(lses, axis=0)
    return top + jnp.log(jnp.sum(jnp.exp(lses - top[None]), axis=0))


def merge_kernel(place_ref, seen_ref, known_ref, cols_ref):
    core, xl = place_ref[0], place_ref[1]

    @pl.when(core == 0)
    def _():
        known_ref[0:8, :] = merged(seen_ref[:, 0:8, :])
        for u in range(8):
            known_ref[8 + u : 9 + u, :] = seen_ref[u, 8:9, :]

    @pl.when(core != 0)
    def _():
        known_ref[...] = jnp.zeros_like(known_ref)
        cols_ref[...] = merged(seen_ref[pl.ds(xl * NZ, NZ), 0:8, :])
        for g in range(4):
            row0, _, trade0 = placed(place_ref[2], 2 * g)
            row1, _, trade1 = placed(place_ref[2], 2 * g + 1)
            known_ref[g : g + 1, :] = jnp.where(
                lane_half() == 0,
                turned(cols_ref[pl.ds(row0, 1), :], trade0),
                turned(cols_ref[pl.ds(row1, 1), :], trade1),
            )

    known_ref[16:24, :] = jnp.broadcast_to(jnp.max(seen_ref[:, 9:10, :], axis=0), (8, LANES))


def merge_stats(place, seen):
    return pl.pallas_call(
        merge_kernel,
        out_shape=jax.ShapeDtypeStruct((24, LANES), jnp.float32),
        in_specs=[SMEM, VMEM],
        out_specs=VMEM,
        scratch_shapes=[pltpu.VMEM((8, LANES), jnp.float32)],
        compiler_params=limit(2),
        cost_estimate=pl.CostEstimate(flops=10**5, bytes_accessed=2**17, transcendentals=2**14),
    )(place, seen)


def couple_kernel(
    place_ref,
    s0_ref,
    s1_ref,
    known_ref,
    told_ref,
    c_ref,
    give_one_ref,
    give_two_ref,
    take_one_ref,
    take_two_ref,
):
    core, xl, z, uhigh = place_ref[0], place_ref[1], place_ref[2], place_ref[3]
    rows = jnp.where(core == 0, known_ref[...], told_ref[...])
    cols = jnp.where(core == 0, told_ref[...], known_ref[...])
    eye = diagonal()
    lane = lax.broadcasted_iota(jnp.int32, (1, LANES), 1)
    index, col_lse = [], []
    for g in range(4):
        first = lax.rem(z + OFFSETS[2 * g] + NZ, NZ)
        second = lax.rem(z + OFFSETS[2 * g + 1] + NZ, NZ)
        user = jnp.where(lane < HALF, first, second) * (NY * NXH) + uhigh
        inside = jnp.where(lane < HALF, lane, lane - HALF)
        index.append((user * ROWS + xl * HALF + inside).astype(jnp.float32))
        col_lse.append(cols[g : g + 1, :])
    index = jnp.concatenate(index, axis=1)
    col_lse = jnp.concatenate(col_lse, axis=1)
    for u in range(NI // LANES):
        here = slice(u * LANES, (u + 1) * LANES)
        half_ref = s0_ref if u < NP // LANES else s1_ref
        start = u * LANES % NP
        s = half_ref[start : start + LANES, :]
        row_lse = jnp.sum(jnp.where(eye, rows[u : u + 1, :], 0.0), axis=1, keepdims=True)
        partner = jnp.sum(jnp.where(eye, rows[8 + u : 9 + u, :], 0.0), axis=1, keepdims=True)
        both = jnp.exp(s - row_lse) + jnp.exp(s - col_lse)
        positive = (partner == index).astype(jnp.float32)
        c_ref[here, :] = (0.5 * both - positive).astype(jnp.bfloat16)
    most_two = jnp.concatenate([rows[16:17, :]] * 4, axis=1)
    most_one = jnp.concatenate([cols[16:17, :]] * 4, axis=1)
    give_one_ref[...] = 128.0 / most_two
    take_one_ref[...] = most_two / 128.0
    give_two_ref[...] = 64.0 / most_one
    take_two_ref[...] = most_one / 64.0


def coupling_of(place, scores0, scores1, known, told):
    return pl.pallas_call(
        couple_kernel,
        out_shape=(
            jax.ShapeDtypeStruct((NI, NJ), jnp.bfloat16),
        )
        + (jax.ShapeDtypeStruct((1, WIDTH), jnp.float32),) * 4,
        in_specs=[SMEM] + [VMEM] * 4,
        out_specs=(VMEM,) * 5,
        compiler_params=limit(5),
        cost_estimate=pl.CostEstimate(
            flops=8 * NI * NJ, bytes_accessed=3 * 2**20, transcendentals=2 * NI * NJ
        ),
    )(place, scores0, scores1, known, told)


def swap(x, axis):
    return lax.ppermute(x, axis, [(0, 1), (1, 0)])


def number(z, y, xh, xl, c):
    return (((z * NY + y) * NXH + xh) * NXL + xl) * NC + c


def line_groups(turn):
    alongs_y = [
        [number(z, y, xh, xl, turn) for y in range(NY)]
        for z in range(NZ)
        for xl in range(NXL)
        for xh in range(NXH)
    ]
    alongs_x = [
        [number(z, y, xh, xl, 1 - turn) for xl in range(NXL) for xh in range(NXH)]
        for z in range(NZ)
        for y in range(NY)
    ]
    return alongs_y + alongs_x


def spread(x, turn):
    return lax.all_to_all(
        jnp.broadcast_to(x[None], (4,) + x.shape),
        EVERY,
        0,
        0,
        axis_index_groups=line_groups(turn),
        tiled=True,
    )


def stat_groups():
    planes = [
        [number(z, y, xh, xl, 0) for xl in range(NXL) for xh in range(NXH) for y in range(NY)]
        for z in range(NZ)
    ]
    columns = [
        [number(z, y, xh, xl, 1) for xl in range(NXL) for z in range(NZ)]
        for y in range(NY)
        for xh in range(NXH)
    ]
    return planes + columns


def to_plane(x, dz):
    return lax.ppermute(x, "z", [(z, (z + dz) % NZ) for z in range(NZ)])


def largest(x):
    return jnp.max(jnp.abs(x), axis=(0, 1)).astype(jnp.float32)


def on_device(view_one, view_two, partner):
    z = lax.axis_index("z")
    uhigh = lax.axis_index("y") * NXH + lax.axis_index("xh")
    xl = lax.axis_index("xl")
    core = lax.axis_index("core")
    place = jnp.stack([core, xl, z, uhigh]).astype(jnp.int32)

    side = swap(view_two, "xl")
    lines = spread(view_one, 0)
    partner = numbers(partner)
    side, partner = lax.optimization_barrier((side, partner))
    lines, _ = lax.optimization_barrier((lines, side))
    here = jnp.where(
        xl == 0,
        jnp.stack([view_two[:HALF], side[:HALF]]),
        jnp.stack([side[HALF:], view_two[HALF:]]),
    )
    up2, down2 = to_plane(here, -2), to_plane(here, 2)
    v1_all = spread(lines, 1).reshape(16, ROWS, WIDTH)
    up = to_plane(jnp.concatenate([here, up2], axis=1), -1)
    down = to_plane(jnp.concatenate([here, down2], axis=1), 1)
    v2_all, most_v2 = join(
        here, to_plane(up2[0], -2), to_plane(down2[1], 2), up2, down2, up, down
    )

    own0 = partial_scores(0, place, v1_all, v2_all)
    other0 = swap(own0, "core")
    own1 = partial_scores(1, place, v1_all, v2_all)
    other1 = swap(own1, "core")
    most = jnp.concatenate([most_v2, largest(v1_all)[None]])
    most_other = swap(most, "core")

    scores0, first, cols = first_stats(own0, other0)
    scores1, pack = second_stats(place, own1, other1, first, cols, partner, most, most_other)
    seen = lax.all_to_all(
        pack, EVERY, 0, 0, axis_index_groups=stat_groups(), tiled=True
    )
    v1_rows = arranged(place, v1_all)
    known = merge_stats(place, seen)
    coupling, give_one, give_two, take_one, take_two = coupling_of(
        place, scores0, scores1, known, swap(known, "core")
    )

    part_one = (
        lax.dot_general(
            jnp.broadcast_to(coupling[None], (NXL, NI, NJ)),
            v2_all,
            (((2,), (1,)), ((0,), (0,))),
            preferred_element_type=jnp.float32,
        )
        * give_one
    ).astype(jnp.float16)
    coupling, part_one = lax.optimization_barrier((coupling, part_one))
    one_parts = lax.all_to_all(part_one.reshape(16, ROWS, WIDTH), PLANE, 0, 0, tiled=True)
    part_two = [
        (
            lax.dot_general(
                coupling, v1_rows[x], (((0,), (0,)), ((), ())), preferred_element_type=jnp.float32
            )
            * give_two
        ).astype(jnp.float16)
        for x in range(NXL)
    ]

    def blocks(start, stop):
        return jnp.stack([part[start * HALF : stop * HALF] for part in part_two])

    from_below, from_above = to_plane(blocks(4, 6), 1), to_plane(blocks(6, 8), -1)
    four0 = to_plane(part_two[0][HALF : 2 * HALF], 2)
    four1 = to_plane(part_two[1][HALF : 2 * HALF], -2)
    wide = [x.astype(jnp.float32) for x in (from_below, from_above, four0, four1)]
    up2 = blocks(2, 3).astype(jnp.float32) + wide[0][:, HALF:]
    up2 = jnp.stack([up2[0] + wide[2], up2[1]])
    down2 = blocks(3, 4).astype(jnp.float32) + wide[1][:, HALF:]
    down2 = jnp.stack([down2[0], down2[1] + wide[3]])
    from_up = to_plane((up2 * 0.25).astype(jnp.float16), 2)
    from_down = to_plane((down2 * 0.25).astype(jnp.float16), -2)
    total = blocks(0, 1).astype(jnp.float32) + wide[0][:, :HALF] + wide[1][:, :HALF]
    total = total + 4.0 * (from_up.astype(jnp.float32) + from_down.astype(jnp.float32))
    total = total * take_two
    stay = jnp.where(xl == 0, total[0], total[1])
    come = swap(jnp.where(xl == 0, total[1], total[0]), "xl")
    grad_one = jnp.sum(one_parts.astype(jnp.float32) * take_one, axis=0)
    come, grad_one = lax.optimization_barrier((come, grad_one))
    grad_two = jnp.where(
        xl == 0, jnp.concatenate([stay, come]), jnp.concatenate([come, stay])
    )
    return (grad_one, grad_two)


def solution(mesh):
    fine = Mesh(mesh.devices.reshape(NZ, NY, NXH, NXL, NC), EVERY)
    users = P(("z", "y", "xh"))
    both = P(("z", "y", "xh"), ("xl", "core"))
    return jax.shard_map(
        on_device,
        mesh=fine,
        in_specs=(both, both, users),
        out_specs=(both, both),
        check_vma=False,
    )
```

```python
import functools
import math

import jax
import jax.numpy as jnp
from jax import lax
from jax.experimental import pallas as pl
from jax.experimental.pallas import tpu as pltpu
from jax.sharding import Mesh
from jax.sharding import PartitionSpec as P

D = 2048
NZ, NY, NXH, NXL, NC = 8, 4, 2, 2, 2
PLANE = ("xl", "xh", "y")
OFFSETS = (0, 4, 2, -2, 1, 3, -1, -3)
GROUP = 128
EVERY = ("z", "y", "xh", "xl", "core")
ROWS = 128
HALF = 64
WIDTH = 512
NI = NY * NXH * ROWS
NJ = NZ * HALF
NP = NI // 2
LANES = 128
SCALE = 2.0 / math.sqrt(D)
VMEM = pl.BlockSpec(memory_space=pltpu.VMEM)
SMEM = pl.BlockSpec(memory_space=pltpu.SMEM)


def limit(mib):
    return pltpu.CompilerParams(vmem_limit_bytes=mib * 1024 * 1024)


def block_of(core, x, u):
    return jnp.where(core == 0, x * 8 + u, u % 4 * 4 + x * 2 + u // 4)


def arrange_kernel(place_ref, v1_ref, *o_refs):
    for x in range(NXL):
        for u in range(8):
            o_refs[x][u * ROWS : (u + 1) * ROWS, :] = v1_ref[block_of(place_ref[0], x, u)]


def arranged(place, v1_all):
    return pl.pallas_call(
        arrange_kernel,
        out_shape=(jax.ShapeDtypeStruct((NI, WIDTH), v1_all.dtype),) * NXL,
        in_specs=[SMEM, VMEM],
        out_specs=(VMEM,) * NXL,
        compiler_params=limit(5),
        cost_estimate=pl.CostEstimate(flops=0, bytes_accessed=2**22, transcendentals=0),
    )(place, v1_all)


def number_kernel(partner_ref, o_ref):
    o_ref[...] = partner_ref[...].astype(jnp.float32)


def numbers(partner):
    return pl.pallas_call(
        number_kernel,
        out_shape=jax.ShapeDtypeStruct((1, ROWS), jnp.float32),
        in_specs=[VMEM],
        out_specs=VMEM,
        compiler_params=limit(1),
        cost_estimate=pl.CostEstimate(flops=8 * 2**30, bytes_accessed=2**10, transcendentals=0),
    )(partner.reshape(1, ROWS))


def four_kernel(x_ref, o_ref):
    for p in range(4):
        o_ref[p] = x_ref[...]


def four_copies(x):
    return pl.pallas_call(
        four_kernel,
        out_shape=jax.ShapeDtypeStruct((4,) + x.shape, x.dtype),
        in_specs=[VMEM],
        out_specs=VMEM,
        compiler_params=limit(2),
        cost_estimate=pl.CostEstimate(flops=0, bytes_accessed=2**19, transcendentals=0),
    )(x)


def join_kernel(own, four0, four1, up2, down2, up, down, v2_ref, most_ref):
    v2_ref[:, :HALF, :] = own[...]
    v2_ref[0, HALF : 2 * HALF, :] = four0[...]
    v2_ref[1, HALF : 2 * HALF, :] = four1[...]
    v2_ref[:, 2 * HALF : 3 * HALF, :] = up2[...]
    v2_ref[:, 3 * HALF : 4 * HALF, :] = down2[...]
    v2_ref[:, 4 * HALF : 6 * HALF, :] = up[...]
    v2_ref[:, 6 * HALF :, :] = down[...]
    size = jnp.maximum(jnp.abs(v2_ref[0]), jnp.abs(v2_ref[1])).astype(jnp.float32)
    most_ref[...] = jnp.max(size, axis=0, keepdims=True)


def join(*parts):
    return pl.pallas_call(
        join_kernel,
        out_shape=(
            jax.ShapeDtypeStruct((NXL, NJ, WIDTH), jnp.bfloat16),
            jax.ShapeDtypeStruct((1, WIDTH), jnp.float32),
        ),
        in_specs=[VMEM] * 7,
        out_specs=(VMEM, VMEM),
        compiler_params=limit(4),
        cost_estimate=pl.CostEstimate(flops=10 * 2**30, bytes_accessed=2**21, transcendentals=0),
    )(*parts)


def score_kernel(part, place_ref, v1_ref, v2_ref, s_ref):
    users = range(part * (NP // ROWS), (part + 1) * (NP // ROWS))
    contract = (((1,), (1,)), ((), ()))
    s_ref[...] = sum(
        lax.dot_general(
            jnp.concatenate([v1_ref[block_of(place_ref[0], x, u)] for u in users]),
            v2_ref[x],
            contract,
            preferred_element_type=jnp.float32,
        )
        for x in range(NXL)
    )


def partial_scores(part, place, v1_all, v2_all):
    return pl.pallas_call(
        functools.partial(score_kernel, part),
        out_shape=jax.ShapeDtypeStruct((NP, NJ), jnp.float32),
        in_specs=[SMEM, VMEM, VMEM],
        out_specs=VMEM,
        compiler_params=limit(6),
        cost_estimate=pl.CostEstimate(
            flops=2 * NP * NJ * NXL * WIDTH, bytes_accessed=3 * 2**20, transcendentals=0
        ),
    )(place, v1_all, v2_all)


def diagonal():
    shape = (LANES, LANES)
    return lax.broadcasted_iota(jnp.int32, shape, 0) == lax.broadcasted_iota(jnp.int32, shape, 1)


def placed(z, k):
    plane = lax.rem(z + OFFSETS[k] + NZ, NZ)
    half = plane // 4
    return plane % 4, half, half != k % 2


def turned(row, trade):
    return jnp.where(trade, pltpu.roll(row, HALF, 1), row)


def lane_half():
    return lax.broadcasted_iota(jnp.int32, (1, LANES), 1) // HALF


def block_stats(own_ref, other_ref, s_ref, row_ref, col_highest, col_total):
    eye = diagonal()
    for u in range(NP // LANES):
        rows = slice(u * LANES, (u + 1) * LANES)
        s = SCALE * (own_ref[rows, :] + other_ref[rows, :])
        s_ref[rows, :] = s
        highest = jnp.max(s, axis=1, keepdims=True)
        lse = highest + jnp.log(jnp.sum(jnp.exp(s - highest), axis=1, keepdims=True))
        row_ref[u : u + 1, :] = jnp.sum(jnp.where(eye, lse, 0.0), axis=0, keepdims=True)
        higher = jnp.maximum(col_highest, jnp.max(s, axis=0, keepdims=True))
        col_total = col_total * jnp.exp(col_highest - higher) + jnp.sum(
            jnp.exp(s - higher), axis=0, keepdims=True
        )
        col_highest = higher
    return col_highest, col_total


def first_kernel(own_ref, other_ref, s_ref, row_ref, col_ref):
    highest, total = block_stats(
        own_ref,
        other_ref,
        s_ref,
        row_ref,
        jnp.full((1, NJ), -jnp.inf, jnp.float32),
        jnp.zeros((1, NJ), jnp.float32),
    )
    col_ref[0:1, :] = highest
    col_ref[1:2, :] = total


def first_stats(own, other):
    return pl.pallas_call(
        first_kernel,
        out_shape=(
            jax.ShapeDtypeStruct((NP, NJ), jnp.float32),
            jax.ShapeDtypeStruct((NP // LANES, LANES), jnp.float32),
            jax.ShapeDtypeStruct((2, NJ), jnp.float32),
        ),
        in_specs=[VMEM] * 2,
        out_specs=(VMEM,) * 3,
        compiler_params=limit(4),
        cost_estimate=pl.CostEstimate(
            flops=10 * NP * NJ, bytes_accessed=3 * 2**20, transcendentals=2 * NP * NJ
        ),
    )(own, other)


def second_kernel(
    place_ref,
    own_ref,
    other_ref,
    first_ref,
    col_ref,
    partner_ref,
    most_ref,
    most_other_ref,
    s_ref,
    out_ref,
    pack_ref,
):
    half = NP // LANES
    pack_ref[...] = jnp.zeros_like(pack_ref)
    pack_ref[0, 0:half, :] = first_ref[...]
    col_highest, col_total = block_stats(
        own_ref,
        other_ref,
        s_ref,
        pack_ref.at[0, half : 2 * half, :],
        col_ref[0:1, :],
        col_ref[1:2, :],
    )
    col_lse = col_highest + jnp.log(col_total)
    for k in range(NZ):
        row, half, trade = placed(place_ref[2], k)
        g = k // 2
        here = turned(col_lse[:, g * LANES : (g + 1) * LANES], trade)
        there = pack_ref[1, pl.ds(row, 1), :]
        pack_ref[1, pl.ds(row, 1), :] = jnp.where(lane_half() == half, here, there)
    most = jnp.max(jnp.maximum(most_ref[...], most_other_ref[...]), axis=1, keepdims=True)
    most = jnp.broadcast_to(jnp.maximum(most, 1e-30), (2, LANES))
    pack_ref[0, 8:9, :] = partner_ref[...]
    pack_ref[0, 9:10, :] = most[0:1, :]
    pack_ref[1, 9:10, :] = most[1:2, :]
    chosen = jnp.where(place_ref[0] == 0, pack_ref[0], pack_ref[1])
    for p in range(16):
        out_ref[p] = chosen


def second_stats(place, own, other, first, cols, partner, most, most_other):
    return pl.pallas_call(
        second_kernel,
        out_shape=(
            jax.ShapeDtypeStruct((NP, NJ), jnp.float32),
            jax.ShapeDtypeStruct((16, 16, LANES), jnp.float32),
        ),
        in_specs=[SMEM] + [VMEM] * 7,
        out_specs=(VMEM, VMEM),
        scratch_shapes=[pltpu.VMEM((2, 16, LANES), jnp.float32)],
        compiler_params=limit(4),
        cost_estimate=pl.CostEstimate(
            flops=10 * NP * NJ, bytes_accessed=3 * 2**20, transcendentals=2 * NP * NJ
        ),
    )(place, own, other, first, cols, partner, most, most_other)


def merged(lses):
    top = jnp.max(lses, axis=0)
    return top + jnp.log(jnp.sum(jnp.exp(lses - top[None]), axis=0))


def merge_kernel(place_ref, seen_ref, known_ref, cols_ref):
    core, xl = place_ref[0], place_ref[1]

    @pl.when(core == 0)
    def _():
        known_ref[0:8, :] = merged(seen_ref[:, 0:8, :])
        for u in range(8):
            known_ref[8 + u : 9 + u, :] = seen_ref[u, 8:9, :]

    @pl.when(core != 0)
    def _():
        known_ref[...] = jnp.zeros_like(known_ref)
        cols_ref[...] = merged(seen_ref[pl.ds(xl * NZ, NZ), 0:8, :])
        for g in range(4):
            row0, _, trade0 = placed(place_ref[2], 2 * g)
            row1, _, trade1 = placed(place_ref[2], 2 * g + 1)
            known_ref[g : g + 1, :] = jnp.where(
                lane_half() == 0,
                turned(cols_ref[pl.ds(row0, 1), :], trade0),
                turned(cols_ref[pl.ds(row1, 1), :], trade1),
            )

    known_ref[16:24, :] = jnp.broadcast_to(jnp.max(seen_ref[:, 9:10, :], axis=0), (8, LANES))


def merge_stats(place, seen):
    return pl.pallas_call(
        merge_kernel,
        out_shape=jax.ShapeDtypeStruct((24, LANES), jnp.float32),
        in_specs=[SMEM, VMEM],
        out_specs=VMEM,
        scratch_shapes=[pltpu.VMEM((8, LANES), jnp.float32)],
        compiler_params=limit(2),
        cost_estimate=pl.CostEstimate(flops=10**5, bytes_accessed=2**17, transcendentals=2**14),
    )(place, seen)


def couple_kernel(
    place_ref,
    s0_ref,
    s1_ref,
    known_ref,
    told_ref,
    c_ref,
    give_one_ref,
    give_two_ref,
    take_one_ref,
    take_two_ref,
):
    core, xl, z, uhigh = place_ref[0], place_ref[1], place_ref[2], place_ref[3]
    rows = jnp.where(core == 0, known_ref[...], told_ref[...])
    cols = jnp.where(core == 0, told_ref[...], known_ref[...])
    eye = diagonal()
    lane = lax.broadcasted_iota(jnp.int32, (1, LANES), 1)
    index, col_lse = [], []
    for g in range(4):
        first = lax.rem(z + OFFSETS[2 * g] + NZ, NZ)
        second = lax.rem(z + OFFSETS[2 * g + 1] + NZ, NZ)
        user = jnp.where(lane < HALF, first, second) * (NY * NXH) + uhigh
        inside = jnp.where(lane < HALF, lane, lane - HALF)
        index.append((user * ROWS + xl * HALF + inside).astype(jnp.float32))
        col_lse.append(cols[g : g + 1, :])
    index = jnp.concatenate(index, axis=1)
    col_lse = jnp.concatenate(col_lse, axis=1)
    for u in range(NI // LANES):
        here = slice(u * LANES, (u + 1) * LANES)
        half_ref = s0_ref if u < NP // LANES else s1_ref
        start = u * LANES % NP
        s = half_ref[start : start + LANES, :]
        row_lse = jnp.sum(jnp.where(eye, rows[u : u + 1, :], 0.0), axis=1, keepdims=True)
        partner = jnp.sum(jnp.where(eye, rows[8 + u : 9 + u, :], 0.0), axis=1, keepdims=True)
        both = jnp.exp(s - row_lse) + jnp.exp(s - col_lse)
        positive = (partner == index).astype(jnp.float32)
        c_ref[here, :] = (0.5 * both - positive).astype(jnp.bfloat16)
    most_two = jnp.concatenate([rows[16:17, :]] * 4, axis=1)
    most_one = jnp.concatenate([cols[16:17, :]] * 4, axis=1)
    give_one_ref[...] = 128.0 / most_two
    take_one_ref[...] = most_two / 128.0
    give_two_ref[...] = 64.0 / most_one
    take_two_ref[...] = most_one / 64.0


def coupling_of(place, scores0, scores1, known, told):
    return pl.pallas_call(
        couple_kernel,
        out_shape=(
            jax.ShapeDtypeStruct((NI, NJ), jnp.bfloat16),
        )
        + (jax.ShapeDtypeStruct((1, WIDTH), jnp.float32),) * 4,
        in_specs=[SMEM] + [VMEM] * 4,
        out_specs=(VMEM,) * 5,
        compiler_params=limit(5),
        cost_estimate=pl.CostEstimate(
            flops=8 * NI * NJ, bytes_accessed=3 * 2**20, transcendentals=2 * NI * NJ
        ),
    )(place, scores0, scores1, known, told)


def swap(x, axis):
    return lax.ppermute(x, axis, [(0, 1), (1, 0)])


def number(z, y, xh, xl, c):
    return (((z * NY + y) * NXH + xh) * NXL + xl) * NC + c


def line_groups(turn):
    alongs_y = [
        [number(z, y, xh, xl, turn) for y in range(NY)]
        for z in range(NZ)
        for xl in range(NXL)
        for xh in range(NXH)
    ]
    alongs_x = [
        [number(z, y, xh, xl, 1 - turn) for xl in range(NXL) for xh in range(NXH)]
        for z in range(NZ)
        for y in range(NY)
    ]
    return alongs_y + alongs_x


def spread(copies, turn):
    return lax.all_to_all(
        copies,
        EVERY,
        0,
        0,
        axis_index_groups=line_groups(turn),
        tiled=True,
    )


def stat_groups():
    planes = [
        [number(z, y, xh, xl, 0) for xl in range(NXL) for xh in range(NXH) for y in range(NY)]
        for z in range(NZ)
    ]
    columns = [
        [number(z, y, xh, xl, 1) for xl in range(NXL) for z in range(NZ)]
        for y in range(NY)
        for xh in range(NXH)
    ]
    return planes + columns


def to_plane(x, dz):
    return lax.ppermute(x, "z", [(z, (z + dz) % NZ) for z in range(NZ)])


def largest(x):
    return jnp.max(jnp.abs(x), axis=(0, 1)).astype(jnp.float32)


def on_device(view_one, view_two, partner):
    z = lax.axis_index("z")
    uhigh = lax.axis_index("y") * NXH + lax.axis_index("xh")
    xl = lax.axis_index("xl")
    core = lax.axis_index("core")
    place = jnp.stack([core, xl, z, uhigh]).astype(jnp.int32)

    side = swap(view_two, "xl")
    lines = spread(four_copies(view_one), 0)
    partner = numbers(partner)
    side, partner = lax.optimization_barrier((side, partner))
    lines, _ = lax.optimization_barrier((lines, side))
    here = jnp.where(
        xl == 0,
        jnp.stack([view_two[:HALF], side[:HALF]]),
        jnp.stack([side[HALF:], view_two[HALF:]]),
    )
    up2, down2 = to_plane(here, -2), to_plane(here, 2)
    v1_all = spread(jnp.broadcast_to(lines[None], (4,) + lines.shape), 1).reshape(16, ROWS, WIDTH)
    up = to_plane(jnp.concatenate([here, up2], axis=1), -1)
    down = to_plane(jnp.concatenate([here, down2], axis=1), 1)
    v2_all, most_v2 = join(
        here, to_plane(up2[0], -2), to_plane(down2[1], 2), up2, down2, up, down
    )

    own0 = partial_scores(0, place, v1_all, v2_all)
    other0 = swap(own0, "core")
    own1 = partial_scores(1, place, v1_all, v2_all)
    other1 = swap(own1, "core")
    most = jnp.concatenate([most_v2, largest(v1_all)[None]])
    most_other = swap(most, "core")

    scores0, first, cols = first_stats(own0, other0)
    scores1, pack = second_stats(place, own1, other1, first, cols, partner, most, most_other)
    seen = lax.all_to_all(
        pack, EVERY, 0, 0, axis_index_groups=stat_groups(), tiled=True
    )
    v1_rows = arranged(place, v1_all)
    known = merge_stats(place, seen)
    coupling, give_one, give_two, take_one, take_two = coupling_of(
        place, scores0, scores1, known, swap(known, "core")
    )

    part_one = (
        lax.dot_general(
            jnp.broadcast_to(coupling[None], (NXL, NI, NJ)),
            v2_all,
            (((2,), (1,)), ((0,), (0,))),
            preferred_element_type=jnp.float32,
        )
        * give_one
    ).astype(jnp.float16)
    coupling, part_one = lax.optimization_barrier((coupling, part_one))
    one_parts = lax.all_to_all(part_one.reshape(16, ROWS, WIDTH), PLANE, 0, 0, tiled=True)
    part_two = [
        (
            lax.dot_general(
                coupling, v1_rows[x], (((0,), (0,)), ((), ())), preferred_element_type=jnp.float32
            )
            * give_two
        ).astype(jnp.float16)
        for x in range(NXL)
    ]

    def blocks(start, stop):
        return jnp.stack([part[start * HALF : stop * HALF] for part in part_two])

    from_below, from_above = to_plane(blocks(4, 6), 1), to_plane(blocks(6, 8), -1)
    four0 = to_plane(part_two[0][HALF : 2 * HALF], 2)
    four1 = to_plane(part_two[1][HALF : 2 * HALF], -2)
    wide = [x.astype(jnp.float32) for x in (from_below, from_above, four0, four1)]
    up2 = blocks(2, 3).astype(jnp.float32) + wide[0][:, HALF:]
    up2 = jnp.stack([up2[0] + wide[2], up2[1]])
    down2 = blocks(3, 4).astype(jnp.float32) + wide[1][:, HALF:]
    down2 = jnp.stack([down2[0], down2[1] + wide[3]])
    from_up = to_plane((up2 * 0.25).astype(jnp.float16), 2)
    from_down = to_plane((down2 * 0.25).astype(jnp.float16), -2)
    total = blocks(0, 1).astype(jnp.float32) + wide[0][:, :HALF] + wide[1][:, :HALF]
    total = total + 4.0 * (from_up.astype(jnp.float32) + from_down.astype(jnp.float32))
    total = total * take_two
    stay = jnp.where(xl == 0, total[0], total[1])
    come = swap(jnp.where(xl == 0, total[1], total[0]), "xl")
    grad_one = jnp.sum(one_parts.astype(jnp.float32) * take_one, axis=0)
    come, grad_one = lax.optimization_barrier((come, grad_one))
    grad_two = jnp.where(
        xl == 0, jnp.concatenate([stay, come]), jnp.concatenate([come, stay])
    )
    return (grad_one, grad_two)


def solution(mesh):
    fine = Mesh(mesh.devices.reshape(NZ, NY, NXH, NXL, NC), EVERY)
    users = P(("z", "y", "xh"))
    both = P(("z", "y", "xh"), ("xl", "core"))
    return jax.shard_map(
        on_device,
        mesh=fine,
        in_specs=(both, both, users),
        out_specs=(both, both),
        check_vma=False,
    )
```

```python
import functools
import math

import jax
import jax.numpy as jnp
from jax import lax
from jax.experimental import pallas as pl
from jax.experimental.pallas import tpu as pltpu
from jax.sharding import Mesh
from jax.sharding import PartitionSpec as P

D = 2048
NZ, NY, NXH, NXL, NC = 8, 4, 2, 2, 2
PLANE = ("xl", "xh", "y")
OFFSETS = (0, 4, 2, -2, 1, 3, -1, -3)
GROUP = 128
EVERY = ("z", "y", "xh", "xl", "core")
ROWS = 128
HALF = 64
WIDTH = 512
NI = NY * NXH * ROWS
NJ = NZ * HALF
NP = NI // 2
LANES = 128
SCALE = 2.0 / math.sqrt(D)
VMEM = pl.BlockSpec(memory_space=pltpu.VMEM)
SMEM = pl.BlockSpec(memory_space=pltpu.SMEM)


def limit(mib):
    return pltpu.CompilerParams(vmem_limit_bytes=mib * 1024 * 1024)


def block_of(core, x, u):
    return jnp.where(core == 0, x * 8 + u, u % 4 * 4 + x * 2 + u // 4)


def arrange_kernel(place_ref, v1_ref, *o_refs):
    for x in range(NXL):
        for u in range(8):
            o_refs[x][u * ROWS : (u + 1) * ROWS, :] = v1_ref[block_of(place_ref[0], x, u)]


def arranged(place, v1_all):
    return pl.pallas_call(
        arrange_kernel,
        out_shape=(jax.ShapeDtypeStruct((NI, WIDTH), v1_all.dtype),) * NXL,
        in_specs=[SMEM, VMEM],
        out_specs=(VMEM,) * NXL,
        compiler_params=limit(5),
        cost_estimate=pl.CostEstimate(flops=0, bytes_accessed=2**22, transcendentals=0),
    )(place, v1_all)


def number_kernel(partner_ref, o_ref):
    o_ref[...] = partner_ref[...].astype(jnp.float32)


def numbers(partner):
    return pl.pallas_call(
        number_kernel,
        out_shape=jax.ShapeDtypeStruct((1, ROWS), jnp.float32),
        in_specs=[VMEM],
        out_specs=VMEM,
        compiler_params=limit(1),
        cost_estimate=pl.CostEstimate(flops=8 * 2**30, bytes_accessed=2**10, transcendentals=0),
    )(partner.reshape(1, ROWS))


def join_kernel(own, four0, four1, up2, down2, up, down, v2_ref, most_ref):
    v2_ref[:, :HALF, :] = own[...]
    v2_ref[0, HALF : 2 * HALF, :] = four0[...]
    v2_ref[1, HALF : 2 * HALF, :] = four1[...]
    v2_ref[:, 2 * HALF : 3 * HALF, :] = up2[...]
    v2_ref[:, 3 * HALF : 4 * HALF, :] = down2[...]
    v2_ref[:, 4 * HALF : 6 * HALF, :] = up[...]
    v2_ref[:, 6 * HALF :, :] = down[...]
    size = jnp.maximum(jnp.abs(v2_ref[0]), jnp.abs(v2_ref[1])).astype(jnp.float32)
    most_ref[...] = jnp.max(size, axis=0, keepdims=True)


def join(*parts):
    return pl.pallas_call(
        join_kernel,
        out_shape=(
            jax.ShapeDtypeStruct((NXL, NJ, WIDTH), jnp.bfloat16),
            jax.ShapeDtypeStruct((1, WIDTH), jnp.float32),
        ),
        in_specs=[VMEM] * 7,
        out_specs=(VMEM, VMEM),
        compiler_params=limit(4),
        cost_estimate=pl.CostEstimate(flops=10 * 2**30, bytes_accessed=2**21, transcendentals=0),
    )(*parts)


def score_kernel(part, place_ref, v1_ref, v2_ref, s_ref):
    users = range(part * (NP // ROWS), (part + 1) * (NP // ROWS))
    contract = (((1,), (1,)), ((), ()))
    s_ref[...] = sum(
        lax.dot_general(
            jnp.concatenate([v1_ref[block_of(place_ref[0], x, u)] for u in users]),
            v2_ref[x],
            contract,
            preferred_element_type=jnp.float32,
        )
        for x in range(NXL)
    )


def partial_scores(part, place, v1_all, v2_all):
    return pl.pallas_call(
        functools.partial(score_kernel, part),
        out_shape=jax.ShapeDtypeStruct((NP, NJ), jnp.float32),
        in_specs=[SMEM, VMEM, VMEM],
        out_specs=VMEM,
        compiler_params=limit(6),
        cost_estimate=pl.CostEstimate(
            flops=2 * NP * NJ * NXL * WIDTH, bytes_accessed=3 * 2**20, transcendentals=0
        ),
    )(place, v1_all, v2_all)


def diagonal():
    shape = (LANES, LANES)
    return lax.broadcasted_iota(jnp.int32, shape, 0) == lax.broadcasted_iota(jnp.int32, shape, 1)


def placed(z, k):
    plane = lax.rem(z + OFFSETS[k] + NZ, NZ)
    half = plane // 4
    return plane % 4, half, half != k % 2


def turned(row, trade):
    return jnp.where(trade, pltpu.roll(row, HALF, 1), row)


def lane_half():
    return lax.broadcasted_iota(jnp.int32, (1, LANES), 1) // HALF


def block_stats(own_ref, other_ref, s_ref, row_ref, col_highest, col_total):
    eye = diagonal()
    for u in range(NP // LANES):
        rows = slice(u * LANES, (u + 1) * LANES)
        s = SCALE * (own_ref[rows, :] + other_ref[rows, :])
        s_ref[rows, :] = s
        highest = jnp.max(s, axis=1, keepdims=True)
        lse = highest + jnp.log(jnp.sum(jnp.exp(s - highest), axis=1, keepdims=True))
        row_ref[u : u + 1, :] = jnp.sum(jnp.where(eye, lse, 0.0), axis=0, keepdims=True)
        higher = jnp.maximum(col_highest, jnp.max(s, axis=0, keepdims=True))
        col_total = col_total * jnp.exp(col_highest - higher) + jnp.sum(
            jnp.exp(s - higher), axis=0, keepdims=True
        )
        col_highest = higher
    return col_highest, col_total


def first_kernel(own_ref, other_ref, s_ref, row_ref, col_ref):
    highest, total = block_stats(
        own_ref,
        other_ref,
        s_ref,
        row_ref,
        jnp.full((1, NJ), -jnp.inf, jnp.float32),
        jnp.zeros((1, NJ), jnp.float32),
    )
    col_ref[0:1, :] = highest
    col_ref[1:2, :] = total


def first_stats(own, other):
    return pl.pallas_call(
        first_kernel,
        out_shape=(
            jax.ShapeDtypeStruct((NP, NJ), jnp.float32),
            jax.ShapeDtypeStruct((NP // LANES, LANES), jnp.float32),
            jax.ShapeDtypeStruct((2, NJ), jnp.float32),
        ),
        in_specs=[VMEM] * 2,
        out_specs=(VMEM,) * 3,
        compiler_params=limit(4),
        cost_estimate=pl.CostEstimate(
            flops=10 * NP * NJ, bytes_accessed=3 * 2**20, transcendentals=2 * NP * NJ
        ),
    )(own, other)


def second_kernel(
    place_ref,
    own_ref,
    other_ref,
    first_ref,
    col_ref,
    partner_ref,
    most_ref,
    most_other_ref,
    s_ref,
    out_ref,
    pack_ref,
):
    half = NP // LANES
    pack_ref[...] = jnp.zeros_like(pack_ref)
    pack_ref[0, 0:half, :] = first_ref[...]
    col_highest, col_total = block_stats(
        own_ref,
        other_ref,
        s_ref,
        pack_ref.at[0, half : 2 * half, :],
        col_ref[0:1, :],
        col_ref[1:2, :],
    )
    col_lse = col_highest + jnp.log(col_total)
    for k in range(NZ):
        row, half, trade = placed(place_ref[2], k)
        g = k // 2
        here = turned(col_lse[:, g * LANES : (g + 1) * LANES], trade)
        there = pack_ref[1, pl.ds(row, 1), :]
        pack_ref[1, pl.ds(row, 1), :] = jnp.where(lane_half() == half, here, there)
    most = jnp.max(jnp.maximum(most_ref[...], most_other_ref[...]), axis=1, keepdims=True)
    most = jnp.broadcast_to(jnp.maximum(most, 1e-30), (2, LANES))
    pack_ref[0, 8:9, :] = partner_ref[...]
    pack_ref[0, 9:10, :] = most[0:1, :]
    pack_ref[1, 9:10, :] = most[1:2, :]
    chosen = jnp.where(place_ref[0] == 0, pack_ref[0], pack_ref[1])
    for p in range(16):
        out_ref[p] = chosen


def second_stats(place, own, other, first, cols, partner, most, most_other):
    return pl.pallas_call(
        second_kernel,
        out_shape=(
            jax.ShapeDtypeStruct((NP, NJ), jnp.float32),
            jax.ShapeDtypeStruct((16, 16, LANES), jnp.float32),
        ),
        in_specs=[SMEM] + [VMEM] * 7,
        out_specs=(VMEM, VMEM),
        scratch_shapes=[pltpu.VMEM((2, 16, LANES), jnp.float32)],
        compiler_params=limit(4),
        cost_estimate=pl.CostEstimate(
            flops=10 * NP * NJ, bytes_accessed=3 * 2**20, transcendentals=2 * NP * NJ
        ),
    )(place, own, other, first, cols, partner, most, most_other)


def merged(lses):
    top = jnp.max(lses, axis=0)
    return top + jnp.log(jnp.sum(jnp.exp(lses - top[None]), axis=0))


def merge_kernel(place_ref, seen_ref, known_ref, cols_ref):
    core, xl = place_ref[0], place_ref[1]

    @pl.when(core == 0)
    def _():
        known_ref[0:8, :] = merged(seen_ref[:, 0:8, :])
        for u in range(8):
            known_ref[8 + u : 9 + u, :] = seen_ref[u, 8:9, :]

    @pl.when(core != 0)
    def _():
        known_ref[...] = jnp.zeros_like(known_ref)
        cols_ref[...] = merged(seen_ref[pl.ds(xl * NZ, NZ), 0:8, :])
        for g in range(4):
            row0, _, trade0 = placed(place_ref[2], 2 * g)
            row1, _, trade1 = placed(place_ref[2], 2 * g + 1)
            known_ref[g : g + 1, :] = jnp.where(
                lane_half() == 0,
                turned(cols_ref[pl.ds(row0, 1), :], trade0),
                turned(cols_ref[pl.ds(row1, 1), :], trade1),
            )

    known_ref[16:24, :] = jnp.broadcast_to(jnp.max(seen_ref[:, 9:10, :], axis=0), (8, LANES))


def merge_stats(place, seen):
    return pl.pallas_call(
        merge_kernel,
        out_shape=jax.ShapeDtypeStruct((24, LANES), jnp.float32),
        in_specs=[SMEM, VMEM],
        out_specs=VMEM,
        scratch_shapes=[pltpu.VMEM((8, LANES), jnp.float32)],
        compiler_params=limit(2),
        cost_estimate=pl.CostEstimate(flops=10**5, bytes_accessed=2**17, transcendentals=2**14),
    )(place, seen)


def couple_kernel(
    place_ref,
    s0_ref,
    s1_ref,
    known_ref,
    told_ref,
    c_ref,
    give_one_ref,
    give_two_ref,
    take_one_ref,
    take_two_ref,
):
    core, xl, z, uhigh = place_ref[0], place_ref[1], place_ref[2], place_ref[3]
    rows = jnp.where(core == 0, known_ref[...], told_ref[...])
    cols = jnp.where(core == 0, told_ref[...], known_ref[...])
    eye = diagonal()
    lane = lax.broadcasted_iota(jnp.int32, (1, LANES), 1)
    index, col_lse = [], []
    for g in range(4):
        first = lax.rem(z + OFFSETS[2 * g] + NZ, NZ)
        second = lax.rem(z + OFFSETS[2 * g + 1] + NZ, NZ)
        user = jnp.where(lane < HALF, first, second) * (NY * NXH) + uhigh
        inside = jnp.where(lane < HALF, lane, lane - HALF)
        index.append((user * ROWS + xl * HALF + inside).astype(jnp.float32))
        col_lse.append(cols[g : g + 1, :])
    index = jnp.concatenate(index, axis=1)
    col_lse = jnp.concatenate(col_lse, axis=1)
    for u in range(NI // LANES):
        here = slice(u * LANES, (u + 1) * LANES)
        half_ref = s0_ref if u < NP // LANES else s1_ref
        start = u * LANES % NP
        s = half_ref[start : start + LANES, :]
        row_lse = jnp.sum(jnp.where(eye, rows[u : u + 1, :], 0.0), axis=1, keepdims=True)
        partner = jnp.sum(jnp.where(eye, rows[8 + u : 9 + u, :], 0.0), axis=1, keepdims=True)
        both = jnp.exp(s - row_lse) + jnp.exp(s - col_lse)
        positive = (partner == index).astype(jnp.float32)
        c_ref[here, :] = (0.5 * both - positive).astype(jnp.bfloat16)
    most_two = jnp.concatenate([rows[16:17, :]] * 4, axis=1)
    most_one = jnp.concatenate([cols[16:17, :]] * 4, axis=1)
    give_one_ref[...] = 128.0 / most_two
    take_one_ref[...] = most_two / 128.0
    give_two_ref[...] = 64.0 / most_one
    take_two_ref[...] = most_one / 64.0


def coupling_of(place, scores0, scores1, known, told):
    return pl.pallas_call(
        couple_kernel,
        out_shape=(
            jax.ShapeDtypeStruct((NI, NJ), jnp.bfloat16),
        )
        + (jax.ShapeDtypeStruct((1, WIDTH), jnp.float32),) * 4,
        in_specs=[SMEM] + [VMEM] * 4,
        out_specs=(VMEM,) * 5,
        compiler_params=limit(5),
        cost_estimate=pl.CostEstimate(
            flops=8 * NI * NJ, bytes_accessed=3 * 2**20, transcendentals=2 * NI * NJ
        ),
    )(place, scores0, scores1, known, told)


def swap(x, axis):
    return lax.ppermute(x, axis, [(0, 1), (1, 0)])


def number(z, y, xh, xl, c):
    return (((z * NY + y) * NXH + xh) * NXL + xl) * NC + c


def line_groups(turn):
    alongs_y = [
        [number(z, y, xh, xl, turn) for y in range(NY)]
        for z in range(NZ)
        for xl in range(NXL)
        for xh in range(NXH)
    ]
    alongs_x = [
        [number(z, y, xh, xl, 1 - turn) for xl in range(NXL) for xh in range(NXH)]
        for z in range(NZ)
        for y in range(NY)
    ]
    return alongs_y + alongs_x


def spread(x, turn):
    return lax.all_to_all(
        jnp.broadcast_to(x[None], (4,) + x.shape),
        EVERY,
        0,
        0,
        axis_index_groups=line_groups(turn),
        tiled=True,
    )


def stat_groups():
    planes = [
        [number(z, y, xh, xl, 0) for xl in range(NXL) for xh in range(NXH) for y in range(NY)]
        for z in range(NZ)
    ]
    columns = [
        [number(z, y, xh, xl, 1) for xl in range(NXL) for z in range(NZ)]
        for y in range(NY)
        for xh in range(NXH)
    ]
    return planes + columns


def to_plane(x, dz):
    return lax.ppermute(x, "z", [(z, (z + dz) % NZ) for z in range(NZ)])


def largest(x):
    return jnp.max(jnp.abs(x), axis=(0, 1)).astype(jnp.float32)


def on_device(view_one, view_two, partner):
    z = lax.axis_index("z")
    uhigh = lax.axis_index("y") * NXH + lax.axis_index("xh")
    xl = lax.axis_index("xl")
    core = lax.axis_index("core")
    place = jnp.stack([core, xl, z, uhigh]).astype(jnp.int32)

    side = swap(view_two, "xl")
    lines = spread(view_one, 0)
    partner = numbers(partner)
    side, partner = lax.optimization_barrier((side, partner))
    lines, _ = lax.optimization_barrier((lines, side))
    here = jnp.where(
        xl == 0,
        jnp.stack([view_two[:HALF], side[:HALF]]),
        jnp.stack([side[HALF:], view_two[HALF:]]),
    )
    up2, down2 = to_plane(here, -2), to_plane(here, 2)
    v1_all = spread(lines, 1).reshape(16, ROWS, WIDTH)
    up = to_plane(jnp.concatenate([here, up2], axis=1), -1)
    down = to_plane(jnp.concatenate([here, down2], axis=1), 1)
    v2_all, most_v2 = join(
        here, to_plane(up2[0], -2), to_plane(down2[1], 2), up2, down2, up, down
    )

    own0 = partial_scores(0, place, v1_all, v2_all)
    other0 = swap(own0, "core")
    own1 = partial_scores(1, place, v1_all, v2_all)
    other1 = swap(own1, "core")
    most = jnp.concatenate([most_v2, largest(v1_all)[None]])
    most_other = swap(most, "core")

    scores0, first, cols = first_stats(own0, other0)
    scores1, pack = second_stats(place, own1, other1, first, cols, partner, most, most_other)
    seen = lax.all_to_all(
        pack, EVERY, 0, 0, axis_index_groups=stat_groups(), tiled=True
    )
    v1_rows = arranged(place, v1_all)
    known = merge_stats(place, seen)
    coupling, give_one, give_two, take_one, take_two = coupling_of(
        place, scores0, scores1, known, swap(known, "core")
    )

    part_one = (
        lax.dot_general(
            jnp.broadcast_to(coupling[None], (NXL, NI, NJ)),
            v2_all,
            (((2,), (1,)), ((0,), (0,))),
            preferred_element_type=jnp.float32,
        )
        * give_one
    ).astype(jnp.float16)
    one_parts = lax.all_to_all(part_one.reshape(16, ROWS, WIDTH), PLANE, 0, 0, tiled=True)
    part_two = [
        (
            lax.dot_general(
                coupling, v1_rows[x], (((0,), (0,)), ((), ())), preferred_element_type=jnp.float32
            )
            * give_two
        ).astype(jnp.float16)
        for x in range(NXL)
    ]

    def blocks(start, stop):
        return jnp.stack([part[start * HALF : stop * HALF] for part in part_two])

    from_below, from_above = to_plane(blocks(4, 6), 1), to_plane(blocks(6, 8), -1)
    four0 = to_plane(part_two[0][HALF : 2 * HALF], 2)
    four1 = to_plane(part_two[1][HALF : 2 * HALF], -2)
    wide = [x.astype(jnp.float32) for x in (from_below, from_above, four0, four1)]
    up2 = blocks(2, 3).astype(jnp.float32) + wide[0][:, HALF:]
    up2 = jnp.stack([up2[0] + wide[2], up2[1]])
    down2 = blocks(3, 4).astype(jnp.float32) + wide[1][:, HALF:]
    down2 = jnp.stack([down2[0], down2[1] + wide[3]])
    from_up = to_plane((up2 * 0.25).astype(jnp.float16), 2)
    from_down = to_plane((down2 * 0.25).astype(jnp.float16), -2)
    total = blocks(0, 1).astype(jnp.float32) + wide[0][:, :HALF] + wide[1][:, :HALF]
    total = total + 4.0 * (from_up.astype(jnp.float32) + from_down.astype(jnp.float32))
    total = total * take_two
    stay = jnp.where(xl == 0, total[0], total[1])
    come = swap(jnp.where(xl == 0, total[1], total[0]), "xl")
    grad_one = jnp.sum(one_parts.astype(jnp.float32) * take_one, axis=0)
    come, grad_one = lax.optimization_barrier((come, grad_one))
    grad_two = jnp.where(
        xl == 0, jnp.concatenate([stay, come]), jnp.concatenate([come, stay])
    )
    return (grad_one, grad_two)


def solution(mesh):
    fine = Mesh(mesh.devices.reshape(NZ, NY, NXH, NXL, NC), EVERY)
    users = P(("z", "y", "xh"))
    both = P(("z", "y", "xh"), ("xl", "core"))
    return jax.shard_map(
        on_device,
        mesh=fine,
        in_specs=(both, both, users),
        out_specs=(both, both),
        check_vma=False,
    )
```
